32 devices in a mesh: section: 2 (over x), dp: 16 (over z, y, core).
Axes of the slice: x: 2, y: 2, z: 4, core: 2. Of those that a mesh axis runs over, the one named last changes fastest.
Arguments:
- token_ids: int32 [32, 512], P('dp'), may hold values from 0 to 15359
- segment_ids: int32 [32, 512], P('dp'), may hold values from 0 to 3, never falling along the last dimension, each value on 1 to 256 neighbouring positions
- masked_pos: int32 [32, 80], P('dp'), may hold values from 0 to 511, as said below
- word_table: bfloat16 [15360, 768], P('dp'), may hold values from -0.3125 to 0.3125
- position_table: bfloat16 [512, 768], replicated, may hold values from -0.3125 to 0.3125
- embed_gain: float32 [768], replicated, may hold values from 0.5 to 1.5
- embed_bias: float32 [768], replicated, may hold values from -1.25 to 1.25
- query_weight: bfloat16 [2, 4, 192, 192], P('section'), may hold values from -0.4375 to 0.4375
- key_weight: bfloat16 [2, 4, 192, 192], P('section'), may hold values from -0.4375 to 0.4375
- value_weight: bfloat16 [2, 4, 192, 192], P('section'), may hold values from -0.4375 to 0.4375
- output_weight: bfloat16 [2, 768, 768], P('section'), may hold values from -1.75 to 1.75
- attention_gain: float32 [2, 768], P('section'), may hold values from 0.5 to 1.5
- attention_bias: float32 [2, 768], P('section'), may hold values from -1.25 to 1.25
- expand_weight: bfloat16 [2, 4, 192, 768], P('section'), may hold values from -0.4375 to 0.4375
- shrink_weight: bfloat16 [2, 4, 768, 192], P('section'), may hold values from -0.3125 to 0.3125
- feed_gain: float32 [2, 768], P('section'), may hold values from 0.5 to 1.5
- feed_bias: float32 [2, 768], P('section'), may hold values from -1.25 to 1.25
- logit_grad: bfloat16 [32, 80, 15360], P('dp', 'section'), may hold values from -1.25 to 1.25
Outputs:
- logits: bfloat16 [32, 80, 15360], P('dp', 'section')
- word_table_grad: float32 [15360, 768], P('dp')
- position_table_grad: float32 [512, 768], P(None, 'section')
- embed_gain_grad: float32 [768], P('section')
- embed_bias_grad: float32 [768], P('section')
- query_weight_grad: float32 [2, 4, 192, 192], P('section')
- key_weight_grad: float32 [2, 4, 192, 192], P('section')
- value_weight_grad: float32 [2, 4, 192, 192], P('section')
- output_weight_grad: float32 [2, 768, 768], P('section')
- attention_gain_grad: float32 [2, 768], P('section')
- attention_bias_grad: float32 [2, 768], P('section')
- expand_weight_grad: float32 [2, 4, 192, 768], P('section')
- shrink_weight_grad: float32 [2, 4, 768, 192], P('section')
- feed_gain_grad: float32 [2, 768], P('section')
- feed_bias_grad: float32 [2, 768], P('section')
The draws below stay inside these ranges and needn't reach their ends.
Inputs may be any that keep to these rules, and one draw needn't show every extreme that they name: `masked_pos`: within a row the 80 positions are distinct.
All inputs are finite; a program needn't handle non-finite values.
Results may differ from the reference program's by a relative error of at most 0.02.
Values may be sent and summed in bfloat16 or wider, within the bound.
No kernel may reach another device: no remote copies, remote signals or barrier semaphores. Data moves between devices by JAX's collectives and lax.ppermute only.
A program may use at most 384 MiB of HBM per device.

```python
import math
import jax
import jax.numpy as jnp
import numpy as np
from jax import lax

HEAD = 64
D = 768
FF = 3072
GROUPS = 4
VOCAB = 15360
SEQ = 512
SEGS = 4
SEG_MOST = 256
MASKS = 80
ROWS = 32
N_SECTION = 2


def draw_masked_pos(key, part):
    key = jax.random.fold_in(key, 7)
    row_keys = jax.random.split(key, ROWS)
    picks = jax.vmap(lambda row_key: jax.random.permutation(row_key, SEQ)[:MASKS])(row_keys)
    return picks.astype(jnp.int32)


def with_ends(values, stream_key, low, top_value):
    shape = values.shape
    index_at = [jax.random.randint(jax.random.fold_in(stream_key, axis), (), 0, shape[axis]) for axis in range(len(shape))]
    values = values.at[tuple(index_at)].set(low)
    longest = shape.index(max(shape))
    index_at[longest] = (index_at[longest] + 1) % shape[longest]
    return values.at[tuple(index_at)].set(top_value)


def strengthened(values, stream_key, source, target, shards_of, factor):
    def block_of(axis_at):
        return (jnp.arange(values.shape[axis_at]) // (values.shape[axis_at] // shards_of)).reshape((-1,) + (1,) * (values.ndim - 1 - axis_at))

    first = jax.random.permutation(stream_key, shards_of)[block_of(target)]
    second = (block_of(target) + shards_of // 2) % shards_of
    return jnp.where((block_of(source) == first) | (block_of(source) == second), factor * values, values)


def levels(own_key, dims, shards, least, high):
    def one(axis_at, blocks):
        draws = jax.random.uniform(jax.random.fold_in(jax.random.fold_in(own_key, 6), axis_at), (blocks,), jnp.float32, least / len(shards), high / len(shards))
        return jnp.repeat(jnp.exp(draws), dims[axis_at] // blocks).reshape((-1,) + (1,) * (len(dims) - axis_at - 1))

    gain = one(*shards[0])
    for cut in shards[1:]:
        gain = gain * one(*cut)
    return gain


def rank_table(amount, lean):
    portions = [(1 << 20) // math.isqrt(rank ** lean) + 1 for rank in range(1, amount + 1)]
    scale = 1 + sum(portions) // (1 << 30)
    return np.cumsum(np.array([max(1, weight // scale) for weight in portions]))


def ranked(key, shape, count, lean):
    grid = rank_table(count, lean)
    ticket = jax.random.randint(jax.random.fold_in(key, 1), shape, 0, int(grid[count - 1]))
    standing = jnp.searchsorted(jnp.asarray(grid, jnp.int32), ticket, side="right")
    return jax.random.permutation(jax.random.fold_in(key, 2), count)[standing].astype(jnp.int32)


def split_up(number_of, total, bound, lean):
    weights = [(1 << 20) // math.isqrt(grade ** lean) + 1 for grade in range(2, number_of + 1)]
    surplus, given = total - bound - (number_of - 1), [1] * (number_of - 1)
    while surplus > 0:
        candidates = [i for i in range(number_of - 1) if given[i] < bound]
        pool, remaining = sum([weights[i] for i in candidates]), surplus
        for i in candidates:
            more = min(bound - given[i], max(1, remaining * weights[i] // pool), surplus)
            given[i] = given[i] + more
            surplus = surplus - more
    return np.array([bound] + given)


def ragged(rng, amount, total, bound, slope):
    if amount == 2:
        one = jax.random.randint(rng, (), max(1, total - bound), min(bound, total - 1) + 1)
        return jnp.stack([one, total - one])
    sizes = jnp.asarray(split_up(amount, total, bound, slope), jnp.int32)
    pairs = (amount - 1) // 2
    source_of, taker = sizes[1:1 + 2 * pairs:2], sizes[2:2 + 2 * pairs:2]
    slack = jnp.minimum(source_of - 1, bound - taker)
    moved = jax.random.randint(jax.random.fold_in(rng, 1), (pairs,), 0, 1 << 20) % (slack + 1)
    sizes = sizes.at[1:1 + 2 * pairs:2].set(source_of - moved).at[2:2 + 2 * pairs:2].set(taker + moved)
    return sizes[jax.random.permutation(jax.random.fold_in(rng, 2), amount)]


def gaussian(key, shape, deviation, limit, cuts=(), held_as=jnp.bfloat16):
    values = deviation * jax.random.normal(key, shape, jnp.float32)
    if cuts:
        values = values * levels(key, shape, cuts, -0.22, 0.18)
    return jnp.clip(values, -limit, limit).astype(held_as)


def gaussian_with(rng, extent, width, most, shards, heavy, held_as=jnp.bfloat16):
    drawn = width * jax.random.normal(rng, extent, jnp.float32)
    if shards:
        drawn = drawn * levels(rng, extent, shards, -0.22, 0.18)
    return jnp.clip(strengthened(drawn, jax.random.fold_in(rng, 3), *heavy), -most, most).astype(held_as)


def setup_inputs(seed: int = 0) -> dict:
    key_of = jax.random.split(jax.random.key(seed), 19)
    token_ids = with_ends(ranked(key_of[0], (ROWS, SEQ), VOCAB, 2), jax.random.fold_in(key_of[0], 3), 0, VOCAB - 1).astype(jnp.int32)
    segment_ids = jax.vmap(lambda own: jnp.searchsorted(jnp.cumsum(ragged(own, SEGS, SEQ, SEG_MOST, 2)), jnp.arange(SEQ), side="right"))(jax.random.split(key_of[1], ROWS)).reshape((ROWS, SEQ)).astype(jnp.int32)
    masked_pos = draw_masked_pos(jax.random.fold_in(key_of[18], 71), 0)
    word_table = gaussian(key_of[3], (VOCAB, D), 0.05, 0.3125, ((0, 16),))
    position_table = gaussian(key_of[4], (SEQ, D), 0.05, 0.3125)
    embed_gain = jnp.clip(1.0 + 0.1 * jax.random.normal(key_of[5], (D,), jnp.float32), 0.5, 1.5)
    embed_bias = gaussian(key_of[6], (D,), 0.2, 1.25, (), jnp.float32)
    query_weight = gaussian(key_of[7], (N_SECTION, GROUPS, D // GROUPS, D // GROUPS), (D // GROUPS) ** -0.5, 0.4375, ((0, 2),))
    key_weight = gaussian(key_of[8], (N_SECTION, GROUPS, D // GROUPS, D // GROUPS), (D // GROUPS) ** -0.5, 0.4375, ((0, 2),))
    value_weight = gaussian(key_of[9], (N_SECTION, GROUPS, D // GROUPS, D // GROUPS), (D // GROUPS) ** -0.5, 0.4375, ((0, 2),))
    output_weight = gaussian(key_of[10], (N_SECTION, D, D), (D // 64) ** -0.5, 1.75, ((0, 2),))
    attention_gain = jnp.clip(1.0 + 0.1 * jax.random.normal(key_of[11], (N_SECTION, D), jnp.float32), 0.5, 1.5)
    attention_bias = gaussian(key_of[12], (N_SECTION, D), 0.2, 1.25, ((0, 2),), jnp.float32)
    expand_weight = gaussian(key_of[13], (N_SECTION, GROUPS, D // GROUPS, FF // GROUPS), (D // GROUPS) ** -0.5, 0.4375, ((0, 2),))
    shrink_weight = gaussian(key_of[14], (N_SECTION, GROUPS, FF // GROUPS, D // GROUPS), (FF // 8) ** -0.5, 0.3125, ((0, 2),))
    feed_gain = jnp.clip(1.0 + 0.1 * jax.random.normal(key_of[15], (N_SECTION, D), jnp.float32), 0.5, 1.5)
    feed_bias = gaussian(key_of[16], (N_SECTION, D), 0.2, 1.25, ((0, 2),), jnp.float32)
    logit_grad = gaussian_with(key_of[17], (ROWS, MASKS, VOCAB), 0.15, 1.25, ((0, 16), (1, 2)), (0, 2, 16, 2.0))
    return dict(token_ids=token_ids, segment_ids=segment_ids, masked_pos=masked_pos, word_table=word_table, position_table=position_table, embed_gain=embed_gain, embed_bias=embed_bias, query_weight=query_weight, key_weight=key_weight, value_weight=value_weight, output_weight=output_weight, attention_gain=attention_gain, attention_bias=attention_bias, expand_weight=expand_weight, shrink_weight=shrink_weight, feed_gain=feed_gain, feed_bias=feed_bias, logit_grad=logit_grad)


@jax.custom_vjp
def low(v):
    return lax.optimization_barrier(v.astype(jnp.bfloat16)).astype(jnp.float32)

@jax.custom_vjp
def low_back(v):
    return v

def low_keep(v):
    return (low(v), None)

def low_pass(kept, grad):
    return (grad,)

def back_keep(v):
    return (v, None)

def back_low(kept, grad):
    return (low(grad),)
low.defvjp(low_keep, low_pass)
low_back.defvjp(back_keep, back_low)
precise = lax.Precision.HIGHEST
norm_eps = 1e-06

def layer_norm(values, gain_vec, bias_vec):
    centre = lax.optimization_barrier(jnp.mean(values, axis=-1, keepdims=True))
    shifted = values - centre
    spread = lax.optimization_barrier(jnp.mean(shifted * shifted, axis=-1, keepdims=True))
    return shifted * lax.rsqrt(spread + norm_eps) * gain_vec + bias_vec

def restart(segments):
    counter = jnp.arange(segments.shape[0], dtype=jnp.int32)
    begins = jnp.concatenate([jnp.ones((1,), dtype=bool), segments[1:] != segments[:-1]])
    return counter - lax.cummax(jnp.where(begins, counter, 0), axis=0)

def grouped(values, weight):
    groups, width_in, width_out = weight.shape
    pieces = values.reshape(values.shape[0], groups, width_in)
    result = jnp.einsum('ngi,gio->ngo', pieces, weight, precision=precise)
    return result.reshape(values.shape[0], groups * width_out)

def encoder_layer(layer_input, same_doc, weights):
    query_weight, key_weight, value_weight, output_weight, attention_gain, attention_bias, expand_weight, shrink_weight, feed_gain, feed_bias = weights
    length, model_width = layer_input.shape
    split_shape = (length, model_width // HEAD, HEAD)
    input_low = low(layer_input)
    queries = low_back(low(grouped(input_low, query_weight))).reshape(split_shape)
    key_rows = low_back(low(grouped(input_low, key_weight))).reshape(split_shape)
    value_rows = low_back(low(grouped(input_low, value_weight))).reshape(split_shape)
    scores = jnp.einsum('qhd,khd->hqk', queries, key_rows, precision=precise) * HEAD ** (-0.5)
    scores = low_back(jnp.where(same_doc[None], scores, -1000000000.0))
    probability = low(jax.nn.softmax(scores, axis=-1))
    mixture = jnp.einsum('hqk,khd->qhd', probability, value_rows, precision=precise).reshape(length, model_width)
    attended = low_back(jnp.dot(low_back(low(mixture)), output_weight, precision=precise, preferred_element_type=jnp.float32))
    hidden = layer_norm(layer_input + attended, attention_gain, attention_bias)
    expanded = low_back(grouped(low(hidden), expand_weight))
    shrunk = low_back(grouped(low(jax.nn.gelu(expanded, approximate=False)), shrink_weight))
    return layer_norm(hidden + shrunk, feed_gain, feed_bias)

def row_forward(params, row_ids, row_segments, row_picks):
    word_rows, position_rows, gain_vec, bias_vec = (params[0], params[1], params[2], params[3])
    positions = restart(row_segments)
    same_doc = row_segments[:, None] == row_segments[None, :]
    started = layer_norm(word_rows[row_ids] + position_rows[positions], gain_vec, bias_vec)
    leading = encoder_layer(started, same_doc, tuple((array[0] for array in params[4:])))
    trailing = encoder_layer(low_back(low(leading)), same_doc, tuple((array[1] for array in params[4:])))
    picked = low(trailing[row_picks])
    return jnp.dot(picked, word_rows.T, precision=precise, preferred_element_type=jnp.float32)

def reference(token_ids, segment_ids, masked_pos, word_table, position_table, embed_gain, embed_bias, query_weight, key_weight, value_weight, output_weight, attention_gain, attention_bias, expand_weight, shrink_weight, feed_gain, feed_bias, logit_grad):
    params = tuple((array.astype(jnp.float32) for array in (word_table, position_table, embed_gain, embed_bias, query_weight, key_weight, value_weight, output_weight, attention_gain, attention_bias, expand_weight, shrink_weight, feed_gain, feed_bias)))

    def whole(params_in):

        def one_row(row_items):
            return row_forward(params_in, row_items[0], row_items[1], row_items[2])
        return lax.map(jax.checkpoint(one_row), (token_ids, segment_ids, masked_pos))
    logits, pull_back = jax.vjp(whole, params)
    gradients, = pull_back(logit_grad.astype(jnp.float32))
    return (logits.astype(jnp.bfloat16), gradients[0], gradients[1], gradients[2], gradients[3], gradients[4], gradients[5], gradients[6], gradients[7], gradients[8], gradients[9], gradients[10], gradients[11], gradients[12], gradients[13])
```

```python
import functools
import jax
import jax.numpy as jnp
from jax import lax
from jax.sharding import PartitionSpec as P
from jax.experimental import pallas as pl
from jax.experimental.pallas import tpu as pltpu

HEAD = 64
norm_eps = 1e-06
BF = jnp.bfloat16
F32 = jnp.float32
LANE = 128
N = 512
D = 768
FF = 3072
GROUPS = 4
WIDE = 192
HEADS = 12
PAIRS = 6
VMEM_LIMIT = 60 * 1024 * 1024
QKV_ROWS = 768
CHUNKS = 16
ROWS_A = 144
ROWS_B = 48
SLAB = 16
GFLOP = 10 ** 9


def mm(a, b):
    return lax.dot_general(a, b, (((1,), (0,)), ((), ())), preferred_element_type=F32)


def mm_nt(a, b):
    return lax.dot_general(a, b, (((1,), (1,)), ((), ())), preferred_element_type=F32)


def mm_tn(a, b):
    return lax.dot_general(a, b, (((0,), (0,)), ((), ())), preferred_element_type=F32)


def window(group):
    return 384 * (group // 2) + 128 * (group % 2)


def lanes(group):
    return slice(window(group), window(group) + 256)


def own_lanes(group):
    counter = lax.broadcasted_iota(jnp.int32, (1, 256), 1)
    return counter < WIDE if group % 2 == 0 else counter >= 64


def fetch_weights(refs, own, other, use_own, core, sems):
    shrink, expand, output, qkv, vecs = refs
    mine, rest = other[0:4], other[4:8]

    def copies(sources, halves):
        made = []
        for number in range(2):
            half = halves[number]
            shrink_src, expand_src, output_src, qkv_src = sources[number]
            for j in range(2 if shrink is not None else 0):
                made.append(pltpu.make_async_copy(shrink_src.at[pl.ds(j * WIDE, WIDE)], shrink.at[2 * half + j, pl.ds(64 * j, WIDE)], sems.at[6 * number + j]))
                made.append(pltpu.make_async_copy(expand_src.at[pl.ds(j * WIDE, WIDE)], expand.at[2 * half + j, pl.ds(64 * j, WIDE)], sems.at[6 * number + 2 + j]))
            if output is not None:
                made.append(pltpu.make_async_copy(output_src, output.at[pl.ds(pl.multiple_of(half * 384, 384), 384)], sems.at[6 * number + 4]))
            if qkv is not None:
                made.append(pltpu.make_async_copy(qkv_src, qkv.at[pl.ds(pl.multiple_of(half * 288, 288), 288)], sems.at[6 * number + 5]))
        return made

    halves_of = [[ref.at[pl.ds(h * (ref.shape[0] // 2), ref.shape[0] // 2)] for ref in own[0:4]] for h in range(2)]
    whole = copies(halves_of, (0, 1))
    parts = copies((mine, rest), (core, 1 - core))
    if vecs is not None:
        whole.append(pltpu.make_async_copy(own[4], vecs, sems.at[12]))
        parts.append(pltpu.make_async_copy(other[8], vecs, sems.at[12]))

    @pl.when(use_own)
    def _():
        for c in whole:
            c.start()

    @pl.when(jnp.logical_not(use_own))
    def _():
        for c in parts:
            c.start()

    for g in range(GROUPS if shrink is not None else 0):
        at = WIDE * (1 - g % 2)
        shrink[g, at : at + 64, :] = jnp.zeros((64, D), BF)
        expand[g, at : at + 64, :] = jnp.zeros((64, D), BF)
    return whole


def pad_qkv(qkv, padded):
    for which in range(3):
        for g in range(GROUPS):
            at = 64 * (g % 2)
            block = qkv[which * WIDE : (which + 1) * WIDE, lanes(g)]
            padded[which, g, at : at + WIDE, :] = jnp.where(own_lanes(g), block, jnp.zeros_like(block))
            gap = WIDE * (1 - g % 2)
            padded[which, g, gap : gap + 64, :] = jnp.zeros((64, 256), BF)


def norm_parts(values):
    centre = jnp.mean(values, axis=-1, keepdims=True)
    shifted = values - centre
    spread = jnp.mean(shifted * shifted, axis=-1, keepdims=True)
    rstd = lax.rsqrt(spread + norm_eps)
    return shifted * rstd, rstd


def norm_back(gradient, hat, rstd, gain):
    scaled = gradient * gain
    first = jnp.mean(scaled, axis=-1, keepdims=True)
    second = jnp.mean(scaled * hat, axis=-1, keepdims=True)
    return rstd * (scaled - first - hat * second)


def join_pair(low, high):
    return jnp.concatenate([low[:, :128], low[:, 128:] + high[:, :128], high[:, 128:]], axis=1)


def layer_fwd(x_ref, bias_ref, w, saves, stats_ref, grow_ref, save_done):
    shrink, expand, output, qkv_pad, vecs = w
    x_low, q_ref, k_ref, v_ref, e_ref, mix_ref, hat_a, hidden_low, active, slope, hat_f, inv_ref, full_ref = saves
    x_low[...] = x_ref[...].astype(BF)
    for which, target in enumerate((q_ref, k_ref, v_ref)):
        for p in range(2):
            low = mm(x_low[:, lanes(2 * p)], qkv_pad[which, 2 * p])
            high = mm(x_low[:, lanes(2 * p + 1)], qkv_pad[which, 2 * p + 1])
            joined = join_pair(low, high).astype(BF)
            if which == 0:
                joined = joined * jnp.asarray(HEAD ** (-0.5), BF)
            target[:, 384 * p : 384 * (p + 1)] = joined
    save_done(0)
    stats_ref[...] = jnp.zeros_like(stats_ref)
    lane = lax.broadcasted_iota(jnp.int32, (1, LANE), 1)

    def pair_body(p, carry):
        at = pl.ds(pl.multiple_of(p * LANE, LANE), LANE)
        qs, ks, vs = q_ref[:, at], k_ref[:, at], v_ref[:, at]
        outs = []
        for side in range(2):
            mine = (lane < HEAD) if side == 0 else (lane >= HEAD)
            scores = mm_nt(jnp.where(mine, qs, jnp.zeros_like(qs)), ks) + bias_ref[...]
            top = jnp.max(scores, axis=-1, keepdims=True)
            e = jnp.exp(scores - top).astype(BF)
            e_ref[2 * p + side] = e
            outs.append(mm(e, jnp.where(mine, vs, jnp.ones_like(vs))))
        inv = 1.0 / pltpu.roll(jnp.where(lane < HEAD, outs[1], outs[0]), HEAD, 1)
        full = jnp.where(lane < HEAD, outs[0], outs[1]) * inv
        inv_ref[:, at] = inv
        full_ref[:, at] = full
        mix_ref[:, at] = full.astype(BF)
        return carry

    lax.fori_loop(0, PAIRS, pair_body, 0)
    save_done(1)
    residual = x_ref[...] + mm(mix_ref[...], output[...])
    hat, rstd = norm_parts(residual)
    hat_a[...] = hat.astype(BF)
    stats_ref[...] = jnp.where(lane == 12, rstd, stats_ref[...])
    hidden = hat * vecs[0:1, :] + vecs[1:2, :]
    hidden_low[...] = hidden.astype(BF)
    grow_ref[...] = hidden
    for g in range(GROUPS):
        wide = slice(g * D, (g + 1) * D)
        expanded = mm(hidden_low[:, lanes(g)], expand[g])
        phi = 0.5 * (1.0 + lax.erf(expanded * (2.0 ** -0.5)))
        density = jnp.exp(expanded * expanded * -0.5) * (2.0 * jnp.pi) ** -0.5
        act = (expanded * phi).astype(BF)
        active[:, wide] = act
        slope[:, wide] = (phi + expanded * density).astype(BF)
        grow_ref[:, lanes(g)] += mm_nt(act, shrink[g])
    save_done(2)
    hat, rstd = norm_parts(grow_ref[...])
    hat_f[...] = hat.astype(BF)
    stats_ref[...] = jnp.where(lane == 13, rstd, stats_ref[...])
    x_ref[...] = hat * vecs[2:3, :] + vecs[3:4, :]
    save_done(3)


SAVE_SHAPES = (
    (N, D), (N, D), (N, D), (N, D), (HEADS, N, N), (N, D), (N, D), (N, D), (N, FF), (N, FF), (N, D),
    (N, D), (N, D), (N, LANE),
)
SAVE_TYPES = (BF,) * 11 + (F32,) * 3
SAVE_STAGES = ((0, 1, 2, 3), (4, 5, 11, 12), (6, 7, 8, 9), (10, 13))
SAVES = 14


def weight_scratch():
    return [
        pltpu.VMEM((GROUPS, 256, D), BF),
        pltpu.VMEM((GROUPS, 256, D), BF),
        pltpu.VMEM((D, D), BF),
        pltpu.VMEM((3 * WIDE, D), BF),
        pltpu.VMEM((8, D), F32),
    ]


def fwd_kernel(flag, slot_rows, dense_rows, slot_col, place_col, seg_col, seg_row, mask_col, place_table, embed_vec, *rest):
    rest = list(rest)

    def take(n):
        got = rest[:n]
        del rest[:n]
        return got

    own, other = take(5), take(9)
    (picked_ref,) = take(1)
    outs = [take(SAVES), take(SAVES)]
    hat_e_ref, stat_e_ref = take(2)
    weights = [take(5), take(5)]
    qkv_pad, bias_ref, x_ref, grow_ref = take(4)
    saves = take(SAVES)
    sem_w, sem_s, sem_d = take(3)
    leading = flag[0] == 0
    waits = [
        fetch_weights(weights[0], own, other, leading, flag[2], sem_w.at[0]),
        fetch_weights(weights[1], own, other, jnp.logical_not(leading), flag[2], sem_w.at[1]),
    ]
    counter = lax.broadcasted_iota(jnp.int32, (N, N), 1)
    one_hot = (place_col[...] == counter).astype(BF)
    slots = slot_rows.shape[0]
    wanted = (slot_col[...] == lax.broadcasted_iota(jnp.int32, (N, slots), 1)).astype(BF)
    x_ref[...] = mm(wanted, slot_rows[...])

    @pl.when(flag[1] != 0)
    def _():
        c = pltpu.make_async_copy(dense_rows, saves[0], sem_d)
        c.start()
        c.wait()
        x_ref[...] = saves[0][...].astype(F32)

    summed = x_ref[...] + mm(one_hot, place_table[...])
    hat, rstd = norm_parts(summed)
    hat_e_ref[...] = hat.astype(BF)
    stat_e_ref[...] = jnp.broadcast_to(rstd, (N, LANE))
    x_ref[...] = hat * embed_vec[0:1, :] + embed_vec[1:2, :]
    bias_ref[...] = jnp.where(seg_col[...] == seg_row[...], 0.0, -1000000000.0)
    drains = []
    for number in range(2):
        for c in waits[number] + drains:
            c.wait()
        drains = []
        shrink, expand, output, qkv, vecs = weights[number]
        pad_qkv(qkv, qkv_pad)

        def save_done(stage, number=number, drains=drains):
            for i in SAVE_STAGES[stage]:
                c = pltpu.make_async_copy(saves[i], outs[number][i], sem_s.at[number, i])
                c.start()
                drains.append(c)

        layer_fwd(
            x_ref, bias_ref, (shrink, expand, output, qkv_pad, vecs),
            saves[:13], saves[13], grow_ref, save_done,
        )
        if number == 0:
            x_ref[...] = x_ref[...].astype(BF).astype(F32)
    picks = (mask_col[...] == lax.broadcasted_iota(jnp.int32, (mask_col.shape[0], N), 1)).astype(BF)
    picked_ref[...] = mm(picks, x_ref[...].astype(BF)).astype(BF)
    for c in drains:
        c.wait()


def save_structs():
    return [jax.ShapeDtypeStruct(s, t) for s, t in zip(SAVE_SHAPES, SAVE_TYPES)]


def save_scratch():
    return [pltpu.VMEM(s, t) for s, t in zip(SAVE_SHAPES, SAVE_TYPES)]


VM = pl.BlockSpec(memory_space=pltpu.VMEM)
HB = pl.BlockSpec(memory_space=pl.ANY)
SM = pl.BlockSpec(memory_space=pltpu.SMEM)


def forward_call(flag, slot_rows, dense_rows, slot_col, place_col, seg_col, seg_row, mask_col, place_table, embed_vec, own, other):
    masks = mask_col.shape[0]
    out = pl.pallas_call(
        fwd_kernel,
        out_shape=[jax.ShapeDtypeStruct((masks, D), BF)] + save_structs() * 2
        + [jax.ShapeDtypeStruct((N, D), BF), jax.ShapeDtypeStruct((N, LANE), F32)],
        in_specs=[SM, VM, HB] + [VM] * 7 + [HB] * 14,
        out_specs=[VM] + [HB] * (2 * SAVES) + [VM] * 2,
        scratch_shapes=weight_scratch() * 2
        + [pltpu.VMEM((3, GROUPS, 256, 256), BF), pltpu.VMEM((N, N), F32), pltpu.VMEM((N, D), F32), pltpu.VMEM((N, D), F32)]
        + save_scratch()
        + [pltpu.SemaphoreType.DMA((2, 13)), pltpu.SemaphoreType.DMA((2, SAVES)), pltpu.SemaphoreType.DMA],
        compiler_params=pltpu.CompilerParams(vmem_limit_bytes=VMEM_LIMIT),
        cost_estimate=pl.CostEstimate(flops=36 * GFLOP, bytes_accessed=60 << 20, transcendentals=0),
        name="forward_layers",
    )(flag, slot_rows, dense_rows, slot_col, place_col, seg_col, seg_row, mask_col, place_table, embed_vec, *own, *other)
    return out[0], out[1 : 1 + SAVES], out[1 + SAVES : 1 + 2 * SAVES], out[-2], out[-1]


def put_chunks(packed_ref, core, source, rows, at):
    for chunk in range(CHUNKS):
        side = core if chunk % 2 == 0 else 1 - core
        packed_ref[side, chunk // 2, at : at + rows, :] = source[chunk * rows : (chunk + 1) * rows, :].astype(BF)


def bwd_a_kernel(last, flag, *rest):
    rest = list(rest)

    def take(n):
        got = rest[:n]
        del rest[:n]
        return got

    if last:
        (go_in,) = take(1)
    else:
        picked_back, mask_row = take(2)
    own, other = take(5), take(9)
    sources = take(7)
    keep_out, away_out, attn_ref, back_low, vec_ref = take(5)
    weights = take(4)
    mid_ref, low_ref, packed_ref = take(3)
    saves = take(7)
    sem_w, sem_s, sem_o, sem_g = take(4)
    mix_ref, hat_a, hidden_low, active, slope, hat_f, stats_ref = saves
    shrink, expand, output, vecs = weights
    leading, core = flag[0] == 0, flag[2]
    use_own = leading if last else jnp.logical_not(leading)
    copies = [pltpu.make_async_copy(sources[i], saves[i], sem_s.at[i]) for i in range(7)]
    wide_copies = []
    for g in range(GROUPS):
        at = pl.ds(g * D, D)
        wide_copies.append([pltpu.make_async_copy(sources[i].at[:, at], saves[i].at[:, at], sem_g.at[i - 3, g]) for i in (3, 4)])
    for i in (5, 6):
        copies[i].start()
    waits = fetch_weights((shrink, expand, output, None, vecs), own, other, use_own, core, sem_w)
    copies[2].start()
    for pair in wide_copies:
        for c in pair:
            c.start()
    for i in (1, 0):
        copies[i].start()
    vec_ref[...] = jnp.zeros_like(vec_ref)
    if last:
        go = go_in[...].astype(F32)
    else:
        masks = mask_row.shape[1]
        spread = (lax.broadcasted_iota(jnp.int32, (N, masks), 0) == mask_row[...]).astype(BF)
        go = mm(spread, picked_back[...])
    lane = lax.broadcasted_iota(jnp.int32, (1, LANE), 1)

    def stat(index):
        return jnp.sum(jnp.where(lane == index, stats_ref[...], 0.0), axis=-1, keepdims=True)

    copies[5].wait()
    copies[6].wait()
    for c in waits:
        c.wait()
    hat = hat_f[...].astype(F32)
    vec_ref[2:3, :] = jnp.sum(go * hat, axis=0, keepdims=True)
    vec_ref[3:4, :] = jnp.sum(go, axis=0, keepdims=True)
    feed_back = norm_back(go, hat, stat(13), vecs[2:3, :])
    mid_ref[...] = feed_back
    low_ref[...] = feed_back.astype(BF)
    copies[2].wait()
    each = WIDE // (CHUNKS // GROUPS)
    for g in range(GROUPS):
        wide = slice(g * D, (g + 1) * D)
        rows = slice(64 * (g % 2), 64 * (g % 2) + WIDE)
        for c in wide_copies[g]:
            c.wait()
        shrink_in = low_ref[:, lanes(g)]
        shrink_grad = mm_tn(shrink_in, active[:, wide])[rows].astype(BF)
        expand_in = (mm(shrink_in, shrink[g]) * slope[:, wide].astype(F32)).astype(BF)
        expand_grad = mm_tn(hidden_low[:, lanes(g)], expand_in)[rows].astype(BF)
        mid_ref[:, lanes(g)] += mm_nt(expand_in, expand[g])
        for part in range(CHUNKS // GROUPS):
            chunk = g * (CHUNKS // GROUPS) + part
            side = core if chunk % 2 == 0 else 1 - core
            packed_ref[side, chunk // 2, 0:each, :] = shrink_grad[part * each : (part + 1) * each, :]
            packed_ref[side, chunk // 2, each : 2 * each, :] = expand_grad[part * each : (part + 1) * each, :]
    copies[1].wait()
    hidden_back = mid_ref[...]
    hat = hat_a[...].astype(F32)
    vec_ref[0:1, :] = jnp.sum(hidden_back * hat, axis=0, keepdims=True)
    vec_ref[1:2, :] = jnp.sum(hidden_back, axis=0, keepdims=True)
    attn_back = norm_back(hidden_back, hat, stat(12), vecs[0:1, :])
    attn_ref[...] = attn_back
    attended_in = attn_back.astype(BF)
    copies[0].wait()
    put_chunks(packed_ref, core, mm_tn(mix_ref[...], attended_in), each, 2 * each)
    ship = [pltpu.make_async_copy(packed_ref.at[1], away_out, sem_o.at[0]), pltpu.make_async_copy(packed_ref.at[0], keep_out, sem_o.at[1])]
    for c in ship:
        c.start()
    back_low[...] = mm_nt(attended_in, output[...]).astype(BF)
    for c in ship:
        c.wait()


def backward_a_call(last, flag, extra, own, other, saved):
    chosen = (5, 6, 7, 8, 9, 10, 13)
    return pl.pallas_call(
        functools.partial(bwd_a_kernel, last),
        out_shape=[
            jax.ShapeDtypeStruct((CHUNKS // 2, ROWS_A, D), BF), jax.ShapeDtypeStruct((CHUNKS // 2, ROWS_A, D), BF),
            jax.ShapeDtypeStruct((N, D), F32), jax.ShapeDtypeStruct((N, D), BF), jax.ShapeDtypeStruct((16, D), F32),
        ],
        in_specs=[SM] + [VM] * len(extra) + [HB] * (14 + len(chosen)),
        out_specs=[HB, HB, VM, VM, VM],
        scratch_shapes=[
            pltpu.VMEM((GROUPS, 256, D), BF), pltpu.VMEM((GROUPS, 256, D), BF), pltpu.VMEM((D, D), BF), pltpu.VMEM((8, D), F32),
            pltpu.VMEM((N, D), F32), pltpu.VMEM((N, D), BF), pltpu.VMEM((2, CHUNKS // 2, ROWS_A, D), BF),
        ]
        + [pltpu.VMEM(SAVE_SHAPES[i], SAVE_TYPES[i]) for i in chosen]
        + [pltpu.SemaphoreType.DMA((13,)), pltpu.SemaphoreType.DMA((len(chosen),)), pltpu.SemaphoreType.DMA((2,)), pltpu.SemaphoreType.DMA((2, GROUPS))],
        compiler_params=pltpu.CompilerParams(vmem_limit_bytes=VMEM_LIMIT),
        cost_estimate=pl.CostEstimate(flops=12 * GFLOP, bytes_accessed=20 << 20, transcendentals=0),
        name="backward_first_a" if last else "backward_second_a",
    )(flag, *extra, *own, *other, *[saved[i] for i in chosen])


def bwd_b_kernel(last, flag, attn_in, back_low, vec_in, *rest):
    rest = list(rest)

    def take(n):
        got = rest[:n]
        del rest[:n]
        return got

    if last:
        slot_row, place_row, hat_e_ref, stat_e_ref, embed_vec = take(5)
    own, other = take(5), take(9)
    sources = take(7)
    keep_out, away_out, back_ref = take(3)
    if last:
        (slot_grad,) = take(1)
    qkv, qkv_pad, go_ref, vec_ref, packed_ref = take(5)
    dq_ref, dk_ref, dv_ref, grad_ref = take(4)
    saves = take(7)
    sem_w, sem_s, sem_o = take(3)
    x_low, q_ref, k_ref, v_ref, e_ref, inv_ref, full_ref = saves
    leading, core = flag[0] == 0, flag[2]
    use_own = leading if last else jnp.logical_not(leading)
    whole = pltpu.make_async_copy(sources[0], saves[0], sem_s.at[0, 0])

    def pair_copies(p):
        at = pl.ds(p * LANE if isinstance(p, int) else pl.multiple_of(p * LANE, LANE), LANE)
        made = [pltpu.make_async_copy(sources[4].at[pl.ds(2 * p, 2)], saves[4].at[pl.ds(2 * p, 2)], sem_s.at[4, p])]
        for i in (1, 2, 3, 5, 6):
            made.append(pltpu.make_async_copy(sources[i].at[:, at], saves[i].at[:, at], sem_s.at[i, p]))
        return made

    for p in range(PAIRS):
        for c in pair_copies(p):
            c.start()
    waits = fetch_weights((None, None, None, qkv, None), own, other, use_own, core, sem_w)
    whole.start()
    lane = lax.broadcasted_iota(jnp.int32, (1, LANE), 1)

    def pair_body(p, carry):
        for c in pair_copies(p):
            c.wait()
        at = pl.ds(pl.multiple_of(p * LANE, LANE), LANE)
        first = lane < HEAD
        d_low = (back_low[:, at].astype(F32) * inv_ref[:, at]).astype(BF)
        weighted = d_low.astype(F32) * full_ref[:, at]
        qs, ks, vs = q_ref[:, at], k_ref[:, at], v_ref[:, at]
        d_v = d_q = d_k = None
        for side in range(2):
            mine = first if side == 0 else jnp.logical_not(first)
            delta = jnp.sum(jnp.where(mine, weighted, 0.0), axis=-1, keepdims=True)
            e = e_ref[2 * p + side]
            d_side = jnp.where(mine, d_low, jnp.zeros_like(d_low))
            prob_back = mm_nt(d_side, vs)
            d_s = (e.astype(F32) * (prob_back - delta)).astype(BF)
            part_v = mm_tn(e, d_side)
            part_q = mm(d_s, jnp.where(mine, ks, jnp.zeros_like(ks)))
            part_k = mm_tn(d_s, jnp.where(mine, qs, jnp.zeros_like(qs)))
            d_v = part_v if d_v is None else d_v + part_v
            d_q = part_q if d_q is None else d_q + part_q
            d_k = part_k if d_k is None else d_k + part_k
        dv_ref[:, at] = d_v.astype(BF)
        dq_ref[:, at] = (d_q * HEAD ** (-0.5)).astype(BF)
        dk_ref[:, at] = d_k.astype(BF)
        return carry

    lax.fori_loop(0, PAIRS, pair_body, 0)
    whole.wait()
    for c in waits:
        c.wait()
    pad_qkv(qkv, qkv_pad)
    go_ref[...] = attn_in[...]
    vec_ref[...] = jnp.zeros_like(vec_ref)
    vec_ref[0:8, :] = vec_in[0:8, :]
    for which, d_ref in enumerate((dq_ref, dk_ref, dv_ref)):
        for p in range(2):
            made = []
            for g in (2 * p, 2 * p + 1):
                rows = slice(64 * (g % 2), 64 * (g % 2) + WIDE)
                d_part = d_ref[:, lanes(g)]
                made.append(jnp.where(own_lanes(g), mm_tn(x_low[:, lanes(g)], d_part)[rows], 0.0))
                go_ref[:, lanes(g)] += mm_nt(d_part, qkv_pad[which, g])
            grad_ref[which * WIDE : (which + 1) * WIDE, 384 * p : 384 * (p + 1)] = join_pair(*made).astype(BF)
    go = go_ref[...]
    if last:
        hat = hat_e_ref[...].astype(F32)
        gain_row = jnp.sum(go * hat, axis=0, keepdims=True)
        bias_row = jnp.sum(go, axis=0, keepdims=True)
        for s in range(2):
            at = slice(s * (D // 2), (s + 1) * (D // 2))
            vec_ref[8 + s : 9 + s, :] = jnp.concatenate([gain_row[:, at], bias_row[:, at]], axis=1)
        back = norm_back(go, hat, stat_e_ref[:, 0:1], embed_vec[0:1, :]).astype(BF)
        back_ref[...] = back
        places = (lax.broadcasted_iota(jnp.int32, (N, N), 0) == place_row[...]).astype(BF)
        grad = mm(places, back).astype(BF)
        for s in range(2):
            block = jnp.concatenate([grad[part * (N // 2) : (part + 1) * (N // 2), s * 384 : (s + 1) * 384] for part in range(2)], axis=1)
            put_chunks(packed_ref, core, block, SLAB, ROWS_B + s * SLAB)
        slots = slot_grad.shape[0]
        slot_grad[...] = mm((lax.broadcasted_iota(jnp.int32, (slots, N), 0) == slot_row[...]).astype(BF), back).astype(BF)
    else:
        back_ref[...] = go.astype(BF)
    grad_ref[3 * WIDE :, :] = vec_ref[...].astype(BF)
    put_chunks(packed_ref, core, grad_ref, ROWS_B, 0)
    ship = [pltpu.make_async_copy(packed_ref.at[1], away_out, sem_o.at[0]), pltpu.make_async_copy(packed_ref.at[0], keep_out, sem_o.at[1])]
    for c in ship:
        c.start()
    for c in ship:
        c.wait()


def backward_b_call(last, flag, extra, own, other, saved, slots=0):
    chosen = (0, 1, 2, 3, 4, 11, 12)
    rows = ROWS_B + 2 * SLAB if last else ROWS_B
    out_shape = [
        jax.ShapeDtypeStruct((CHUNKS // 2, rows, D), BF), jax.ShapeDtypeStruct((CHUNKS // 2, rows, D), BF),
        jax.ShapeDtypeStruct((N, D), BF),
    ]
    if last:
        out_shape.append(jax.ShapeDtypeStruct((slots, D), BF))
    return pl.pallas_call(
        functools.partial(bwd_b_kernel, last),
        out_shape=out_shape,
        in_specs=[SM] + [VM] * len(extra) + [HB] * (14 + len(chosen)),
        out_specs=[HB, HB] + [VM] * (len(out_shape) - 2),
        scratch_shapes=[
            pltpu.VMEM((3 * WIDE, D), BF), pltpu.VMEM((3, GROUPS, 256, 256), BF), pltpu.VMEM((N, D), F32),
            pltpu.VMEM((QKV_ROWS - 3 * WIDE, D), F32), pltpu.VMEM((2, CHUNKS // 2, rows, D), BF),
        ]
        + [pltpu.VMEM((N, D), BF)] * 3 + [pltpu.VMEM((QKV_ROWS, D), BF)]
        + [pltpu.VMEM(SAVE_SHAPES[i], SAVE_TYPES[i]) for i in chosen]
        + [pltpu.SemaphoreType.DMA((13,)), pltpu.SemaphoreType.DMA((len(chosen), PAIRS)), pltpu.SemaphoreType.DMA((2,))],
        compiler_params=pltpu.CompilerParams(vmem_limit_bytes=VMEM_LIMIT),
        cost_estimate=pl.CostEstimate(flops=15 * GFLOP, bytes_accessed=20 << 20, transcendentals=0),
        name="backward_first_b" if last else "backward_second_b",
    )(flag, *extra, *own, *other, *[saved[i] for i in chosen])


def step_y_kernel(side_ref, keep_ref, came_ref, next_keep, next_away):
    side = side_ref[0]
    for j in range(next_keep.shape[0]):
        for target, which in ((next_keep, side), (next_away, 1 - side)):
            at = 2 * j + which
            target[j] = (keep_ref[at].astype(F32) + came_ref[at].astype(F32)).astype(BF)


def step_y(side, keep, came):
    half = jax.ShapeDtypeStruct((keep.shape[0] // 2,) + keep.shape[1:], BF)
    return pl.pallas_call(
        step_y_kernel, out_shape=[half, half], in_specs=[SM, VM, VM], out_specs=[VM, VM],
        compiler_params=pltpu.CompilerParams(vmem_limit_bytes=VMEM_LIMIT),
        cost_estimate=pl.CostEstimate(flops=GFLOP, bytes_accessed=6 << 20, transcendentals=0), name="halve_chunks",
    )(side, keep, came)


def step_z_kernel(me_ref, keep_ref, came_ref, *outs):
    for step in range(4):
        at = me_ref[0] ^ step
        outs[step][...] = (keep_ref[at].astype(F32) + came_ref[at].astype(F32)).astype(BF)


def step_z(me, keep, came):
    one = jax.ShapeDtypeStruct(keep.shape[1:], BF)
    return pl.pallas_call(
        step_z_kernel, out_shape=[one] * 4, in_specs=[SM, VM, VM], out_specs=[VM] * 4,
        compiler_params=pltpu.CompilerParams(vmem_limit_bytes=VMEM_LIMIT),
        cost_estimate=pl.CostEstimate(flops=GFLOP, bytes_accessed=4 << 20, transcendentals=0), name="four_chunks",
    )(me, keep, came)


def finish_kernel(part, flag, place_ref, *refs):
    parts1, parts0 = refs[0:4], refs[4:8]
    mine, theirs = refs[8:10]
    sums = []
    for parts in (parts0, parts1):
        total = parts[0][...].astype(F32)
        for ref in parts[1:]:
            total = total + ref[...].astype(F32)
        sums.append(total)
    first, second = sums
    if part == 1:
        row = lax.broadcasted_iota(jnp.int32, (ROWS_B, 1), 0) + place_ref[0] * ROWS_B
        extra = jnp.where(row >= 3 * WIDE + 8, first[:ROWS_B], 0.0)
        second = jnp.concatenate([second + extra, first[ROWS_B + SLAB :]], axis=0)
        first = first[: ROWS_B + SLAB]
    leading = flag[0] == 0
    mine[...] = jnp.where(leading, first, second).astype(BF)
    theirs[...] = jnp.where(leading, second, first).astype(BF)


def finish_call(part, flag, place, parts1, parts0):
    rows = ROWS_A if part == 0 else ROWS_B + SLAB
    one = jax.ShapeDtypeStruct((rows, D), BF)
    return pl.pallas_call(
        functools.partial(finish_kernel, part), out_shape=[one, one], in_specs=[SM, SM] + [VM] * 8, out_specs=[VM] * 2,
        compiler_params=pltpu.CompilerParams(vmem_limit_bytes=VMEM_LIMIT),
        cost_estimate=pl.CostEstimate(flops=GFLOP, bytes_accessed=2 << 20, transcendentals=0), name="finish_chunks",
    )(flag, place, *parts1, *parts0)


def unpack_kernel(flag, place_ref, a_own, a_came, b_own, b_came, shrink, expand, output, query, key, value, vecs, embed, position, grid, slab):
    each = ROWS_A // 3
    half = CHUNKS // 2
    for core in range(2):
        a_ref, b_ref = (a_own, b_own) if core == 0 else (a_came, b_came)
        for i in range(half):
            device = place_ref[0] ^ (4 * (i % 4) + 2 * (i // 4) + core)
            rows = pl.ds(pl.multiple_of(device * each, each), each)
            block = a_ref[i].astype(F32)
            shrink[rows, :] = block[0:each]
            expand[rows, :] = block[each : 2 * each]
            output[rows, :] = block[2 * each :]
            block = b_ref[i].astype(F32)
            grid[pl.ds(pl.multiple_of(device * ROWS_B, ROWS_B), ROWS_B), :] = block[:ROWS_B]
            slab[pl.ds(pl.multiple_of(device * SLAB, SLAB), SLAB), :] = block[ROWS_B:]
    for which, target in enumerate((query, key, value)):
        for g in range(GROUPS):
            target[g] = grid[which * WIDE : (which + 1) * WIDE, g * WIDE : (g + 1) * WIDE]
    vecs[...] = grid[3 * WIDE : 3 * WIDE + 8, :]
    rows = grid[3 * WIDE + 8 : 3 * WIDE + 16, :]
    embed[...] = jnp.where(flag[0] == 0, rows[0:1], rows[1:2])
    for part in range(2):
        position[part * (N // 2) : (part + 1) * (N // 2), :] = slab[:, part * (D // 2) : (part + 1) * (D // 2)]


def unpack_call(flag, place, a_own, a_came, b_own, b_came):
    square = jax.ShapeDtypeStruct((D, D), F32)
    group = jax.ShapeDtypeStruct((GROUPS, WIDE, WIDE), F32)
    return pl.pallas_call(
        unpack_kernel,
        out_shape=[square] * 3 + [group] * 3
        + [jax.ShapeDtypeStruct((8, D), F32), jax.ShapeDtypeStruct((1, D), F32), jax.ShapeDtypeStruct((N, D // 2), F32)],
        in_specs=[SM, SM] + [VM] * 4,
        out_specs=[VM] * 9,
        scratch_shapes=[pltpu.VMEM((QKV_ROWS, D), F32), pltpu.VMEM((CHUNKS * SLAB, D), F32)],
        compiler_params=pltpu.CompilerParams(vmem_limit_bytes=VMEM_LIMIT),
        cost_estimate=pl.CostEstimate(flops=GFLOP, bytes_accessed=16 << 20, transcendentals=0), name="unpack_sums",
    )(flag, place, a_own, a_came, b_own, b_came)


def plan_kernel(room, id_row, id_col, owner_row, owner_col, slot_col, slot_row, want_ref, most_ref):
    slots = want_ref.shape[1]
    across = lax.broadcasted_iota(jnp.int32, (N, N), 1)
    down = lax.broadcasted_iota(jnp.int32, (N, N), 0)
    same = id_col[...] == id_row[...]
    first_col = jnp.min(jnp.where(same, across, N).astype(F32), axis=1, keepdims=True).astype(jnp.int32)
    first_row = jnp.min(jnp.where(same, down, N).astype(F32), axis=0, keepdims=True).astype(jnp.int32)
    fresh_row = first_row == lax.broadcasted_iota(jnp.int32, (1, N), 1)
    fresh_col = first_col == lax.broadcasted_iota(jnp.int32, (N, 1), 0)
    mates = owner_col[...] == owner_row[...]
    rank_col = jnp.sum(jnp.where(mates & fresh_row & (across < first_col), 1.0, 0.0), axis=1, keepdims=True).astype(jnp.int32)
    rank_row = jnp.sum(jnp.where(mates & fresh_col & (down < first_row), 1.0, 0.0), axis=0, keepdims=True).astype(jnp.int32)
    col = jnp.where(rank_col < room, owner_col[...] * room + rank_col, -1)
    slot_col[...] = col
    slot_row[...] = jnp.where(rank_row < room, owner_row[...] * room + rank_row, -1)
    chosen = (col == lax.broadcasted_iota(jnp.int32, (N, slots), 1)) & fresh_col
    want = jnp.sum(jnp.where(chosen, (id_col[...] + 1).astype(F32), 0.0), axis=0, keepdims=True)
    want_ref[...] = want.astype(jnp.int32) - 1
    most = jnp.max(rank_row.astype(F32), axis=1, keepdims=True).astype(jnp.int32) + 1
    most_ref[...] = jnp.broadcast_to(most, most_ref.shape)


def plan_call(ids, owners, room, slots):
    return pl.pallas_call(
        functools.partial(plan_kernel, room),
        out_shape=[
            jax.ShapeDtypeStruct((N, 1), jnp.int32), jax.ShapeDtypeStruct((1, N), jnp.int32),
            jax.ShapeDtypeStruct((1, slots), jnp.int32), jax.ShapeDtypeStruct((8, LANE), jnp.int32),
        ],
        in_specs=[VM] * 4,
        out_specs=[VM] * 4,
        compiler_params=pltpu.CompilerParams(vmem_limit_bytes=VMEM_LIMIT),
        name="plan_slots",
    )(ids[None], ids[:, None], owners[None], owners[:, None])


def serve_kernel(base_ref, ids_ref, table_ref, out_ref):
    counter = lax.broadcasted_iota(jnp.int32, (ids_ref.shape[0], table_ref.shape[0]), 1) + base_ref[0]
    out_ref[...] = mm((ids_ref[...] == counter).astype(BF), table_ref[...]).astype(BF)


def serve_call(base, ids_col, table):
    return pl.pallas_call(
        serve_kernel,
        out_shape=jax.ShapeDtypeStruct((ids_col.shape[0], D), BF),
        in_specs=[SM, VM, VM],
        out_specs=VM,
        compiler_params=pltpu.CompilerParams(vmem_limit_bytes=VMEM_LIMIT),
        cost_estimate=pl.CostEstimate(flops=3 * GFLOP, bytes_accessed=3 << 20, transcendentals=0),
        name="serve_rows",
    )(base, ids_col, table)


def stream_kernel(grad_ref, head_ref, table_ref, back_ref, logit_ref):
    @pl.when(pl.program_id(0) == 0)
    def _():
        back_ref[...] = jnp.zeros_like(back_ref)

    back_ref[...] += mm(grad_ref[...], table_ref[...])
    logit_ref[...] = mm_nt(head_ref[...], table_ref[...]).astype(BF)


def stream_call(flat_grad, head_rows, table):
    vocab, masks = table.shape[0], flat_grad.shape[0]
    tile = 1024
    return pl.pallas_call(
        stream_kernel,
        grid=(vocab // tile,),
        out_shape=[jax.ShapeDtypeStruct((masks, D), F32), jax.ShapeDtypeStruct((masks, vocab), BF)],
        in_specs=[
            pl.BlockSpec((masks, tile), lambda i: (0, i)),
            pl.BlockSpec((masks, D), lambda i: (0, 0)),
            pl.BlockSpec((tile, D), lambda i: (i, 0)),
        ],
        out_specs=[pl.BlockSpec((masks, D), lambda i: (0, 0)), pl.BlockSpec((masks, tile), lambda i: (0, i))],
        compiler_params=pltpu.CompilerParams(vmem_limit_bytes=VMEM_LIMIT),
        cost_estimate=pl.CostEstimate(flops=10 * GFLOP, bytes_accessed=28 << 20, transcendentals=0),
        name="table_pass",
    )(flat_grad, head_rows, table)


def owner_kernel(base_ref, ids_ref, rows_ref, acc_ref, out_ref):
    counter = lax.broadcasted_iota(jnp.int32, (out_ref.shape[0], ids_ref.shape[1]), 0) + base_ref[0]
    out_ref[...] = (acc_ref[...] + mm((counter == ids_ref[...]).astype(BF), rows_ref[...])).astype(BF)


def owner_call(base, ids_row, rows, total):
    return pl.pallas_call(
        owner_kernel,
        out_shape=jax.ShapeDtypeStruct(total.shape, BF),
        in_specs=[SM, VM, VM, VM],
        out_specs=VM,
        compiler_params=pltpu.CompilerParams(vmem_limit_bytes=VMEM_LIMIT),
        cost_estimate=pl.CostEstimate(flops=3 * GFLOP, bytes_accessed=6 << 20, transcendentals=0),
        name="owner_sum",
    )(base, ids_row, rows, total)


def dense_kernel(base_ref, ids_ref, rows_ref, out_ref):
    @pl.when(pl.program_id(0) == 0)
    def _():
        out_ref[...] = jnp.zeros_like(out_ref)

    counter = lax.broadcasted_iota(jnp.int32, (out_ref.shape[0], N), 0) + base_ref[0]
    out_ref[...] += mm((counter == ids_ref[0]).astype(BF), rows_ref[0])


def dense_call(base, ids, rows, entries):
    return pl.pallas_call(
        dense_kernel,
        grid=(ids.shape[0],),
        out_shape=jax.ShapeDtypeStruct((entries, D), F32),
        in_specs=[SM, pl.BlockSpec((1, 1, N), lambda i: (i, 0, 0)), pl.BlockSpec((1, N, D), lambda i: (i, 0, 0))],
        out_specs=pl.BlockSpec((entries, D), lambda i: (0, 0)),
        compiler_params=pltpu.CompilerParams(vmem_limit_bytes=VMEM_LIMIT),
        name="dense_sum",
    )(base, ids, rows)


def partner(values, axis, bit):
    size = lax.axis_size(axis)
    return lax.ppermute(values, axis, [(i, i ^ bit) for i in range(size)])


def bits_of(axis):
    return [1 << b for b in range(lax.axis_size(axis).bit_length() - 1)]


def exclusive(place, stacked):
    count = stacked.shape[0]
    bit = 1
    while bit < count:
        paired = stacked.reshape((count // (2 * bit), 2, bit) + stacked.shape[1:])
        flipped = jnp.stack([paired[:, 1], paired[:, 0]], axis=1)
        stacked = jnp.where((place & bit) != 0, flipped, paired).reshape(stacked.shape)
        bit *= 2
    return stacked


def packed(weight):
    return jnp.swapaxes(weight, 0, 1).reshape(WIDE, D)


def per_device(
    token_ids,
    segment_ids,
    masked_pos,
    word_table,
    position_table,
    embed_gain,
    embed_bias,
    query_weight,
    key_weight,
    value_weight,
    output_weight,
    attention_gain,
    attention_bias,
    expand_weight,
    shrink_weight,
    feed_gain,
    feed_bias,
    logit_grad,
):
    section = lax.axis_index("section")
    place = lax.axis_index("dp")
    devices = lax.axis_size("dp")
    leading = section == 0
    shard_rows = word_table.shape[0]
    vocab = shard_rows * devices
    masks = masked_pos.shape[1]
    half = masks // 2
    room = max(16, 768 // devices)
    slots = room * devices
    base = (place * shard_rows).astype(jnp.int32).reshape(1)

    def swap(values):
        return lax.ppermute(values, "section", [(0, 1), (1, 0)])

    core = place % 2

    def after(values, *others):
        return lax.optimization_barrier((values, *others))[0]

    def exchange(values):
        return lax.all_to_all(values, "dp", 0, 0, tiled=True)

    ids = jnp.where(leading, token_ids[0], token_ids[1])
    table = lax.all_gather(word_table, "dp", axis=0, tiled=True)
    flat_grad = logit_grad.reshape(masks, vocab)

    def gather_by_exchange(array):
        if devices > 16:
            return lax.all_gather(array, "dp")
        return exchange(jnp.broadcast_to(array[None], (devices,) + array.shape))

    slot_col, slot_row, want, most = plan_call(ids, ids // shard_rows, room, slots)
    told = jnp.concatenate([want.reshape(devices, room), jnp.broadcast_to(most[:1, :16], (devices, 16))], axis=1)
    heard = exchange(told)
    asked = heard[:, :room].reshape(1, slots)
    served = serve_call(base, asked.reshape(slots, 1), word_table)
    slot_rows = exchange(served.reshape(devices, room, D)).reshape(slots, D)
    grad_parts = jnp.swapaxes(flat_grad.reshape(masks, devices, shard_rows), 0, 1)
    slot_rows, grad_parts = lax.optimization_barrier((slot_rows, grad_parts))

    most = after(jnp.max(heard[:, room:]).reshape(1, 1), served)
    most = jnp.maximum(most, swap(most))[0, 0]
    crowded = most > room
    flag = jnp.stack([section.astype(jnp.int32), crowded.astype(jnp.int32), core.astype(jnp.int32)])
    dense_rows = lax.cond(
        crowded,
        lambda: gather_by_exchange(word_table).reshape(vocab, D)[ids],
        lambda: jnp.zeros((N, D), BF),
    )

    vectors = jnp.concatenate([attention_gain, attention_bias, feed_gain, feed_bias, jnp.zeros((4, D), F32)], axis=0)
    own = (
        jnp.swapaxes(shrink_weight[0], 1, 2).reshape(D, D),
        expand_weight[0].reshape(D, D),
        output_weight[0],
        jnp.concatenate([packed(query_weight[0]), packed(key_weight[0]), packed(value_weight[0])], axis=0),
        vectors,
    )
    halves = []
    for array in own[:4]:
        rows = array.shape[0] // 2
        halves.append(swap(lax.dynamic_slice_in_dim(array, core * rows, rows, 0)))
    rest = [partner(array, "dp", 1) for array in halves]
    other = tuple(halves) + tuple(rest) + (swap(own[4]),)

    seg_row = jnp.where(leading, segment_ids[0], segment_ids[1])[None]
    mask_row = jnp.where(leading, masked_pos[0], masked_pos[1])[None]
    earlier = jnp.sum((seg_row < seg_row.T).astype(jnp.int32), axis=1)
    places = lax.iota(jnp.int32, N) - earlier
    embed_vec = jnp.stack([embed_gain, embed_bias])

    def chunked(arrays):
        return jnp.concatenate([array.reshape(devices, -1, D) for array in arrays], axis=1)

    def split_halves(values):
        mine = jnp.where(leading, values[:half], values[half:])
        theirs = jnp.where(leading, values[half:], values[:half])
        return mine, theirs

    def join_halves(mine, theirs):
        return jnp.where(leading, jnp.concatenate([mine, theirs]), jnp.concatenate([theirs, mine]))

    picked, saved0, saved1, hat_e, stat_e = forward_call(
        flag, slot_rows, dense_rows, slot_col, places[:, None], seg_row.T, seg_row, mask_row.T, position_table, embed_vec, own, other
    )
    mine, theirs = split_halves(picked)
    head_rows = join_halves(mine, swap(theirs))
    small = devices <= 16
    heads = [partner(head_rows, "dp", 4 * step) for step in (1, 2, 3)] if small else [lax.all_gather(head_rows, "dp", axis=0)]
    rows_back, logits = stream_call(flat_grad, head_rows, table)
    logits = logits.reshape(2, half, vocab)
    rows_back, heads = lax.optimization_barrier((rows_back, heads))
    if small:
        heads = jnp.stack([head_rows] + heads)
        heads = [heads, partner(heads, "dp", 2)]
    grad_parts = after(grad_parts, rows_back)
    grad_rows = exchange(grad_parts).reshape(devices * masks, shard_rows)
    mine, theirs = split_halves(rows_back)
    picked_back = join_halves(mine, swap(theirs)).astype(BF)

    def spread_on(array):
        if devices <= 16:
            return array
        groups = [list(range(low, devices, 16)) for low in range(16)]
        return lax.psum(array.astype(F32), "dp", axis_index_groups=groups).astype(BF)

    low_place = (place % 16).astype(jnp.int32).reshape(1)
    side_y = ((place // 2) % 2).astype(jnp.int32).reshape(1)
    me_z = ((place // 4) % 4).astype(jnp.int32).reshape(1)

    def across_z(parts):
        return [spread_on(parts[0])] + [partner(spread_on(parts[step]), "dp", 4 * step) for step in (1, 2, 3)]

    keep_a1, away_a1, attn1, low1, vec1 = backward_a_call(False, flag, [picked_back, mask_row], own, other, saved1)
    came = partner(away_a1, "dp", 1)
    keep_b1, away_b1, middle = backward_b_call(False, flag, [attn1, low1, vec1], own, other, saved1)
    middle, came, heads = lax.optimization_barrier((middle, came, heads))
    if small:
        heads = jnp.concatenate(heads)
        heads = [heads, partner(heads, "dp", 1)]
    keep_a1, away_a1 = step_y(side_y, keep_a1, came)
    middle, away_a1 = lax.optimization_barrier((middle, away_a1))
    came_a = partner(away_a1, "dp", 2)
    came_b = partner(away_b1, "dp", 1)
    keep_a0, away_a0, attn0, low0, vec0 = backward_a_call(True, flag, [middle], own, other, saved0)
    attn0, came_a, came_b, grad_rows = lax.optimization_barrier((attn0, came_a, came_b, grad_rows))
    parts_a1 = across_z(step_z(me_z, keep_a1, came_a))
    keep_b1, away_b1 = step_y(side_y, keep_b1, came_b)
    came_b = partner(away_b1, "dp", 2)
    came_a = partner(away_a0, "dp", 1)
    keep_b0, away_b0, back, slot_grad = backward_b_call(
        True, flag, [attn0, low0, vec0, slot_row, places[None], hat_e, stat_e, embed_vec], own, other, saved0, slots
    )
    slot_grad, away_b0, parts_a1, came_a, came_b = lax.optimization_barrier((slot_grad, away_b0, parts_a1, came_a, came_b))
    keep_a0, away_a0 = step_y(side_y, keep_a0, came_a)
    away_a0, slot_grad, away_b0, keep_b1, parts_a1, heads = lax.optimization_barrier(
        (away_a0, slot_grad, away_b0, keep_b1, parts_a1, heads)
    )
    came_a = partner(away_a0, "dp", 2)
    if small:
        heads = jnp.concatenate(heads)
        every_head = exclusive(place, jnp.stack([heads[c * 8 + b * 4 + z] for z in range(4) for b in range(2) for c in range(2)]))
    else:
        every_head = heads[0]
    every_head = every_head.reshape(devices * masks, D)
    table_back = lax.dot_general(grad_rows, every_head, (((0,), (0,)), ((), ())), preferred_element_type=F32)

    sent = exchange(slot_grad.reshape(devices, room, D)).reshape(slots, D)
    crowd_sum = lax.cond(
        crowded,
        lambda: dense_call(base, gather_by_exchange(ids[None]), gather_by_exchange(back), shard_rows),
        lambda: jnp.zeros((shard_rows, D), F32),
    )
    names = jnp.where(crowded, -1, asked)
    partial = owner_call(base, names, sent, table_back + crowd_sum)
    parts_b1 = across_z(step_z(me_z, keep_b1, came_b))
    came_b = partner(away_b0, "dp", 1)
    parts_a0 = across_z(step_z(me_z, keep_a0, came_a))
    partial, parts_a0 = lax.optimization_barrier((partial, parts_a0))
    keep_b0, away_b0 = step_y(side_y, keep_b0, came_b)
    came_b = partner(away_b0, "dp", 2)
    parts_b0 = across_z(step_z(me_z, keep_b0, came_b))

    def to_all(mine, theirs):
        chunk = (mine.astype(F32) + theirs.astype(F32)).astype(BF)
        held = jnp.stack([chunk] + [partner(chunk, "dp", 4 * step) for step in (1, 2, 3)])
        held = jnp.concatenate([held, partner(held, "dp", 2)])
        return held, partner(held, "dp", 1)

    mine_a, theirs_a = finish_call(0, flag, low_place, parts_a1, parts_a0)
    theirs_a = swap(theirs_a)
    mine_b, theirs_b = finish_call(1, flag, low_place, parts_b1, parts_b0)
    theirs_b = swap(theirs_b)
    partial, theirs_b = lax.optimization_barrier((partial, theirs_b))
    table_total = partial.astype(F32) + swap(partial).astype(F32)
    shrink_total, expand_total, output_total, query_total, key_total, value_total, vec_total, embed_total, position_total = unpack_call(
        flag, low_place, *to_all(mine_a, theirs_a), *to_all(mine_b, theirs_b)
    )
    embed_total = embed_total.reshape(2, D // 2)
    return (
        logits,
        table_total,
        position_total,
        embed_total[0],
        embed_total[1],
        query_total[None],
        key_total[None],
        value_total[None],
        output_total[None],
        vec_total[0:1],
        vec_total[1:2],
        expand_total.reshape(1, GROUPS, WIDE, D),
        jnp.swapaxes(shrink_total.reshape(1, GROUPS, WIDE, D), 2, 3),
        vec_total[2:3],
        vec_total[3:4],
    )


def solution(mesh):
    placed = (
        P("dp", None),
        P("dp", None),
        P("dp", None),
        P("dp", None),
        P(),
        P(),
        P(),
        P("section", None, None, None),
        P("section", None, None, None),
        P("section", None, None, None),
        P("section", None, None),
        P("section", None),
        P("section", None),
        P("section", None, None, None),
        P("section", None, None, None),
        P("section", None),
        P("section", None),
        P("dp", "section", None),
    )
    return jax.shard_map(
        per_device,
        mesh=mesh,
        in_specs=placed,
        out_specs=(
            P("dp", "section", None),
            P("dp", None),
            P(None, "section"),
            P("section"),
            P("section"),
            P("section", None, None, None),
            P("section", None, None, None),
            P("section", None, None, None),
            P("section", None, None),
            P("section", None),
            P("section", None),
            P("section", None, None, None),
            P("section", None, None, None),
            P("section", None),
            P("section", None),
        ),
        check_vma=False,
    )
```

```python
import functools
import jax
import jax.numpy as jnp
from jax import lax
from jax.sharding import PartitionSpec as P
from jax.experimental import pallas as pl
from jax.experimental.pallas import tpu as pltpu

HEAD = 64
norm_eps = 1e-06
BF = jnp.bfloat16
F32 = jnp.float32
LANE = 128
N = 512
D = 768
FF = 3072
GROUPS = 4
WIDE = 192
HEADS = 12
PAIRS = 6
VMEM_LIMIT = 60 * 1024 * 1024
QKV_ROWS = 768
CHUNKS = 16
ROWS_A = 144
ROWS_B = 48
SLAB = 16
GFLOP = 10 ** 9


def mm(a, b):
    return lax.dot_general(a, b, (((1,), (0,)), ((), ())), preferred_element_type=F32)


def mm_nt(a, b):
    return lax.dot_general(a, b, (((1,), (1,)), ((), ())), preferred_element_type=F32)


def mm_tn(a, b):
    return lax.dot_general(a, b, (((0,), (0,)), ((), ())), preferred_element_type=F32)


def window(group):
    return 384 * (group // 2) + 128 * (group % 2)


def lanes(group):
    return slice(window(group), window(group) + 256)


def own_lanes(group):
    counter = lax.broadcasted_iota(jnp.int32, (1, 256), 1)
    return counter < WIDE if group % 2 == 0 else counter >= 64


def fetch_weights(refs, own, other, use_own, core, sems):
    shrink, expand, output, qkv, vecs = refs
    mine, rest = other[0:4], other[4:8]

    def copies(sources, halves):
        made = []
        for number in range(2):
            half = halves[number]
            shrink_src, expand_src, output_src, qkv_src = sources[number]
            for j in range(2 if shrink is not None else 0):
                made.append(pltpu.make_async_copy(shrink_src.at[pl.ds(j * WIDE, WIDE)], shrink.at[2 * half + j, pl.ds(64 * j, WIDE)], sems.at[6 * number + j]))
                made.append(pltpu.make_async_copy(expand_src.at[pl.ds(j * WIDE, WIDE)], expand.at[2 * half + j, pl.ds(64 * j, WIDE)], sems.at[6 * number + 2 + j]))
            if output is not None:
                made.append(pltpu.make_async_copy(output_src, output.at[pl.ds(pl.multiple_of(half * 384, 384), 384)], sems.at[6 * number + 4]))
            if qkv is not None:
                made.append(pltpu.make_async_copy(qkv_src, qkv.at[pl.ds(pl.multiple_of(half * 288, 288), 288)], sems.at[6 * number + 5]))
        return made

    halves_of = [[ref.at[pl.ds(h * (ref.shape[0] // 2), ref.shape[0] // 2)] for ref in own[0:4]] for h in range(2)]
    whole = copies(halves_of, (0, 1))
    parts = copies((mine, rest), (core, 1 - core))
    if vecs is not None:
        whole.append(pltpu.make_async_copy(own[4], vecs, sems.at[12]))
        parts.append(pltpu.make_async_copy(other[8], vecs, sems.at[12]))

    @pl.when(use_own)
    def _():
        for c in whole:
            c.start()

    @pl.when(jnp.logical_not(use_own))
    def _():
        for c in parts:
            c.start()

    for g in range(GROUPS if shrink is not None else 0):
        at = WIDE * (1 - g % 2)
        shrink[g, at : at + 64, :] = jnp.zeros((64, D), BF)
        expand[g, at : at + 64, :] = jnp.zeros((64, D), BF)
    return whole


def pad_qkv(qkv, padded):
    for which in range(3):
        for g in range(GROUPS):
            at = 64 * (g % 2)
            block = qkv[which * WIDE : (which + 1) * WIDE, lanes(g)]
            padded[which, g, at : at + WIDE, :] = jnp.where(own_lanes(g), block, jnp.zeros_like(block))
            gap = WIDE * (1 - g % 2)
            padded[which, g, gap : gap + 64, :] = jnp.zeros((64, 256), BF)


def norm_parts(values):
    centre = jnp.mean(values, axis=-1, keepdims=True)
    shifted = values - centre
    spread = jnp.mean(shifted * shifted, axis=-1, keepdims=True)
    rstd = lax.rsqrt(spread + norm_eps)
    return shifted * rstd, rstd


def norm_back(gradient, hat, rstd, gain):
    scaled = gradient * gain
    first = jnp.mean(scaled, axis=-1, keepdims=True)
    second = jnp.mean(scaled * hat, axis=-1, keepdims=True)
    return rstd * (scaled - first - hat * second)


def join_pair(low, high):
    return jnp.concatenate([low[:, :128], low[:, 128:] + high[:, :128], high[:, 128:]], axis=1)


def layer_fwd(x_ref, bias_ref, w, saves, stats_ref, grow_ref, save_done):
    shrink, expand, output, qkv_pad, vecs = w
    x_low, q_ref, k_ref, v_ref, e_ref, mix_ref, hat_a, hidden_low, active, slope, hat_f, inv_ref, full_ref = saves
    x_low[...] = x_ref[...].astype(BF)
    for which, target in enumerate((q_ref, k_ref, v_ref)):
        for p in range(2):
            low = mm(x_low[:, lanes(2 * p)], qkv_pad[which, 2 * p])
            high = mm(x_low[:, lanes(2 * p + 1)], qkv_pad[which, 2 * p + 1])
            joined = join_pair(low, high).astype(BF)
            if which == 0:
                joined = joined * jnp.asarray(HEAD ** (-0.5), BF)
            target[:, 384 * p : 384 * (p + 1)] = joined
    save_done(0)
    stats_ref[...] = jnp.zeros_like(stats_ref)
    lane = lax.broadcasted_iota(jnp.int32, (1, LANE), 1)

    def pair_body(p, carry):
        at = pl.ds(pl.multiple_of(p * LANE, LANE), LANE)
        qs, ks, vs = q_ref[:, at], k_ref[:, at], v_ref[:, at]
        outs = []
        for side in range(2):
            mine = (lane < HEAD) if side == 0 else (lane >= HEAD)
            scores = mm_nt(jnp.where(mine, qs, jnp.zeros_like(qs)), ks) + bias_ref[...]
            top = jnp.max(scores, axis=-1, keepdims=True)
            e = jnp.exp(scores - top).astype(BF)
            e_ref[2 * p + side] = e
            outs.append(mm(e, jnp.where(mine, vs, jnp.ones_like(vs))))
        inv = 1.0 / pltpu.roll(jnp.where(lane < HEAD, outs[1], outs[0]), HEAD, 1)
        full = jnp.where(lane < HEAD, outs[0], outs[1]) * inv
        inv_ref[:, at] = inv
        full_ref[:, at] = full
        mix_ref[:, at] = full.astype(BF)
        return carry

    lax.fori_loop(0, PAIRS, pair_body, 0)
    save_done(1)
    residual = x_ref[...] + mm(mix_ref[...], output[...])
    hat, rstd = norm_parts(residual)
    hat_a[...] = hat.astype(BF)
    stats_ref[...] = jnp.where(lane == 12, rstd, stats_ref[...])
    hidden = hat * vecs[0:1, :] + vecs[1:2, :]
    hidden_low[...] = hidden.astype(BF)
    grow_ref[...] = hidden
    for g in range(GROUPS):
        wide = slice(g * D, (g + 1) * D)
        expanded = mm(hidden_low[:, lanes(g)], expand[g])
        phi = 0.5 * (1.0 + lax.erf(expanded * (2.0 ** -0.5)))
        density = jnp.exp(expanded * expanded * -0.5) * (2.0 * jnp.pi) ** -0.5
        act = (expanded * phi).astype(BF)
        active[:, wide] = act
        slope[:, wide] = (phi + expanded * density).astype(BF)
        grow_ref[:, lanes(g)] += mm_nt(act, shrink[g])
    save_done(2)
    hat, rstd = norm_parts(grow_ref[...])
    hat_f[...] = hat.astype(BF)
    stats_ref[...] = jnp.where(lane == 13, rstd, stats_ref[...])
    x_ref[...] = hat * vecs[2:3, :] + vecs[3:4, :]
    save_done(3)


SAVE_SHAPES = (
    (N, D), (N, D), (N, D), (N, D), (HEADS, N, N), (N, D), (N, D), (N, D), (N, FF), (N, FF), (N, D),
    (N, D), (N, D), (N, LANE),
)
SAVE_TYPES = (BF,) * 11 + (F32,) * 3
SAVE_STAGES = ((0, 1, 2, 3), (4, 5, 11, 12), (6, 7, 8, 9), (10, 13))
SAVES = 14


def weight_scratch():
    return [
        pltpu.VMEM((GROUPS, 256, D), BF),
        pltpu.VMEM((GROUPS, 256, D), BF),
        pltpu.VMEM((D, D), BF),
        pltpu.VMEM((3 * WIDE, D), BF),
        pltpu.VMEM((8, D), F32),
    ]


def fwd_kernel(flag, slot_rows, dense_rows, slot_col, place_col, seg_col, seg_row, mask_col, place_table, embed_vec, *rest):
    rest = list(rest)

    def take(n):
        got = rest[:n]
        del rest[:n]
        return got

    own, other = take(5), take(9)
    (picked_ref,) = take(1)
    outs = [take(SAVES), take(SAVES)]
    hat_e_ref, stat_e_ref = take(2)
    weights = [take(5), take(5)]
    qkv_pad, bias_ref, x_ref, grow_ref = take(4)
    saves = take(SAVES)
    sem_w, sem_s, sem_d = take(3)
    leading = flag[0] == 0
    waits = [
        fetch_weights(weights[0], own, other, leading, flag[2], sem_w.at[0]),
        fetch_weights(weights[1], own, other, jnp.logical_not(leading), flag[2], sem_w.at[1]),
    ]
    counter = lax.broadcasted_iota(jnp.int32, (N, N), 1)
    one_hot = (place_col[...] == counter).astype(BF)
    slots = slot_rows.shape[0]
    wanted = (slot_col[...] == lax.broadcasted_iota(jnp.int32, (N, slots), 1)).astype(BF)
    x_ref[...] = mm(wanted, slot_rows[...])

    @pl.when(flag[1] != 0)
    def _():
        c = pltpu.make_async_copy(dense_rows, saves[0], sem_d)
        c.start()
        c.wait()
        x_ref[...] = saves[0][...].astype(F32)

    summed = x_ref[...] + mm(one_hot, place_table[...])
    hat, rstd = norm_parts(summed)
    hat_e_ref[...] = hat.astype(BF)
    stat_e_ref[...] = jnp.broadcast_to(rstd, (N, LANE))
    x_ref[...] = hat * embed_vec[0:1, :] + embed_vec[1:2, :]
    bias_ref[...] = jnp.where(seg_col[...] == seg_row[...], 0.0, -1000000000.0)
    drains = []
    for number in range(2):
        for c in waits[number] + drains:
            c.wait()
        drains = []
        shrink, expand, output, qkv, vecs = weights[number]
        pad_qkv(qkv, qkv_pad)

        def save_done(stage, number=number, drains=drains):
            for i in SAVE_STAGES[stage]:
                c = pltpu.make_async_copy(saves[i], outs[number][i], sem_s.at[number, i])
                c.start()
                drains.append(c)

        layer_fwd(
            x_ref, bias_ref, (shrink, expand, output, qkv_pad, vecs),
            saves[:13], saves[13], grow_ref, save_done,
        )
        if number == 0:
            x_ref[...] = x_ref[...].astype(BF).astype(F32)
    picks = (mask_col[...] == lax.broadcasted_iota(jnp.int32, (mask_col.shape[0], N), 1)).astype(BF)
    picked_ref[...] = mm(picks, x_ref[...].astype(BF)).astype(BF)
    for c in drains:
        c.wait()


def save_structs():
    return [jax.ShapeDtypeStruct(s, t) for s, t in zip(SAVE_SHAPES, SAVE_TYPES)]


def save_scratch():
    return [pltpu.VMEM(s, t) for s, t in zip(SAVE_SHAPES, SAVE_TYPES)]


VM = pl.BlockSpec(memory_space=pltpu.VMEM)
HB = pl.BlockSpec(memory_space=pl.ANY)
SM = pl.BlockSpec(memory_space=pltpu.SMEM)


def forward_call(flag, slot_rows, dense_rows, slot_col, place_col, seg_col, seg_row, mask_col, place_table, embed_vec, own, other):
    masks = mask_col.shape[0]
    out = pl.pallas_call(
        fwd_kernel,
        out_shape=[jax.ShapeDtypeStruct((masks, D), BF)] + save_structs() * 2
        + [jax.ShapeDtypeStruct((N, D), BF), jax.ShapeDtypeStruct((N, LANE), F32)],
        in_specs=[SM, VM, HB] + [VM] * 7 + [HB] * 14,
        out_specs=[VM] + [HB] * (2 * SAVES) + [VM] * 2,
        scratch_shapes=weight_scratch() * 2
        + [pltpu.VMEM((3, GROUPS, 256, 256), BF), pltpu.VMEM((N, N), F32), pltpu.VMEM((N, D), F32), pltpu.VMEM((N, D), F32)]
        + save_scratch()
        + [pltpu.SemaphoreType.DMA((2, 13)), pltpu.SemaphoreType.DMA((2, SAVES)), pltpu.SemaphoreType.DMA],
        compiler_params=pltpu.CompilerParams(vmem_limit_bytes=VMEM_LIMIT),
        cost_estimate=pl.CostEstimate(flops=36 * GFLOP, bytes_accessed=60 << 20, transcendentals=0),
        name="forward_layers",
    )(flag, slot_rows, dense_rows, slot_col, place_col, seg_col, seg_row, mask_col, place_table, embed_vec, *own, *other)
    return out[0], out[1 : 1 + SAVES], out[1 + SAVES : 1 + 2 * SAVES], out[-2], out[-1]


def chunk_place(chunk, core, in_order):
    if in_order:
        return chunk
    return chunk // 2 + (CHUNKS // 2) * (core if chunk % 2 == 0 else 1 - core)


def put_chunks(packed_ref, core, in_order, source, rows, at):
    for chunk in range(CHUNKS):
        packed_ref[chunk_place(chunk, core, in_order), at : at + rows, :] = source[chunk * rows : (chunk + 1) * rows, :].astype(BF)


def ship_chunks(packed_ref, outs, sems):
    if len(outs) == 1:
        made = [pltpu.make_async_copy(packed_ref, outs[0], sems.at[0])]
    else:
        half = CHUNKS // 2
        made = [pltpu.make_async_copy(packed_ref.at[pl.ds(i * half, half)], outs[i], sems.at[i]) for i in range(2)]
    for c in made:
        c.start()
    return made


def bwd_a_kernel(last, flag, *rest):
    rest = list(rest)

    def take(n):
        got = rest[:n]
        del rest[:n]
        return got

    if last:
        (go_in,) = take(1)
    else:
        picked_back, mask_row = take(2)
    own, other = take(5), take(9)
    sources = take(7)
    packed_out = take(1 if last else 2)
    attn_ref, back_low, vec_ref = take(3)
    weights = take(4)
    mid_ref, low_ref, packed_ref = take(3)
    saves = take(7)
    sem_w, sem_s, sem_o, sem_g = take(4)
    mix_ref, hat_a, hidden_low, active, slope, hat_f, stats_ref = saves
    shrink, expand, output, vecs = weights
    leading, core = flag[0] == 0, flag[2]
    use_own = leading if last else jnp.logical_not(leading)
    copies = [pltpu.make_async_copy(sources[i], saves[i], sem_s.at[i]) for i in range(7)]
    wide_copies = []
    for g in range(GROUPS):
        at = pl.ds(g * D, D)
        wide_copies.append([pltpu.make_async_copy(sources[i].at[:, at], saves[i].at[:, at], sem_g.at[i - 3, g]) for i in (3, 4)])
    for i in (5, 6):
        copies[i].start()
    waits = fetch_weights((shrink, expand, output, None, vecs), own, other, use_own, core, sem_w)
    copies[2].start()
    for pair in wide_copies:
        for c in pair:
            c.start()
    for i in (1, 0):
        copies[i].start()
    vec_ref[...] = jnp.zeros_like(vec_ref)
    if last:
        go = go_in[...].astype(F32)
    else:
        masks = mask_row.shape[1]
        spread = (lax.broadcasted_iota(jnp.int32, (N, masks), 0) == mask_row[...]).astype(BF)
        go = mm(spread, picked_back[...])
    lane = lax.broadcasted_iota(jnp.int32, (1, LANE), 1)

    def stat(index):
        return jnp.sum(jnp.where(lane == index, stats_ref[...], 0.0), axis=-1, keepdims=True)

    copies[5].wait()
    copies[6].wait()
    for c in waits:
        c.wait()
    hat = hat_f[...].astype(F32)
    vec_ref[2:3, :] = jnp.sum(go * hat, axis=0, keepdims=True)
    vec_ref[3:4, :] = jnp.sum(go, axis=0, keepdims=True)
    feed_back = norm_back(go, hat, stat(13), vecs[2:3, :])
    mid_ref[...] = feed_back
    low_ref[...] = feed_back.astype(BF)
    copies[2].wait()
    each = WIDE // (CHUNKS // GROUPS)
    for g in range(GROUPS):
        wide = slice(g * D, (g + 1) * D)
        rows = slice(64 * (g % 2), 64 * (g % 2) + WIDE)
        for c in wide_copies[g]:
            c.wait()
        shrink_in = low_ref[:, lanes(g)]
        shrink_grad = mm_tn(shrink_in, active[:, wide])[rows].astype(BF)
        expand_in = (mm(shrink_in, shrink[g]) * slope[:, wide].astype(F32)).astype(BF)
        expand_grad = mm_tn(hidden_low[:, lanes(g)], expand_in)[rows].astype(BF)
        mid_ref[:, lanes(g)] += mm_nt(expand_in, expand[g])
        for part in range(CHUNKS // GROUPS):
            chunk = g * (CHUNKS // GROUPS) + part
            at = chunk_place(chunk, core, last)
            packed_ref[at, 0:each, :] = shrink_grad[part * each : (part + 1) * each, :]
            packed_ref[at, each : 2 * each, :] = expand_grad[part * each : (part + 1) * each, :]
    copies[1].wait()
    hidden_back = mid_ref[...]
    hat = hat_a[...].astype(F32)
    vec_ref[0:1, :] = jnp.sum(hidden_back * hat, axis=0, keepdims=True)
    vec_ref[1:2, :] = jnp.sum(hidden_back, axis=0, keepdims=True)
    attn_back = norm_back(hidden_back, hat, stat(12), vecs[0:1, :])
    attn_ref[...] = attn_back
    attended_in = attn_back.astype(BF)
    copies[0].wait()
    put_chunks(packed_ref, core, last, mm_tn(mix_ref[...], attended_in), each, 2 * each)
    ship = ship_chunks(packed_ref, packed_out, sem_o)
    back_low[...] = mm_nt(attended_in, output[...]).astype(BF)
    for c in ship:
        c.wait()


def backward_a_call(last, flag, extra, own, other, saved):
    chosen = (5, 6, 7, 8, 9, 10, 13)
    return pl.pallas_call(
        functools.partial(bwd_a_kernel, last),
        out_shape=([jax.ShapeDtypeStruct((CHUNKS, ROWS_A, D), BF)] if last else [jax.ShapeDtypeStruct((CHUNKS // 2, ROWS_A, D), BF)] * 2)
        + [
            jax.ShapeDtypeStruct((N, D), F32), jax.ShapeDtypeStruct((N, D), BF), jax.ShapeDtypeStruct((16, D), F32),
        ],
        in_specs=[SM] + [VM] * len(extra) + [HB] * (14 + len(chosen)),
        out_specs=[HB] * (1 if last else 2) + [VM, VM, VM],
        scratch_shapes=[
            pltpu.VMEM((GROUPS, 256, D), BF), pltpu.VMEM((GROUPS, 256, D), BF), pltpu.VMEM((D, D), BF), pltpu.VMEM((8, D), F32),
            pltpu.VMEM((N, D), F32), pltpu.VMEM((N, D), BF), pltpu.VMEM((CHUNKS, ROWS_A, D), BF),
        ]
        + [pltpu.VMEM(SAVE_SHAPES[i], SAVE_TYPES[i]) for i in chosen]
        + [pltpu.SemaphoreType.DMA((13,)), pltpu.SemaphoreType.DMA((len(chosen),)), pltpu.SemaphoreType.DMA((2,)), pltpu.SemaphoreType.DMA((2, GROUPS))],
        compiler_params=pltpu.CompilerParams(vmem_limit_bytes=VMEM_LIMIT),
        cost_estimate=pl.CostEstimate(flops=12 * GFLOP, bytes_accessed=20 << 20, transcendentals=0),
        name="backward_first_a" if last else "backward_second_a",
    )(flag, *extra, *own, *other, *[saved[i] for i in chosen])


def bwd_b_kernel(last, flag, attn_in, back_low, vec_in, *rest):
    rest = list(rest)

    def take(n):
        got = rest[:n]
        del rest[:n]
        return got

    if last:
        slot_row, place_row, hat_e_ref, stat_e_ref, embed_vec = take(5)
    own, other = take(5), take(9)
    sources = take(7)
    keep_out, away_out, back_ref = take(3)
    if last:
        (slot_grad,) = take(1)
    qkv, qkv_pad, go_ref, vec_ref, packed_ref = take(5)
    dq_ref, dk_ref, dv_ref, grad_ref = take(4)
    saves = take(7)
    sem_w, sem_s, sem_o = take(3)
    x_low, q_ref, k_ref, v_ref, e_ref, inv_ref, full_ref = saves
    leading, core = flag[0] == 0, flag[2]
    use_own = leading if last else jnp.logical_not(leading)
    whole = pltpu.make_async_copy(sources[0], saves[0], sem_s.at[0, 0])

    def pair_copies(p):
        at = pl.ds(p * LANE if isinstance(p, int) else pl.multiple_of(p * LANE, LANE), LANE)
        made = [pltpu.make_async_copy(sources[4].at[pl.ds(2 * p, 2)], saves[4].at[pl.ds(2 * p, 2)], sem_s.at[4, p])]
        for i in (1, 2, 3, 5, 6):
            made.append(pltpu.make_async_copy(sources[i].at[:, at], saves[i].at[:, at], sem_s.at[i, p]))
        return made

    for p in range(PAIRS):
        for c in pair_copies(p):
            c.start()
    waits = fetch_weights((None, None, None, qkv, None), own, other, use_own, core, sem_w)
    whole.start()
    lane = lax.broadcasted_iota(jnp.int32, (1, LANE), 1)

    def pair_body(p, carry):
        for c in pair_copies(p):
            c.wait()
        at = pl.ds(pl.multiple_of(p * LANE, LANE), LANE)
        first = lane < HEAD
        d_low = (back_low[:, at].astype(F32) * inv_ref[:, at]).astype(BF)
        weighted = d_low.astype(F32) * full_ref[:, at]
        qs, ks, vs = q_ref[:, at], k_ref[:, at], v_ref[:, at]
        d_v = d_q = d_k = None
        for side in range(2):
            mine = first if side == 0 else jnp.logical_not(first)
            delta = jnp.sum(jnp.where(mine, weighted, 0.0), axis=-1, keepdims=True)
            e = e_ref[2 * p + side]
            d_side = jnp.where(mine, d_low, jnp.zeros_like(d_low))
            prob_back = mm_nt(d_side, vs)
            d_s = (e.astype(F32) * (prob_back - delta)).astype(BF)
            part_v = mm_tn(e, d_side)
            part_q = mm(d_s, jnp.where(mine, ks, jnp.zeros_like(ks)))
            part_k = mm_tn(d_s, jnp.where(mine, qs, jnp.zeros_like(qs)))
            d_v = part_v if d_v is None else d_v + part_v
            d_q = part_q if d_q is None else d_q + part_q
            d_k = part_k if d_k is None else d_k + part_k
        dv_ref[:, at] = d_v.astype(BF)
        dq_ref[:, at] = (d_q * HEAD ** (-0.5)).astype(BF)
        dk_ref[:, at] = d_k.astype(BF)
        return carry

    lax.fori_loop(0, PAIRS, pair_body, 0)
    whole.wait()
    for c in waits:
        c.wait()
    pad_qkv(qkv, qkv_pad)
    go_ref[...] = attn_in[...]
    vec_ref[...] = jnp.zeros_like(vec_ref)
    vec_ref[0:8, :] = vec_in[0:8, :]
    for which, d_ref in enumerate((dq_ref, dk_ref, dv_ref)):
        for p in range(2):
            made = []
            for g in (2 * p, 2 * p + 1):
                rows = slice(64 * (g % 2), 64 * (g % 2) + WIDE)
                d_part = d_ref[:, lanes(g)]
                made.append(jnp.where(own_lanes(g), mm_tn(x_low[:, lanes(g)], d_part)[rows], 0.0))
                go_ref[:, lanes(g)] += mm_nt(d_part, qkv_pad[which, g])
            grad_ref[which * WIDE : (which + 1) * WIDE, 384 * p : 384 * (p + 1)] = join_pair(*made).astype(BF)
    go = go_ref[...]
    if last:
        hat = hat_e_ref[...].astype(F32)
        gain_row = jnp.sum(go * hat, axis=0, keepdims=True)
        bias_row = jnp.sum(go, axis=0, keepdims=True)
        for s in range(2):
            at = slice(s * (D // 2), (s + 1) * (D // 2))
            vec_ref[8 + s : 9 + s, :] = jnp.concatenate([gain_row[:, at], bias_row[:, at]], axis=1)
        back = norm_back(go, hat, stat_e_ref[:, 0:1], embed_vec[0:1, :]).astype(BF)
        back_ref[...] = back
        places = (lax.broadcasted_iota(jnp.int32, (N, N), 0) == place_row[...]).astype(BF)
        grad = mm(places, back).astype(BF)
        for s in range(2):
            block = jnp.concatenate([grad[part * (N // 2) : (part + 1) * (N // 2), s * 384 : (s + 1) * 384] for part in range(2)], axis=1)
            put_chunks(packed_ref, core, False, block, SLAB, ROWS_B + s * SLAB)
        slots = slot_grad.shape[0]
        slot_grad[...] = mm((lax.broadcasted_iota(jnp.int32, (slots, N), 0) == slot_row[...]).astype(BF), back).astype(BF)
    else:
        back_ref[...] = go.astype(BF)
    grad_ref[3 * WIDE :, :] = vec_ref[...].astype(BF)
    put_chunks(packed_ref, core, False, grad_ref, ROWS_B, 0)
    for c in ship_chunks(packed_ref, (keep_out, away_out), sem_o):
        c.wait()


def backward_b_call(last, flag, extra, own, other, saved, slots=0):
    chosen = (0, 1, 2, 3, 4, 11, 12)
    rows = ROWS_B + 2 * SLAB if last else ROWS_B
    out_shape = [
        jax.ShapeDtypeStruct((CHUNKS // 2, rows, D), BF), jax.ShapeDtypeStruct((CHUNKS // 2, rows, D), BF),
        jax.ShapeDtypeStruct((N, D), BF),
    ]
    if last:
        out_shape.append(jax.ShapeDtypeStruct((slots, D), BF))
    return pl.pallas_call(
        functools.partial(bwd_b_kernel, last),
        out_shape=out_shape,
        in_specs=[SM] + [VM] * len(extra) + [HB] * (14 + len(chosen)),
        out_specs=[HB, HB] + [VM] * (len(out_shape) - 2),
        scratch_shapes=[
            pltpu.VMEM((3 * WIDE, D), BF), pltpu.VMEM((3, GROUPS, 256, 256), BF), pltpu.VMEM((N, D), F32),
            pltpu.VMEM((QKV_ROWS - 3 * WIDE, D), F32), pltpu.VMEM((CHUNKS, rows, D), BF),
        ]
        + [pltpu.VMEM((N, D), BF)] * 3 + [pltpu.VMEM((QKV_ROWS, D), BF)]
        + [pltpu.VMEM(SAVE_SHAPES[i], SAVE_TYPES[i]) for i in chosen]
        + [pltpu.SemaphoreType.DMA((13,)), pltpu.SemaphoreType.DMA((len(chosen), PAIRS)), pltpu.SemaphoreType.DMA((2,))],
        compiler_params=pltpu.CompilerParams(vmem_limit_bytes=VMEM_LIMIT),
        cost_estimate=pl.CostEstimate(flops=15 * GFLOP, bytes_accessed=20 << 20, transcendentals=0),
        name="backward_first_b" if last else "backward_second_b",
    )(flag, *extra, *own, *other, *[saved[i] for i in chosen])


def step_y_kernel(side_ref, keep_ref, came_ref, next_keep, next_away):
    side = side_ref[0]
    for j in range(next_keep.shape[0]):
        for target, which in ((next_keep, side), (next_away, 1 - side)):
            at = 2 * j + which
            target[j] = (keep_ref[at].astype(F32) + came_ref[at].astype(F32)).astype(BF)


def step_y(side, keep, came):
    half = jax.ShapeDtypeStruct((keep.shape[0] // 2,) + keep.shape[1:], BF)
    return pl.pallas_call(
        step_y_kernel, out_shape=[half, half], in_specs=[SM, VM, VM], out_specs=[VM, VM],
        compiler_params=pltpu.CompilerParams(vmem_limit_bytes=VMEM_LIMIT),
        cost_estimate=pl.CostEstimate(flops=GFLOP, bytes_accessed=6 << 20, transcendentals=0), name="halve_chunks",
    )(side, keep, came)


def step_z_kernel(me_ref, keep_ref, came_ref, *outs):
    for step in range(4):
        at = me_ref[0] ^ step
        outs[step][...] = (keep_ref[at].astype(F32) + came_ref[at].astype(F32)).astype(BF)


def step_z(me, keep, came):
    one = jax.ShapeDtypeStruct(keep.shape[1:], BF)
    return pl.pallas_call(
        step_z_kernel, out_shape=[one] * 4, in_specs=[SM, VM, VM], out_specs=[VM] * 4,
        compiler_params=pltpu.CompilerParams(vmem_limit_bytes=VMEM_LIMIT),
        cost_estimate=pl.CostEstimate(flops=GFLOP, bytes_accessed=4 << 20, transcendentals=0), name="four_chunks",
    )(me, keep, came)


def finish_kernel(part, count1, flag, place_ref, *refs):
    parts1, parts0 = refs[:count1], refs[count1:-2]
    mine, theirs = refs[-2:]
    sums = []
    for parts in (parts0, parts1):
        total = parts[0][...].astype(F32)
        for ref in parts[1:]:
            total = total + ref[...].astype(F32)
        sums.append(total)
    first, second = sums
    if part == 1:
        row = lax.broadcasted_iota(jnp.int32, (ROWS_B, 1), 0) + place_ref[0] * ROWS_B
        extra = jnp.where(row >= 3 * WIDE + 8, first[:ROWS_B], 0.0)
        second = jnp.concatenate([second + extra, first[ROWS_B + SLAB :]], axis=0)
        first = first[: ROWS_B + SLAB]
    leading = flag[0] == 0
    mine[...] = jnp.where(leading, first, second).astype(BF)
    theirs[...] = jnp.where(leading, second, first).astype(BF)


def finish_call(part, flag, place, parts1, parts0):
    rows = ROWS_A if part == 0 else ROWS_B + SLAB
    one = jax.ShapeDtypeStruct((rows, D), BF)
    return pl.pallas_call(
        functools.partial(finish_kernel, part, len(parts1)), out_shape=[one, one],
        in_specs=[SM, SM] + [VM] * (len(parts1) + len(parts0)), out_specs=[VM] * 2,
        compiler_params=pltpu.CompilerParams(vmem_limit_bytes=VMEM_LIMIT),
        cost_estimate=pl.CostEstimate(flops=GFLOP, bytes_accessed=2 << 20, transcendentals=0), name="finish_chunks",
    )(flag, place, *parts1, *parts0)


def unpack_kernel(flag, place_ref, a_all, b_own, b_came, shrink, expand, output, query, key, value, vecs, embed, position, grid, slab):
    each = ROWS_A // 3
    half = CHUNKS // 2
    for i in range(CHUNKS):
        rows = slice(i * each, (i + 1) * each)
        block = a_all[i].astype(F32)
        shrink[rows, :] = block[0:each]
        expand[rows, :] = block[each : 2 * each]
        output[rows, :] = block[2 * each :]
    for core in range(2):
        b_ref = b_own if core == 0 else b_came
        for i in range(half):
            device = place_ref[0] ^ (4 * (i % 4) + 2 * (i // 4) + core)
            block = b_ref[i].astype(F32)
            grid[pl.ds(pl.multiple_of(device * ROWS_B, ROWS_B), ROWS_B), :] = block[:ROWS_B]
            slab[pl.ds(pl.multiple_of(device * SLAB, SLAB), SLAB), :] = block[ROWS_B:]
    for which, target in enumerate((query, key, value)):
        for g in range(GROUPS):
            target[g] = grid[which * WIDE : (which + 1) * WIDE, g * WIDE : (g + 1) * WIDE]
    vecs[...] = grid[3 * WIDE : 3 * WIDE + 8, :]
    rows = grid[3 * WIDE + 8 : 3 * WIDE + 16, :]
    embed[...] = jnp.where(flag[0] == 0, rows[0:1], rows[1:2])
    for part in range(2):
        position[part * (N // 2) : (part + 1) * (N // 2), :] = slab[:, part * (D // 2) : (part + 1) * (D // 2)]


def unpack_call(flag, place, a_all, b_own, b_came):
    square = jax.ShapeDtypeStruct((D, D), F32)
    group = jax.ShapeDtypeStruct((GROUPS, WIDE, WIDE), F32)
    return pl.pallas_call(
        unpack_kernel,
        out_shape=[square] * 3 + [group] * 3
        + [jax.ShapeDtypeStruct((8, D), F32), jax.ShapeDtypeStruct((1, D), F32), jax.ShapeDtypeStruct((N, D // 2), F32)],
        in_specs=[SM, SM] + [VM] * 3,
        out_specs=[VM] * 9,
        scratch_shapes=[pltpu.VMEM((QKV_ROWS, D), F32), pltpu.VMEM((CHUNKS * SLAB, D), F32)],
        compiler_params=pltpu.CompilerParams(vmem_limit_bytes=VMEM_LIMIT),
        cost_estimate=pl.CostEstimate(flops=GFLOP, bytes_accessed=16 << 20, transcendentals=0), name="unpack_sums",
    )(flag, place, a_all, b_own, b_came)


def plan_kernel(room, id_row, id_col, owner_row, owner_col, slot_col, slot_row, want_ref, most_ref):
    slots = want_ref.shape[1]
    across = lax.broadcasted_iota(jnp.int32, (N, N), 1)
    down = lax.broadcasted_iota(jnp.int32, (N, N), 0)
    same = id_col[...] == id_row[...]
    first_col = jnp.min(jnp.where(same, across, N).astype(F32), axis=1, keepdims=True).astype(jnp.int32)
    first_row = jnp.min(jnp.where(same, down, N).astype(F32), axis=0, keepdims=True).astype(jnp.int32)
    fresh_row = first_row == lax.broadcasted_iota(jnp.int32, (1, N), 1)
    fresh_col = first_col == lax.broadcasted_iota(jnp.int32, (N, 1), 0)
    mates = owner_col[...] == owner_row[...]
    rank_col = jnp.sum(jnp.where(mates & fresh_row & (across < first_col), 1.0, 0.0), axis=1, keepdims=True).astype(jnp.int32)
    rank_row = jnp.sum(jnp.where(mates & fresh_col & (down < first_row), 1.0, 0.0), axis=0, keepdims=True).astype(jnp.int32)
    col = jnp.where(rank_col < room, owner_col[...] * room + rank_col, -1)
    slot_col[...] = col
    slot_row[...] = jnp.where(rank_row < room, owner_row[...] * room + rank_row, -1)
    chosen = (col == lax.broadcasted_iota(jnp.int32, (N, slots), 1)) & fresh_col
    want = jnp.sum(jnp.where(chosen, (id_col[...] + 1).astype(F32), 0.0), axis=0, keepdims=True)
    want_ref[...] = want.astype(jnp.int32) - 1
    most = jnp.max(rank_row.astype(F32), axis=1, keepdims=True).astype(jnp.int32) + 1
    most_ref[...] = jnp.broadcast_to(most, most_ref.shape)


def plan_call(ids, owners, room, slots):
    return pl.pallas_call(
        functools.partial(plan_kernel, room),
        out_shape=[
            jax.ShapeDtypeStruct((N, 1), jnp.int32), jax.ShapeDtypeStruct((1, N), jnp.int32),
            jax.ShapeDtypeStruct((1, slots), jnp.int32), jax.ShapeDtypeStruct((8, LANE), jnp.int32),
        ],
        in_specs=[VM] * 4,
        out_specs=[VM] * 4,
        compiler_params=pltpu.CompilerParams(vmem_limit_bytes=VMEM_LIMIT),
        name="plan_slots",
    )(ids[None], ids[:, None], owners[None], owners[:, None])


def serve_kernel(base_ref, ids_ref, table_ref, out_ref):
    counter = lax.broadcasted_iota(jnp.int32, (ids_ref.shape[0], table_ref.shape[0]), 1) + base_ref[0]
    out_ref[...] = mm((ids_ref[...] == counter).astype(BF), table_ref[...]).astype(BF)


def serve_call(base, ids_col, table):
    return pl.pallas_call(
        serve_kernel,
        out_shape=jax.ShapeDtypeStruct((ids_col.shape[0], D), BF),
        in_specs=[SM, VM, VM],
        out_specs=VM,
        compiler_params=pltpu.CompilerParams(vmem_limit_bytes=VMEM_LIMIT),
        cost_estimate=pl.CostEstimate(flops=3 * GFLOP, bytes_accessed=20 << 20, transcendentals=0),
        name="serve_rows",
    )(base, ids_col, table)


def back_pass_kernel(grad_ref, table_ref, back_ref):
    @pl.when(pl.program_id(0) == 0)
    def _():
        back_ref[...] = jnp.zeros_like(back_ref)

    back_ref[...] += mm(grad_ref[...], table_ref[...])


def back_pass(flat_grad, table):
    vocab, masks = table.shape[0], flat_grad.shape[0]
    tile = 1536
    return pl.pallas_call(
        back_pass_kernel,
        grid=(vocab // tile,),
        out_shape=jax.ShapeDtypeStruct((masks, D), F32),
        in_specs=[pl.BlockSpec((masks, tile), lambda i: (0, i)), pl.BlockSpec((tile, D), lambda i: (i, 0))],
        out_specs=pl.BlockSpec((masks, D), lambda i: (0, 0)),
        compiler_params=pltpu.CompilerParams(vmem_limit_bytes=VMEM_LIMIT),
        cost_estimate=pl.CostEstimate(flops=10 * GFLOP, bytes_accessed=20 << 20, transcendentals=0),
        name="table_back_pass",
    )(flat_grad, table)


def logit_pass_kernel(head_ref, table_ref, logit_ref):
    logit_ref[...] = mm_nt(head_ref[...], table_ref[...]).astype(BF)


def logit_pass(head_rows, table):
    vocab, masks = table.shape[0], head_rows.shape[0]
    tile = 1536
    return pl.pallas_call(
        logit_pass_kernel,
        grid=(vocab // tile,),
        out_shape=jax.ShapeDtypeStruct((masks, vocab), BF),
        in_specs=[pl.BlockSpec((masks, D), lambda i: (0, 0)), pl.BlockSpec((tile, D), lambda i: (i, 0))],
        out_specs=pl.BlockSpec((masks, tile), lambda i: (0, i)),
        compiler_params=pltpu.CompilerParams(vmem_limit_bytes=VMEM_LIMIT),
        cost_estimate=pl.CostEstimate(flops=10 * GFLOP, bytes_accessed=20 << 20, transcendentals=0),
        name="table_logit_pass",
    )(head_rows, table)


def owner_kernel(place_ref, base_ref, ids_ref, rows_ref, grads_ref, heads_own, heads_came, crowd_ref, out_ref, ordered):
    masks = heads_own.shape[1]
    for core in range(2):
        heads = heads_own if core == 0 else heads_came
        for i in range(heads.shape[0]):
            device = place_ref[0] ^ (4 * (i % 4) + 2 * (i // 4) + core)
            ordered[pl.ds(pl.multiple_of(device * masks, masks), masks), :] = heads[i]
    counter = lax.broadcasted_iota(jnp.int32, (out_ref.shape[0], ids_ref.shape[1]), 0) + base_ref[0]
    total = crowd_ref[...] + mm((counter == ids_ref[...]).astype(BF), rows_ref[...])
    out_ref[...] = (total + mm_tn(grads_ref[...], ordered[...])).astype(BF)


def owner_call(place, base, ids_row, rows, grads, heads, crowd):
    masks = heads[0].shape[1]
    return pl.pallas_call(
        owner_kernel,
        out_shape=jax.ShapeDtypeStruct(crowd.shape, BF),
        in_specs=[SM, SM] + [VM] * 6,
        out_specs=VM,
        scratch_shapes=[pltpu.VMEM((2 * heads[0].shape[0] * masks, D), BF)],
        compiler_params=pltpu.CompilerParams(vmem_limit_bytes=VMEM_LIMIT),
        cost_estimate=pl.CostEstimate(flops=6 * GFLOP, bytes_accessed=20 << 20, transcendentals=0),
        name="owner_sum",
    )(place, base, ids_row, rows, grads, heads[0], heads[1], crowd)


def dense_kernel(base_ref, ids_ref, rows_ref, out_ref):
    @pl.when(pl.program_id(0) == 0)
    def _():
        out_ref[...] = jnp.zeros_like(out_ref)

    counter = lax.broadcasted_iota(jnp.int32, (out_ref.shape[0], N), 0) + base_ref[0]
    out_ref[...] += mm((counter == ids_ref[0]).astype(BF), rows_ref[0])


def dense_call(base, ids, rows, entries):
    return pl.pallas_call(
        dense_kernel,
        grid=(ids.shape[0],),
        out_shape=jax.ShapeDtypeStruct((entries, D), F32),
        in_specs=[SM, pl.BlockSpec((1, 1, N), lambda i: (i, 0, 0)), pl.BlockSpec((1, N, D), lambda i: (i, 0, 0))],
        out_specs=pl.BlockSpec((entries, D), lambda i: (0, 0)),
        compiler_params=pltpu.CompilerParams(vmem_limit_bytes=VMEM_LIMIT),
        name="dense_sum",
    )(base, ids, rows)


def partner(values, axis, bit):
    size = lax.axis_size(axis)
    return lax.ppermute(values, axis, [(i, i ^ bit) for i in range(size)])


def bits_of(axis):
    return [1 << b for b in range(lax.axis_size(axis).bit_length() - 1)]


def packed(weight):
    return jnp.swapaxes(weight, 0, 1).reshape(WIDE, D)


def per_device(
    token_ids,
    segment_ids,
    masked_pos,
    word_table,
    position_table,
    embed_gain,
    embed_bias,
    query_weight,
    key_weight,
    value_weight,
    output_weight,
    attention_gain,
    attention_bias,
    expand_weight,
    shrink_weight,
    feed_gain,
    feed_bias,
    logit_grad,
):
    section = lax.axis_index("section")
    place = lax.axis_index("dp")
    devices = lax.axis_size("dp")
    leading = section == 0
    shard_rows = word_table.shape[0]
    vocab = shard_rows * devices
    masks = masked_pos.shape[1]
    half = masks // 2
    room = max(16, 768 // devices)
    slots = room * devices
    base = (place * shard_rows).astype(jnp.int32).reshape(1)

    def swap(values):
        return lax.ppermute(values, "section", [(0, 1), (1, 0)])

    core = place % 2

    def after(values, *others):
        return lax.optimization_barrier((values, *others))[0]

    def exchange(values):
        return lax.all_to_all(values, "dp", 0, 0, tiled=True)

    ids = jnp.where(leading, token_ids[0], token_ids[1])
    table = lax.all_gather(word_table, "dp", axis=0, tiled=True)
    flat_grad = logit_grad.reshape(masks, vocab)

    def gather_by_exchange(array):
        if devices > 16:
            return lax.all_gather(array, "dp")
        return exchange(jnp.broadcast_to(array[None], (devices,) + array.shape))

    slot_col, slot_row, want, most = plan_call(ids, ids // shard_rows, room, slots)
    told = jnp.concatenate([want.reshape(devices, room), jnp.broadcast_to(most[:1, :16], (devices, 16))], axis=1)
    heard = exchange(told)
    asked = heard[:, :room].reshape(1, slots)
    served = serve_call(base, asked.reshape(slots, 1), word_table)
    slot_rows = exchange(served.reshape(devices, room, D)).reshape(slots, D)
    grad_parts = jnp.swapaxes(flat_grad.reshape(masks, devices, shard_rows), 0, 1)
    slot_rows, grad_parts = lax.optimization_barrier((slot_rows, grad_parts))

    most = after(jnp.max(heard[:, room:]).reshape(1, 1), served)
    most = jnp.maximum(most, swap(most))[0, 0]
    crowded = most > room
    flag = jnp.stack([section.astype(jnp.int32), crowded.astype(jnp.int32), core.astype(jnp.int32)])
    dense_rows = lax.cond(
        crowded,
        lambda: gather_by_exchange(word_table).reshape(vocab, D)[ids],
        lambda: jnp.zeros((N, D), BF),
    )

    vectors = jnp.concatenate([attention_gain, attention_bias, feed_gain, feed_bias, jnp.zeros((4, D), F32)], axis=0)
    own = (
        jnp.swapaxes(shrink_weight[0], 1, 2).reshape(D, D),
        expand_weight[0].reshape(D, D),
        output_weight[0],
        jnp.concatenate([packed(query_weight[0]), packed(key_weight[0]), packed(value_weight[0])], axis=0),
        vectors,
    )
    halves = []
    for array in own[:4]:
        rows = array.shape[0] // 2
        halves.append(swap(lax.dynamic_slice_in_dim(array, core * rows, rows, 0)))
    rest = [partner(array, "dp", 1) for array in halves]
    other = tuple(halves) + tuple(rest) + (swap(own[4]),)

    seg_row = jnp.where(leading, segment_ids[0], segment_ids[1])[None]
    mask_row = jnp.where(leading, masked_pos[0], masked_pos[1])[None]
    earlier = jnp.sum((seg_row < seg_row.T).astype(jnp.int32), axis=1)
    places = lax.iota(jnp.int32, N) - earlier
    embed_vec = jnp.stack([embed_gain, embed_bias])

    def chunked(arrays):
        return jnp.concatenate([array.reshape(devices, -1, D) for array in arrays], axis=1)

    def split_halves(values):
        mine = jnp.where(leading, values[:half], values[half:])
        theirs = jnp.where(leading, values[half:], values[:half])
        return mine, theirs

    def join_halves(mine, theirs):
        return jnp.where(leading, jnp.concatenate([mine, theirs]), jnp.concatenate([theirs, mine]))

    picked, saved0, saved1, hat_e, stat_e = forward_call(
        flag, slot_rows, dense_rows, slot_col, places[:, None], seg_row.T, seg_row, mask_row.T, position_table, embed_vec, own, other
    )
    mine, theirs = split_halves(picked)
    head_rows = join_halves(mine, swap(theirs))
    small = devices <= 16
    heads = [partner(head_rows, "dp", 4 * step) for step in (1, 2, 3)] if small else [lax.all_gather(head_rows, "dp", axis=0)]
    rows_back = back_pass(flat_grad, table)
    rows_back, heads = lax.optimization_barrier((rows_back, heads))
    if small:
        heads = jnp.stack([head_rows] + heads)
        heads = [heads, partner(heads, "dp", 2)]
    grad_parts = after(grad_parts, rows_back)
    grad_rows = exchange(grad_parts).reshape(devices * masks, shard_rows)
    mine, theirs = split_halves(rows_back)
    picked_back = join_halves(mine, swap(theirs)).astype(BF)

    def spread_on(array):
        if devices <= 16:
            return array
        groups = [list(range(low, devices, 16)) for low in range(16)]
        return lax.psum(array.astype(F32), "dp", axis_index_groups=groups).astype(BF)

    low_place = (place % 16).astype(jnp.int32).reshape(1)
    side_y = ((place // 2) % 2).astype(jnp.int32).reshape(1)
    me_z = ((place // 4) % 4).astype(jnp.int32).reshape(1)

    def across_z(parts):
        return [spread_on(parts[0])] + [partner(spread_on(parts[step]), "dp", 4 * step) for step in (1, 2, 3)]

    keep_a1, away_a1, attn1, low1, vec1 = backward_a_call(False, flag, [picked_back, mask_row], own, other, saved1)
    came = partner(away_a1, "dp", 1)
    keep_b1, away_b1, middle = backward_b_call(False, flag, [attn1, low1, vec1], own, other, saved1)
    middle, came, away_b1 = lax.optimization_barrier((middle, came, away_b1))
    keep_a1, away_a1 = step_y(side_y, keep_a1, came)
    middle, away_a1 = lax.optimization_barrier((middle, away_a1))
    came_a1 = partner(away_a1, "dp", 2)
    came_b1 = partner(away_b1, "dp", 1)
    packed_a0, attn0, low0, vec0 = backward_a_call(True, flag, [middle], own, other, saved0)
    attn0, heads, packed_a0, grad_rows = lax.optimization_barrier((attn0, heads, packed_a0, grad_rows))
    if small:
        heads = jnp.concatenate(heads)
        heads = [heads, partner(heads, "dp", 1)]
    sixteens = [list(range(low, low + 16)) for low in range(0, devices, 16)]
    part_a0 = spread_on(lax.psum_scatter(packed_a0, "dp", scatter_dimension=0, axis_index_groups=sixteens, tiled=True)[0])
    keep_b0, away_b0, back, slot_grad = backward_b_call(
        True, flag, [attn0, low0, vec0, slot_row, places[None], hat_e, stat_e, embed_vec], own, other, saved0, slots
    )
    slot_grad, away_b0, keep_a1, came_a1, head_rows, heads = lax.optimization_barrier(
        (slot_grad, away_b0, keep_a1, came_a1, head_rows, heads)
    )
    came_b0 = partner(away_b0, "dp", 1)
    local_a1 = step_z(me_z, keep_a1, came_a1)
    parts_a1 = across_z(local_a1)
    keep_b0, away_b0 = step_y(side_y, keep_b0, came_b0)
    came_b0 = partner(away_b0, "dp", 2)
    keep_b1, away_b1 = step_y(side_y, keep_b1, came_b1)
    came_b1 = partner(away_b1, "dp", 2)
    logits = logit_pass(head_rows, table)
    came_b0, came_b1, logits = lax.optimization_barrier((came_b0, came_b1, logits))
    logits = logits.reshape(2, half, vocab)
    parts_b0 = across_z(step_z(me_z, keep_b0, came_b0))
    parts_b1 = across_z(step_z(me_z, keep_b1, came_b1))

    sent = exchange(slot_grad.reshape(devices, room, D)).reshape(slots, D)
    crowd_sum = lax.cond(
        crowded,
        lambda: dense_call(base, gather_by_exchange(ids[None]), gather_by_exchange(back), shard_rows),
        lambda: jnp.zeros((shard_rows, D), F32),
    )
    names = jnp.where(crowded, -1, asked)
    if small:
        partial = owner_call(low_place, base, names, sent, grad_rows, heads, crowd_sum)
    else:
        one_hot = (names.reshape(1, slots) == (lax.iota(jnp.int32, shard_rows) + base)[:, None]).astype(BF)
        partial = jnp.dot(one_hot, sent, preferred_element_type=F32) + crowd_sum
        every_head = heads[0].reshape(devices * masks, D)
        partial += lax.dot_general(grad_rows, every_head, (((0,), (0,)), ((), ())), preferred_element_type=F32)
        partial = partial.astype(BF)
    def to_all(chunk):
        held = jnp.stack([chunk] + [partner(chunk, "dp", 4 * step) for step in (1, 2, 3)])
        held = jnp.concatenate([held, partner(held, "dp", 2)])
        return held, partner(held, "dp", 1)

    mine_b, theirs_b = finish_call(1, flag, low_place, parts_b1, parts_b0)
    theirs_b = swap(theirs_b)
    chunk_b = (mine_b.astype(F32) + theirs_b.astype(F32)).astype(BF)
    part_a0 = after(part_a0, chunk_b, partial)
    mine_a, theirs_a = finish_call(0, flag, low_place, parts_a1, [part_a0])
    theirs_a = swap(theirs_a)
    chunk_a = (mine_a.astype(F32) + theirs_a.astype(F32)).astype(BF)
    all_a = lax.all_gather(chunk_a, "dp", axis=0, axis_index_groups=sixteens)
    table_total = partial.astype(F32) + swap(partial).astype(F32)
    shrink_total, expand_total, output_total, query_total, key_total, value_total, vec_total, embed_total, position_total = unpack_call(
        flag, low_place, all_a, *to_all(chunk_b)
    )
    embed_total = embed_total.reshape(2, D // 2)
    return (
        logits,
        table_total,
        position_total,
        embed_total[0],
        embed_total[1],
        query_total[None],
        key_total[None],
        value_total[None],
        output_total[None],
        vec_total[0:1],
        vec_total[1:2],
        expand_total.reshape(1, GROUPS, WIDE, D),
        jnp.swapaxes(shrink_total.reshape(1, GROUPS, WIDE, D), 2, 3),
        vec_total[2:3],
        vec_total[3:4],
    )


def solution(mesh):
    placed = (
        P("dp", None),
        P("dp", None),
        P("dp", None),
        P("dp", None),
        P(),
        P(),
        P(),
        P("section", None, None, None),
        P("section", None, None, None),
        P("section", None, None, None),
        P("section", None, None),
        P("section", None),
        P("section", None),
        P("section", None, None, None),
        P("section", None, None, None),
        P("section", None),
        P("section", None),
        P("dp", "section", None),
    )
    return jax.shard_map(
        per_device,
        mesh=mesh,
        in_specs=placed,
        out_specs=(
            P("dp", "section", None),
            P("dp", None),
            P(None, "section"),
            P("section"),
            P("section"),
            P("section", None, None, None),
            P("section", None, None, None),
            P("section", None, None, None),
            P("section", None, None),
            P("section", None),
            P("section", None),
            P("section", None, None, None),
            P("section", None, None, None),
            P("section", None),
            P("section", None),
        ),
        check_vma=False,
    )
```

```python
import functools
import jax
import jax.numpy as jnp
from jax import lax
from jax.sharding import PartitionSpec as P
from jax.experimental import pallas as pl
from jax.experimental.pallas import tpu as pltpu

HEAD = 64
norm_eps = 1e-06
BF = jnp.bfloat16
F32 = jnp.float32
LANE = 128
N = 512
D = 768
FF = 3072
GROUPS = 4
WIDE = 192
HEADS = 12
PAIRS = 6
VMEM_LIMIT = 60 * 1024 * 1024
QKV_ROWS = 768
CHUNKS = 16
ROWS_A = 144
ROWS_B = 48
SLAB = 16
GFLOP = 10 ** 9


def mm(a, b):
    return lax.dot_general(a, b, (((1,), (0,)), ((), ())), preferred_element_type=F32)


def mm_nt(a, b):
    return lax.dot_general(a, b, (((1,), (1,)), ((), ())), preferred_element_type=F32)


def mm_tn(a, b):
    return lax.dot_general(a, b, (((0,), (0,)), ((), ())), preferred_element_type=F32)


def window(group):
    return 384 * (group // 2) + 128 * (group % 2)


def lanes(group):
    return slice(window(group), window(group) + 256)


def own_lanes(group):
    counter = lax.broadcasted_iota(jnp.int32, (1, 256), 1)
    return counter < WIDE if group % 2 == 0 else counter >= 64


def fetch_weights(refs, own, other, use_own, core, sems):
    shrink, expand, output, qkv, vecs = refs
    mine, rest = other[0:4], other[4:8]

    def copies(sources, halves):
        made = []
        for number in range(2):
            half = halves[number]
            shrink_src, expand_src, output_src, qkv_src = sources[number]
            for j in range(2 if shrink is not None else 0):
                made.append(pltpu.make_async_copy(shrink_src.at[pl.ds(j * WIDE, WIDE)], shrink.at[2 * half + j, pl.ds(64 * j, WIDE)], sems.at[6 * number + j]))
                made.append(pltpu.make_async_copy(expand_src.at[pl.ds(j * WIDE, WIDE)], expand.at[2 * half + j, pl.ds(64 * j, WIDE)], sems.at[6 * number + 2 + j]))
            if output is not None:
                made.append(pltpu.make_async_copy(output_src, output.at[pl.ds(pl.multiple_of(half * 384, 384), 384)], sems.at[6 * number + 4]))
            if qkv is not None:
                made.append(pltpu.make_async_copy(qkv_src, qkv.at[pl.ds(pl.multiple_of(half * 288, 288), 288)], sems.at[6 * number + 5]))
        return made

    halves_of = [[ref.at[pl.ds(h * (ref.shape[0] // 2), ref.shape[0] // 2)] for ref in own[0:4]] for h in range(2)]
    whole = copies(halves_of, (0, 1))
    parts = copies((mine, rest), (core, 1 - core))
    if vecs is not None:
        whole.append(pltpu.make_async_copy(own[4], vecs, sems.at[12]))
        parts.append(pltpu.make_async_copy(other[8], vecs, sems.at[12]))

    @pl.when(use_own)
    def _():
        for c in whole:
            c.start()

    @pl.when(jnp.logical_not(use_own))
    def _():
        for c in parts:
            c.start()

    for g in range(GROUPS if shrink is not None else 0):
        at = WIDE * (1 - g % 2)
        shrink[g, at : at + 64, :] = jnp.zeros((64, D), BF)
        expand[g, at : at + 64, :] = jnp.zeros((64, D), BF)
    return whole


def pad_qkv(qkv, padded):
    for which in range(3):
        for g in range(GROUPS):
            at = 64 * (g % 2)
            block = qkv[which * WIDE : (which + 1) * WIDE, lanes(g)]
            padded[which, g, at : at + WIDE, :] = jnp.where(own_lanes(g), block, jnp.zeros_like(block))
            gap = WIDE * (1 - g % 2)
            padded[which, g, gap : gap + 64, :] = jnp.zeros((64, 256), BF)


def norm_parts(values):
    centre = jnp.mean(values, axis=-1, keepdims=True)
    shifted = values - centre
    spread = jnp.mean(shifted * shifted, axis=-1, keepdims=True)
    rstd = lax.rsqrt(spread + norm_eps)
    return shifted * rstd, rstd


def norm_back(gradient, hat, rstd, gain):
    scaled = gradient * gain
    first = jnp.mean(scaled, axis=-1, keepdims=True)
    second = jnp.mean(scaled * hat, axis=-1, keepdims=True)
    return rstd * (scaled - first - hat * second)


def join_pair(low, high):
    return jnp.concatenate([low[:, :128], low[:, 128:] + high[:, :128], high[:, 128:]], axis=1)


def layer_fwd(x_ref, bias_ref, w, saves, stats_ref, grow_ref, save_done):
    shrink, expand, output, qkv_pad, vecs = w
    x_low, q_ref, k_ref, v_ref, e_ref, mix_ref, hat_a, hidden_low, active, slope, hat_f, inv_ref, full_ref = saves
    x_low[...] = x_ref[...].astype(BF)
    for which, target in enumerate((q_ref, k_ref, v_ref)):
        for p in range(2):
            low = mm(x_low[:, lanes(2 * p)], qkv_pad[which, 2 * p])
            high = mm(x_low[:, lanes(2 * p + 1)], qkv_pad[which, 2 * p + 1])
            joined = join_pair(low, high).astype(BF)
            if which == 0:
                joined = joined * jnp.asarray(HEAD ** (-0.5), BF)
            target[:, 384 * p : 384 * (p + 1)] = joined
    save_done(0)
    stats_ref[...] = jnp.zeros_like(stats_ref)
    lane = lax.broadcasted_iota(jnp.int32, (1, LANE), 1)

    def pair_body(p, carry):
        at = pl.ds(pl.multiple_of(p * LANE, LANE), LANE)
        qs, ks, vs = q_ref[:, at], k_ref[:, at], v_ref[:, at]
        outs = []
        for side in range(2):
            mine = (lane < HEAD) if side == 0 else (lane >= HEAD)
            scores = mm_nt(jnp.where(mine, qs, jnp.zeros_like(qs)), ks) + bias_ref[...]
            top = jnp.max(scores, axis=-1, keepdims=True)
            e = jnp.exp(scores - top).astype(BF)
            e_ref[2 * p + side] = e
            outs.append(mm(e, jnp.where(mine, vs, jnp.ones_like(vs))))
        inv = 1.0 / pltpu.roll(jnp.where(lane < HEAD, outs[1], outs[0]), HEAD, 1)
        full = jnp.where(lane < HEAD, outs[0], outs[1]) * inv
        inv_ref[:, at] = inv
        full_ref[:, at] = full
        mix_ref[:, at] = full.astype(BF)
        return carry

    lax.fori_loop(0, PAIRS, pair_body, 0)
    save_done(1)
    residual = x_ref[...] + mm(mix_ref[...], output[...])
    hat, rstd = norm_parts(residual)
    hat_a[...] = hat.astype(BF)
    stats_ref[...] = jnp.where(lane == 12, rstd, stats_ref[...])
    hidden = hat * vecs[0:1, :] + vecs[1:2, :]
    hidden_low[...] = hidden.astype(BF)
    grow_ref[...] = hidden
    for g in range(GROUPS):
        wide = slice(g * D, (g + 1) * D)
        expanded = mm(hidden_low[:, lanes(g)], expand[g])
        phi = 0.5 * (1.0 + lax.erf(expanded * (2.0 ** -0.5)))
        density = jnp.exp(expanded * expanded * -0.5) * (2.0 * jnp.pi) ** -0.5
        act = (expanded * phi).astype(BF)
        active[:, wide] = act
        slope[:, wide] = (phi + expanded * density).astype(BF)
        grow_ref[:, lanes(g)] += mm_nt(act, shrink[g])
    save_done(2)
    hat, rstd = norm_parts(grow_ref[...])
    hat_f[...] = hat.astype(BF)
    stats_ref[...] = jnp.where(lane == 13, rstd, stats_ref[...])
    x_ref[...] = hat * vecs[2:3, :] + vecs[3:4, :]
    save_done(3)


SAVE_SHAPES = (
    (N, D), (N, D), (N, D), (N, D), (HEADS, N, N), (N, D), (N, D), (N, D), (N, FF), (N, FF), (N, D),
    (N, D), (N, D), (N, LANE),
)
SAVE_TYPES = (BF,) * 11 + (F32,) * 3
SAVE_STAGES = ((0, 1, 2, 3), (4, 5, 11, 12), (6, 7, 8, 9), (10, 13))
SAVES = 14


def weight_scratch():
    return [
        pltpu.VMEM((GROUPS, 256, D), BF),
        pltpu.VMEM((GROUPS, 256, D), BF),
        pltpu.VMEM((D, D), BF),
        pltpu.VMEM((3 * WIDE, D), BF),
        pltpu.VMEM((8, D), F32),
    ]


def fwd_kernel(flag, slot_rows, dense_rows, slot_col, place_col, seg_col, seg_row, mask_col, place_table, embed_vec, *rest):
    rest = list(rest)

    def take(n):
        got = rest[:n]
        del rest[:n]
        return got

    own, other = take(5), take(9)
    (picked_ref,) = take(1)
    outs = [take(SAVES), take(SAVES)]
    hat_e_ref, stat_e_ref = take(2)
    weights = [take(5), take(5)]
    qkv_pad, bias_ref, x_ref, grow_ref = take(4)
    saves = take(SAVES)
    sem_w, sem_s, sem_d = take(3)
    leading = flag[0] == 0
    waits = [
        fetch_weights(weights[0], own, other, leading, flag[2], sem_w.at[0]),
        fetch_weights(weights[1], own, other, jnp.logical_not(leading), flag[2], sem_w.at[1]),
    ]
    counter = lax.broadcasted_iota(jnp.int32, (N, N), 1)
    one_hot = (place_col[...] == counter).astype(BF)
    slots = slot_rows.shape[0]
    wanted = (slot_col[...] == lax.broadcasted_iota(jnp.int32, (N, slots), 1)).astype(BF)
    x_ref[...] = mm(wanted, slot_rows[...])

    @pl.when(flag[1] != 0)
    def _():
        c = pltpu.make_async_copy(dense_rows, saves[0], sem_d)
        c.start()
        c.wait()
        x_ref[...] = saves[0][...].astype(F32)

    summed = x_ref[...] + mm(one_hot, place_table[...])
    hat, rstd = norm_parts(summed)
    hat_e_ref[...] = hat.astype(BF)
    stat_e_ref[...] = jnp.broadcast_to(rstd, (N, LANE))
    x_ref[...] = hat * embed_vec[0:1, :] + embed_vec[1:2, :]
    bias_ref[...] = jnp.where(seg_col[...] == seg_row[...], 0.0, -1000000000.0)
    drains = []
    for number in range(2):
        for c in waits[number] + drains:
            c.wait()
        drains = []
        shrink, expand, output, qkv, vecs = weights[number]
        pad_qkv(qkv, qkv_pad)

        def save_done(stage, number=number, drains=drains):
            for i in SAVE_STAGES[stage]:
                c = pltpu.make_async_copy(saves[i], outs[number][i], sem_s.at[number, i])
                c.start()
                drains.append(c)

        layer_fwd(
            x_ref, bias_ref, (shrink, expand, output, qkv_pad, vecs),
            saves[:13], saves[13], grow_ref, save_done,
        )
        if number == 0:
            x_ref[...] = x_ref[...].astype(BF).astype(F32)
    picks = (mask_col[...] == lax.broadcasted_iota(jnp.int32, (mask_col.shape[0], N), 1)).astype(BF)
    picked_ref[...] = mm(picks, x_ref[...].astype(BF)).astype(BF)
    for c in drains:
        c.wait()


def save_structs():
    return [jax.ShapeDtypeStruct(s, t) for s, t in zip(SAVE_SHAPES, SAVE_TYPES)]


def save_scratch():
    return [pltpu.VMEM(s, t) for s, t in zip(SAVE_SHAPES, SAVE_TYPES)]


VM = pl.BlockSpec(memory_space=pltpu.VMEM)
HB = pl.BlockSpec(memory_space=pl.ANY)
SM = pl.BlockSpec(memory_space=pltpu.SMEM)


def forward_call(flag, slot_rows, dense_rows, slot_col, place_col, seg_col, seg_row, mask_col, place_table, embed_vec, own, other):
    masks = mask_col.shape[0]
    out = pl.pallas_call(
        fwd_kernel,
        out_shape=[jax.ShapeDtypeStruct((masks, D), BF)] + save_structs() * 2
        + [jax.ShapeDtypeStruct((N, D), BF), jax.ShapeDtypeStruct((N, LANE), F32)],
        in_specs=[SM, VM, HB] + [VM] * 7 + [HB] * 14,
        out_specs=[VM] + [HB] * (2 * SAVES) + [VM] * 2,
        scratch_shapes=weight_scratch() * 2
        + [pltpu.VMEM((3, GROUPS, 256, 256), BF), pltpu.VMEM((N, N), F32), pltpu.VMEM((N, D), F32), pltpu.VMEM((N, D), F32)]
        + save_scratch()
        + [pltpu.SemaphoreType.DMA((2, 13)), pltpu.SemaphoreType.DMA((2, SAVES)), pltpu.SemaphoreType.DMA],
        compiler_params=pltpu.CompilerParams(vmem_limit_bytes=VMEM_LIMIT),
        cost_estimate=pl.CostEstimate(flops=36 * GFLOP, bytes_accessed=60 << 20, transcendentals=0),
        name="forward_layers",
    )(flag, slot_rows, dense_rows, slot_col, place_col, seg_col, seg_row, mask_col, place_table, embed_vec, *own, *other)
    return out[0], out[1 : 1 + SAVES], out[1 + SAVES : 1 + 2 * SAVES], out[-2], out[-1]


def chunk_place(chunk, core, in_order):
    if in_order:
        return chunk
    return chunk // 2 + (CHUNKS // 2) * (core if chunk % 2 == 0 else 1 - core)


def put_chunks(packed_ref, core, in_order, source, rows, at):
    for chunk in range(CHUNKS):
        packed_ref[chunk_place(chunk, core, in_order), at : at + rows, :] = source[chunk * rows : (chunk + 1) * rows, :].astype(BF)


def ship_chunks(packed_ref, outs, sems):
    if len(outs) == 1:
        made = [pltpu.make_async_copy(packed_ref, outs[0], sems.at[0])]
    else:
        half = CHUNKS // 2
        made = [pltpu.make_async_copy(packed_ref.at[pl.ds(i * half, half)], outs[i], sems.at[i]) for i in range(2)]
    for c in made:
        c.start()
    return made


def bwd_a_kernel(last, flag, *rest):
    rest = list(rest)

    def take(n):
        got = rest[:n]
        del rest[:n]
        return got

    if last:
        (go_in,) = take(1)
    else:
        picked_back, mask_row = take(2)
    own, other = take(5), take(9)
    sources = take(7)
    packed_out = take(2 if last else 1)
    attn_ref, back_low, vec_ref = take(3)
    weights = take(4)
    mid_ref, low_ref, packed_ref = take(3)
    saves = take(7)
    sem_w, sem_s, sem_o, sem_g = take(4)
    mix_ref, hat_a, hidden_low, active, slope, hat_f, stats_ref = saves
    shrink, expand, output, vecs = weights
    leading, core = flag[0] == 0, flag[2]
    use_own = leading if last else jnp.logical_not(leading)
    copies = [pltpu.make_async_copy(sources[i], saves[i], sem_s.at[i]) for i in range(7)]
    wide_copies = []
    for g in range(GROUPS):
        at = pl.ds(g * D, D)
        wide_copies.append([pltpu.make_async_copy(sources[i].at[:, at], saves[i].at[:, at], sem_g.at[i - 3, g]) for i in (3, 4)])
    for i in (5, 6):
        copies[i].start()
    waits = fetch_weights((shrink, expand, output, None, vecs), own, other, use_own, core, sem_w)
    copies[2].start()
    for pair in wide_copies:
        for c in pair:
            c.start()
    for i in (1, 0):
        copies[i].start()
    vec_ref[...] = jnp.zeros_like(vec_ref)
    if last:
        go = go_in[...].astype(F32)
    else:
        masks = mask_row.shape[1]
        spread = (lax.broadcasted_iota(jnp.int32, (N, masks), 0) == mask_row[...]).astype(BF)
        go = mm(spread, picked_back[...])
    lane = lax.broadcasted_iota(jnp.int32, (1, LANE), 1)

    def stat(index):
        return jnp.sum(jnp.where(lane == index, stats_ref[...], 0.0), axis=-1, keepdims=True)

    copies[5].wait()
    copies[6].wait()
    for c in waits:
        c.wait()
    hat = hat_f[...].astype(F32)
    vec_ref[2:3, :] = jnp.sum(go * hat, axis=0, keepdims=True)
    vec_ref[3:4, :] = jnp.sum(go, axis=0, keepdims=True)
    feed_back = norm_back(go, hat, stat(13), vecs[2:3, :])
    mid_ref[...] = feed_back
    low_ref[...] = feed_back.astype(BF)
    copies[2].wait()
    each = WIDE // (CHUNKS // GROUPS)
    for g in range(GROUPS):
        wide = slice(g * D, (g + 1) * D)
        rows = slice(64 * (g % 2), 64 * (g % 2) + WIDE)
        for c in wide_copies[g]:
            c.wait()
        shrink_in = low_ref[:, lanes(g)]
        shrink_grad = mm_tn(shrink_in, active[:, wide])[rows].astype(BF)
        expand_in = (mm(shrink_in, shrink[g]) * slope[:, wide].astype(F32)).astype(BF)
        expand_grad = mm_tn(hidden_low[:, lanes(g)], expand_in)[rows].astype(BF)
        mid_ref[:, lanes(g)] += mm_nt(expand_in, expand[g])
        for part in range(CHUNKS // GROUPS):
            chunk = g * (CHUNKS // GROUPS) + part
            at = chunk_place(chunk, core, not last)
            packed_ref[at, 0:each, :] = shrink_grad[part * each : (part + 1) * each, :]
            packed_ref[at, each : 2 * each, :] = expand_grad[part * each : (part + 1) * each, :]
    copies[1].wait()
    hidden_back = mid_ref[...]
    hat = hat_a[...].astype(F32)
    vec_ref[0:1, :] = jnp.sum(hidden_back * hat, axis=0, keepdims=True)
    vec_ref[1:2, :] = jnp.sum(hidden_back, axis=0, keepdims=True)
    attn_back = norm_back(hidden_back, hat, stat(12), vecs[0:1, :])
    attn_ref[...] = attn_back
    attended_in = attn_back.astype(BF)
    copies[0].wait()
    put_chunks(packed_ref, core, not last, mm_tn(mix_ref[...], attended_in), each, 2 * each)
    ship = ship_chunks(packed_ref, packed_out, sem_o)
    back_low[...] = mm_nt(attended_in, output[...]).astype(BF)
    for c in ship:
        c.wait()


def backward_a_call(last, flag, extra, own, other, saved):
    chosen = (5, 6, 7, 8, 9, 10, 13)
    return pl.pallas_call(
        functools.partial(bwd_a_kernel, last),
        out_shape=([jax.ShapeDtypeStruct((CHUNKS // 2, ROWS_A, D), BF)] * 2 if last else [jax.ShapeDtypeStruct((CHUNKS, ROWS_A, D), BF)])
        + [
            jax.ShapeDtypeStruct((N, D), F32), jax.ShapeDtypeStruct((N, D), BF), jax.ShapeDtypeStruct((16, D), F32),
        ],
        in_specs=[SM] + [VM] * len(extra) + [HB] * (14 + len(chosen)),
        out_specs=[HB] * (2 if last else 1) + [VM, VM, VM],
        scratch_shapes=[
            pltpu.VMEM((GROUPS, 256, D), BF), pltpu.VMEM((GROUPS, 256, D), BF), pltpu.VMEM((D, D), BF), pltpu.VMEM((8, D), F32),
            pltpu.VMEM((N, D), F32), pltpu.VMEM((N, D), BF), pltpu.VMEM((CHUNKS, ROWS_A, D), BF),
        ]
        + [pltpu.VMEM(SAVE_SHAPES[i], SAVE_TYPES[i]) for i in chosen]
        + [pltpu.SemaphoreType.DMA((13,)), pltpu.SemaphoreType.DMA((len(chosen),)), pltpu.SemaphoreType.DMA((2,)), pltpu.SemaphoreType.DMA((2, GROUPS))],
        compiler_params=pltpu.CompilerParams(vmem_limit_bytes=VMEM_LIMIT),
        cost_estimate=pl.CostEstimate(flops=12 * GFLOP, bytes_accessed=20 << 20, transcendentals=0),
        name="backward_first_a" if last else "backward_second_a",
    )(flag, *extra, *own, *other, *[saved[i] for i in chosen])


def bwd_b_kernel(last, flag, attn_in, back_low, vec_in, *rest):
    rest = list(rest)

    def take(n):
        got = rest[:n]
        del rest[:n]
        return got

    if last:
        slot_row, place_row, hat_e_ref, stat_e_ref, embed_vec = take(5)
    own, other = take(5), take(9)
    sources = take(7)
    keep_out, away_out, back_ref = take(3)
    if last:
        (slot_grad,) = take(1)
    qkv, qkv_pad, go_ref, vec_ref, packed_ref = take(5)
    dq_ref, dk_ref, dv_ref, grad_ref = take(4)
    saves = take(7)
    sem_w, sem_s, sem_o = take(3)
    x_low, q_ref, k_ref, v_ref, e_ref, inv_ref, full_ref = saves
    leading, core = flag[0] == 0, flag[2]
    use_own = leading if last else jnp.logical_not(leading)
    whole = pltpu.make_async_copy(sources[0], saves[0], sem_s.at[0, 0])

    def pair_copies(p):
        at = pl.ds(p * LANE if isinstance(p, int) else pl.multiple_of(p * LANE, LANE), LANE)
        made = [pltpu.make_async_copy(sources[4].at[pl.ds(2 * p, 2)], saves[4].at[pl.ds(2 * p, 2)], sem_s.at[4, p])]
        for i in (1, 2, 3, 5, 6):
            made.append(pltpu.make_async_copy(sources[i].at[:, at], saves[i].at[:, at], sem_s.at[i, p]))
        return made

    for p in range(PAIRS):
        for c in pair_copies(p):
            c.start()
    waits = fetch_weights((None, None, None, qkv, None), own, other, use_own, core, sem_w)
    whole.start()
    lane = lax.broadcasted_iota(jnp.int32, (1, LANE), 1)

    def pair_body(p, carry):
        for c in pair_copies(p):
            c.wait()
        at = pl.ds(pl.multiple_of(p * LANE, LANE), LANE)
        first = lane < HEAD
        d_low = (back_low[:, at].astype(F32) * inv_ref[:, at]).astype(BF)
        weighted = d_low.astype(F32) * full_ref[:, at]
        qs, ks, vs = q_ref[:, at], k_ref[:, at], v_ref[:, at]
        d_v = d_q = d_k = None
        for side in range(2):
            mine = first if side == 0 else jnp.logical_not(first)
            delta = jnp.sum(jnp.where(mine, weighted, 0.0), axis=-1, keepdims=True)
            e = e_ref[2 * p + side]
            d_side = jnp.where(mine, d_low, jnp.zeros_like(d_low))
            prob_back = mm_nt(d_side, vs)
            d_s = (e.astype(F32) * (prob_back - delta)).astype(BF)
            part_v = mm_tn(e, d_side)
            part_q = mm(d_s, jnp.where(mine, ks, jnp.zeros_like(ks)))
            part_k = mm_tn(d_s, jnp.where(mine, qs, jnp.zeros_like(qs)))
            d_v = part_v if d_v is None else d_v + part_v
            d_q = part_q if d_q is None else d_q + part_q
            d_k = part_k if d_k is None else d_k + part_k
        dv_ref[:, at] = d_v.astype(BF)
        dq_ref[:, at] = (d_q * HEAD ** (-0.5)).astype(BF)
        dk_ref[:, at] = d_k.astype(BF)
        return carry

    lax.fori_loop(0, PAIRS, pair_body, 0)
    whole.wait()
    for c in waits:
        c.wait()
    pad_qkv(qkv, qkv_pad)
    go_ref[...] = attn_in[...]
    vec_ref[...] = jnp.zeros_like(vec_ref)
    vec_ref[0:8, :] = vec_in[0:8, :]
    for which, d_ref in enumerate((dq_ref, dk_ref, dv_ref)):
        for p in range(2):
            made = []
            for g in (2 * p, 2 * p + 1):
                rows = slice(64 * (g % 2), 64 * (g % 2) + WIDE)
                d_part = d_ref[:, lanes(g)]
                made.append(jnp.where(own_lanes(g), mm_tn(x_low[:, lanes(g)], d_part)[rows], 0.0))
                go_ref[:, lanes(g)] += mm_nt(d_part, qkv_pad[which, g])
            grad_ref[which * WIDE : (which + 1) * WIDE, 384 * p : 384 * (p + 1)] = join_pair(*made).astype(BF)
    go = go_ref[...]
    if last:
        hat = hat_e_ref[...].astype(F32)
        gain_row = jnp.sum(go * hat, axis=0, keepdims=True)
        bias_row = jnp.sum(go, axis=0, keepdims=True)
        for s in range(2):
            at = slice(s * (D // 2), (s + 1) * (D // 2))
            vec_ref[8 + s : 9 + s, :] = jnp.concatenate([gain_row[:, at], bias_row[:, at]], axis=1)
        back = norm_back(go, hat, stat_e_ref[:, 0:1], embed_vec[0:1, :]).astype(BF)
        back_ref[...] = back
        places = (lax.broadcasted_iota(jnp.int32, (N, N), 0) == place_row[...]).astype(BF)
        grad = mm(places, back).astype(BF)
        for s in range(2):
            block = jnp.concatenate([grad[part * (N // 2) : (part + 1) * (N // 2), s * 384 : (s + 1) * 384] for part in range(2)], axis=1)
            put_chunks(packed_ref, core, False, block, SLAB, ROWS_B + s * SLAB)
        slots = slot_grad.shape[0]
        slot_grad[...] = mm((lax.broadcasted_iota(jnp.int32, (slots, N), 0) == slot_row[...]).astype(BF), back).astype(BF)
    else:
        back_ref[...] = go.astype(BF)
    grad_ref[3 * WIDE :, :] = vec_ref[...].astype(BF)
    put_chunks(packed_ref, core, False, grad_ref, ROWS_B, 0)
    for c in ship_chunks(packed_ref, (keep_out, away_out), sem_o):
        c.wait()


def backward_b_call(last, flag, extra, own, other, saved, slots=0):
    chosen = (0, 1, 2, 3, 4, 11, 12)
    rows = ROWS_B + 2 * SLAB if last else ROWS_B
    out_shape = [
        jax.ShapeDtypeStruct((CHUNKS // 2, rows, D), BF), jax.ShapeDtypeStruct((CHUNKS // 2, rows, D), BF),
        jax.ShapeDtypeStruct((N, D), BF),
    ]
    if last:
        out_shape.append(jax.ShapeDtypeStruct((slots, D), BF))
    return pl.pallas_call(
        functools.partial(bwd_b_kernel, last),
        out_shape=out_shape,
        in_specs=[SM] + [VM] * len(extra) + [HB] * (14 + len(chosen)),
        out_specs=[HB, HB] + [VM] * (len(out_shape) - 2),
        scratch_shapes=[
            pltpu.VMEM((3 * WIDE, D), BF), pltpu.VMEM((3, GROUPS, 256, 256), BF), pltpu.VMEM((N, D), F32),
            pltpu.VMEM((QKV_ROWS - 3 * WIDE, D), F32), pltpu.VMEM((CHUNKS, rows, D), BF),
        ]
        + [pltpu.VMEM((N, D), BF)] * 3 + [pltpu.VMEM((QKV_ROWS, D), BF)]
        + [pltpu.VMEM(SAVE_SHAPES[i], SAVE_TYPES[i]) for i in chosen]
        + [pltpu.SemaphoreType.DMA((13,)), pltpu.SemaphoreType.DMA((len(chosen), PAIRS)), pltpu.SemaphoreType.DMA((2,))],
        compiler_params=pltpu.CompilerParams(vmem_limit_bytes=VMEM_LIMIT),
        cost_estimate=pl.CostEstimate(flops=15 * GFLOP, bytes_accessed=20 << 20, transcendentals=0),
        name="backward_first_b" if last else "backward_second_b",
    )(flag, *extra, *own, *other, *[saved[i] for i in chosen])


def step_y_kernel(side_ref, keep_ref, came_ref, next_keep, next_away):
    side = side_ref[0]
    for j in range(next_keep.shape[0]):
        for target, which in ((next_keep, side), (next_away, 1 - side)):
            at = 2 * j + which
            target[j] = (keep_ref[at].astype(F32) + came_ref[at].astype(F32)).astype(BF)


def step_y(side, keep, came):
    half = jax.ShapeDtypeStruct((keep.shape[0] // 2,) + keep.shape[1:], BF)
    return pl.pallas_call(
        step_y_kernel, out_shape=[half, half], in_specs=[SM, VM, VM], out_specs=[VM, VM],
        compiler_params=pltpu.CompilerParams(vmem_limit_bytes=VMEM_LIMIT),
        cost_estimate=pl.CostEstimate(flops=GFLOP, bytes_accessed=6 << 20, transcendentals=0), name="halve_chunks",
    )(side, keep, came)


def step_z_kernel(me_ref, keep_ref, came_ref, *outs):
    for step in range(4):
        at = me_ref[0] ^ step
        outs[step][...] = (keep_ref[at].astype(F32) + came_ref[at].astype(F32)).astype(BF)


def step_z(me, keep, came):
    one = jax.ShapeDtypeStruct(keep.shape[1:], BF)
    return pl.pallas_call(
        step_z_kernel, out_shape=[one] * 4, in_specs=[SM, VM, VM], out_specs=[VM] * 4,
        compiler_params=pltpu.CompilerParams(vmem_limit_bytes=VMEM_LIMIT),
        cost_estimate=pl.CostEstimate(flops=GFLOP, bytes_accessed=4 << 20, transcendentals=0), name="four_chunks",
    )(me, keep, came)


def finish_kernel(part, count1, flag, place_ref, *refs):
    parts1, parts0 = refs[:count1], refs[count1:-2]
    mine, theirs = refs[-2:]
    sums = []
    for parts in (parts0, parts1):
        total = parts[0][...].astype(F32)
        for ref in parts[1:]:
            total = total + ref[...].astype(F32)
        sums.append(total)
    first, second = sums
    if part == 1:
        row = lax.broadcasted_iota(jnp.int32, (ROWS_B, 1), 0) + place_ref[0] * ROWS_B
        extra = jnp.where(row >= 3 * WIDE + 8, first[:ROWS_B], 0.0)
        second = jnp.concatenate([second + extra, first[ROWS_B + SLAB :]], axis=0)
        first = first[: ROWS_B + SLAB]
    leading = flag[0] == 0
    mine[...] = jnp.where(leading, first, second).astype(BF)
    theirs[...] = jnp.where(leading, second, first).astype(BF)


def finish_call(part, flag, place, parts1, parts0):
    rows = ROWS_A if part == 0 else ROWS_B + SLAB
    one = jax.ShapeDtypeStruct((rows, D), BF)
    return pl.pallas_call(
        functools.partial(finish_kernel, part, len(parts1)), out_shape=[one, one],
        in_specs=[SM, SM] + [VM] * (len(parts1) + len(parts0)), out_specs=[VM] * 2,
        compiler_params=pltpu.CompilerParams(vmem_limit_bytes=VMEM_LIMIT),
        cost_estimate=pl.CostEstimate(flops=GFLOP, bytes_accessed=2 << 20, transcendentals=0), name="finish_chunks",
    )(flag, place, *parts1, *parts0)


def unpack_kernel(flag, place_ref, a_all, b_own, b_came, shrink, expand, output, query, key, value, vecs, embed, position, grid, slab):
    each = ROWS_A // 3
    half = CHUNKS // 2
    for i in range(CHUNKS):
        rows = slice(i * each, (i + 1) * each)
        block = a_all[i].astype(F32)
        shrink[rows, :] = block[0:each]
        expand[rows, :] = block[each : 2 * each]
        output[rows, :] = block[2 * each :]
    for core in range(2):
        b_ref = b_own if core == 0 else b_came
        for i in range(half):
            device = place_ref[0] ^ (4 * (i % 4) + 2 * (i // 4) + core)
            block = b_ref[i].astype(F32)
            grid[pl.ds(pl.multiple_of(device * ROWS_B, ROWS_B), ROWS_B), :] = block[:ROWS_B]
            slab[pl.ds(pl.multiple_of(device * SLAB, SLAB), SLAB), :] = block[ROWS_B:]
    for which, target in enumerate((query, key, value)):
        for g in range(GROUPS):
            target[g] = grid[which * WIDE : (which + 1) * WIDE, g * WIDE : (g + 1) * WIDE]
    vecs[...] = grid[3 * WIDE : 3 * WIDE + 8, :]
    rows = grid[3 * WIDE + 8 : 3 * WIDE + 16, :]
    embed[...] = jnp.where(flag[0] == 0, rows[0:1], rows[1:2])
    for part in range(2):
        position[part * (N // 2) : (part + 1) * (N // 2), :] = slab[:, part * (D // 2) : (part + 1) * (D // 2)]


def unpack_call(flag, place, a_all, b_own, b_came):
    square = jax.ShapeDtypeStruct((D, D), F32)
    group = jax.ShapeDtypeStruct((GROUPS, WIDE, WIDE), F32)
    return pl.pallas_call(
        unpack_kernel,
        out_shape=[square] * 3 + [group] * 3
        + [jax.ShapeDtypeStruct((8, D), F32), jax.ShapeDtypeStruct((1, D), F32), jax.ShapeDtypeStruct((N, D // 2), F32)],
        in_specs=[SM, SM] + [VM] * 3,
        out_specs=[VM] * 9,
        scratch_shapes=[pltpu.VMEM((QKV_ROWS, D), F32), pltpu.VMEM((CHUNKS * SLAB, D), F32)],
        compiler_params=pltpu.CompilerParams(vmem_limit_bytes=VMEM_LIMIT),
        cost_estimate=pl.CostEstimate(flops=GFLOP, bytes_accessed=16 << 20, transcendentals=0), name="unpack_sums",
    )(flag, place, a_all, b_own, b_came)


def plan_kernel(room, id_row, id_col, owner_row, owner_col, slot_col, slot_row, want_ref, most_ref):
    slots = want_ref.shape[1]
    across = lax.broadcasted_iota(jnp.int32, (N, N), 1)
    down = lax.broadcasted_iota(jnp.int32, (N, N), 0)
    same = id_col[...] == id_row[...]
    first_col = jnp.min(jnp.where(same, across, N).astype(F32), axis=1, keepdims=True).astype(jnp.int32)
    first_row = jnp.min(jnp.where(same, down, N).astype(F32), axis=0, keepdims=True).astype(jnp.int32)
    fresh_row = first_row == lax.broadcasted_iota(jnp.int32, (1, N), 1)
    fresh_col = first_col == lax.broadcasted_iota(jnp.int32, (N, 1), 0)
    mates = owner_col[...] == owner_row[...]
    rank_col = jnp.sum(jnp.where(mates & fresh_row & (across < first_col), 1.0, 0.0), axis=1, keepdims=True).astype(jnp.int32)
    rank_row = jnp.sum(jnp.where(mates & fresh_col & (down < first_row), 1.0, 0.0), axis=0, keepdims=True).astype(jnp.int32)
    col = jnp.where(rank_col < room, owner_col[...] * room + rank_col, -1)
    slot_col[...] = col
    slot_row[...] = jnp.where(rank_row < room, owner_row[...] * room + rank_row, -1)
    chosen = (col == lax.broadcasted_iota(jnp.int32, (N, slots), 1)) & fresh_col
    want = jnp.sum(jnp.where(chosen, (id_col[...] + 1).astype(F32), 0.0), axis=0, keepdims=True)
    want_ref[...] = want.astype(jnp.int32) - 1
    most = jnp.max(rank_row.astype(F32), axis=1, keepdims=True).astype(jnp.int32) + 1
    most_ref[...] = jnp.broadcast_to(most, most_ref.shape)


def plan_call(ids, owners, room, slots):
    return pl.pallas_call(
        functools.partial(plan_kernel, room),
        out_shape=[
            jax.ShapeDtypeStruct((N, 1), jnp.int32), jax.ShapeDtypeStruct((1, N), jnp.int32),
            jax.ShapeDtypeStruct((1, slots), jnp.int32), jax.ShapeDtypeStruct((8, LANE), jnp.int32),
        ],
        in_specs=[VM] * 4,
        out_specs=[VM] * 4,
        compiler_params=pltpu.CompilerParams(vmem_limit_bytes=VMEM_LIMIT),
        name="plan_slots",
    )(ids[None], ids[:, None], owners[None], owners[:, None])


def serve_kernel(base_ref, ids_ref, table_ref, out_ref):
    counter = lax.broadcasted_iota(jnp.int32, (ids_ref.shape[0], table_ref.shape[0]), 1) + base_ref[0]
    out_ref[...] = mm((ids_ref[...] == counter).astype(BF), table_ref[...]).astype(BF)


def serve_call(base, ids_col, table):
    return pl.pallas_call(
        serve_kernel,
        out_shape=jax.ShapeDtypeStruct((ids_col.shape[0], D), BF),
        in_specs=[SM, VM, VM],
        out_specs=VM,
        compiler_params=pltpu.CompilerParams(vmem_limit_bytes=VMEM_LIMIT),
        cost_estimate=pl.CostEstimate(flops=3 * GFLOP, bytes_accessed=20 << 20, transcendentals=0),
        name="serve_rows",
    )(base, ids_col, table)


def back_pass_kernel(grad_ref, table_ref, back_ref):
    @pl.when(pl.program_id(0) == 0)
    def _():
        back_ref[...] = jnp.zeros_like(back_ref)

    back_ref[...] += mm(grad_ref[...], table_ref[...])


def back_pass(flat_grad, table):
    vocab, masks = table.shape[0], flat_grad.shape[0]
    tile = 1536
    return pl.pallas_call(
        back_pass_kernel,
        grid=(vocab // tile,),
        out_shape=jax.ShapeDtypeStruct((masks, D), F32),
        in_specs=[pl.BlockSpec((masks, tile), lambda i: (0, i)), pl.BlockSpec((tile, D), lambda i: (i, 0))],
        out_specs=pl.BlockSpec((masks, D), lambda i: (0, 0)),
        compiler_params=pltpu.CompilerParams(vmem_limit_bytes=VMEM_LIMIT),
        cost_estimate=pl.CostEstimate(flops=10 * GFLOP, bytes_accessed=20 << 20, transcendentals=0),
        name="table_back_pass",
    )(flat_grad, table)


def logit_pass_kernel(head_ref, table_ref, logit_ref):
    logit_ref[...] = mm_nt(head_ref[...], table_ref[...]).astype(BF)


def logit_pass(head_rows, table):
    vocab, masks = table.shape[0], head_rows.shape[0]
    tile = 1536
    return pl.pallas_call(
        logit_pass_kernel,
        grid=(vocab // tile,),
        out_shape=jax.ShapeDtypeStruct((masks, vocab), BF),
        in_specs=[pl.BlockSpec((masks, D), lambda i: (0, 0)), pl.BlockSpec((tile, D), lambda i: (i, 0))],
        out_specs=pl.BlockSpec((masks, tile), lambda i: (0, i)),
        compiler_params=pltpu.CompilerParams(vmem_limit_bytes=VMEM_LIMIT),
        cost_estimate=pl.CostEstimate(flops=10 * GFLOP, bytes_accessed=20 << 20, transcendentals=0),
        name="table_logit_pass",
    )(head_rows, table)


def owner_kernel(place_ref, base_ref, ids_ref, rows_ref, grads_ref, heads_own, heads_came, crowd_ref, out_ref, ordered):
    masks = heads_own.shape[1]
    for core in range(2):
        heads = heads_own if core == 0 else heads_came
        for i in range(heads.shape[0]):
            device = place_ref[0] ^ (4 * (i % 4) + 2 * (i // 4) + core)
            ordered[pl.ds(pl.multiple_of(device * masks, masks), masks), :] = heads[i]
    counter = lax.broadcasted_iota(jnp.int32, (out_ref.shape[0], ids_ref.shape[1]), 0) + base_ref[0]
    total = crowd_ref[...] + mm((counter == ids_ref[...]).astype(BF), rows_ref[...])
    out_ref[...] = (total + mm_tn(grads_ref[...], ordered[...])).astype(BF)


def owner_call(place, base, ids_row, rows, grads, heads, crowd):
    masks = heads[0].shape[1]
    return pl.pallas_call(
        owner_kernel,
        out_shape=jax.ShapeDtypeStruct(crowd.shape, BF),
        in_specs=[SM, SM] + [VM] * 6,
        out_specs=VM,
        scratch_shapes=[pltpu.VMEM((2 * heads[0].shape[0] * masks, D), BF)],
        compiler_params=pltpu.CompilerParams(vmem_limit_bytes=VMEM_LIMIT),
        cost_estimate=pl.CostEstimate(flops=6 * GFLOP, bytes_accessed=20 << 20, transcendentals=0),
        name="owner_sum",
    )(place, base, ids_row, rows, grads, heads[0], heads[1], crowd)


def dense_kernel(base_ref, ids_ref, rows_ref, out_ref):
    @pl.when(pl.program_id(0) == 0)
    def _():
        out_ref[...] = jnp.zeros_like(out_ref)

    counter = lax.broadcasted_iota(jnp.int32, (out_ref.shape[0], N), 0) + base_ref[0]
    out_ref[...] += mm((counter == ids_ref[0]).astype(BF), rows_ref[0])


def dense_call(base, ids, rows, entries):
    return pl.pallas_call(
        dense_kernel,
        grid=(ids.shape[0],),
        out_shape=jax.ShapeDtypeStruct((entries, D), F32),
        in_specs=[SM, pl.BlockSpec((1, 1, N), lambda i: (i, 0, 0)), pl.BlockSpec((1, N, D), lambda i: (i, 0, 0))],
        out_specs=pl.BlockSpec((entries, D), lambda i: (0, 0)),
        compiler_params=pltpu.CompilerParams(vmem_limit_bytes=VMEM_LIMIT),
        name="dense_sum",
    )(base, ids, rows)


def partner(values, axis, bit):
    size = lax.axis_size(axis)
    return lax.ppermute(values, axis, [(i, i ^ bit) for i in range(size)])


def bits_of(axis):
    return [1 << b for b in range(lax.axis_size(axis).bit_length() - 1)]


def packed(weight):
    return jnp.swapaxes(weight, 0, 1).reshape(WIDE, D)


def per_device(
    token_ids,
    segment_ids,
    masked_pos,
    word_table,
    position_table,
    embed_gain,
    embed_bias,
    query_weight,
    key_weight,
    value_weight,
    output_weight,
    attention_gain,
    attention_bias,
    expand_weight,
    shrink_weight,
    feed_gain,
    feed_bias,
    logit_grad,
):
    section = lax.axis_index("section")
    place = lax.axis_index("dp")
    devices = lax.axis_size("dp")
    leading = section == 0
    shard_rows = word_table.shape[0]
    vocab = shard_rows * devices
    masks = masked_pos.shape[1]
    half = masks // 2
    room = max(16, 768 // devices)
    slots = room * devices
    base = (place * shard_rows).astype(jnp.int32).reshape(1)

    def swap(values):
        return lax.ppermute(values, "section", [(0, 1), (1, 0)])

    core = place % 2

    def after(values, *others):
        return lax.optimization_barrier((values, *others))[0]

    def exchange(values):
        return lax.all_to_all(values, "dp", 0, 0, tiled=True)

    ids = jnp.where(leading, token_ids[0], token_ids[1])
    table = lax.all_gather(word_table, "dp", axis=0, tiled=True)
    flat_grad = logit_grad.reshape(masks, vocab)

    def gather_by_exchange(array):
        if devices > 16:
            return lax.all_gather(array, "dp")
        return exchange(jnp.broadcast_to(array[None], (devices,) + array.shape))

    slot_col, slot_row, want, most = plan_call(ids, ids // shard_rows, room, slots)
    told = jnp.concatenate([want.reshape(devices, room), jnp.broadcast_to(most[:1, :16], (devices, 16))], axis=1)
    heard = exchange(told)
    asked = heard[:, :room].reshape(1, slots)
    served = serve_call(base, asked.reshape(slots, 1), word_table)
    slot_rows = exchange(served.reshape(devices, room, D)).reshape(slots, D)
    grad_parts = jnp.swapaxes(flat_grad.reshape(masks, devices, shard_rows), 0, 1)
    slot_rows, grad_parts = lax.optimization_barrier((slot_rows, grad_parts))

    most = after(jnp.max(heard[:, room:]).reshape(1, 1), served)
    most = jnp.maximum(most, swap(most))[0, 0]
    crowded = most > room
    flag = jnp.stack([section.astype(jnp.int32), crowded.astype(jnp.int32), core.astype(jnp.int32)])
    dense_rows = lax.cond(
        crowded,
        lambda: gather_by_exchange(word_table).reshape(vocab, D)[ids],
        lambda: jnp.zeros((N, D), BF),
    )

    vectors = jnp.concatenate([attention_gain, attention_bias, feed_gain, feed_bias, jnp.zeros((4, D), F32)], axis=0)
    own = (
        jnp.swapaxes(shrink_weight[0], 1, 2).reshape(D, D),
        expand_weight[0].reshape(D, D),
        output_weight[0],
        jnp.concatenate([packed(query_weight[0]), packed(key_weight[0]), packed(value_weight[0])], axis=0),
        vectors,
    )
    halves = []
    for array in own[:4]:
        rows = array.shape[0] // 2
        halves.append(swap(lax.dynamic_slice_in_dim(array, core * rows, rows, 0)))
    rest = [partner(array, "dp", 1) for array in halves]
    other = tuple(halves) + tuple(rest) + (swap(own[4]),)

    seg_row = jnp.where(leading, segment_ids[0], segment_ids[1])[None]
    mask_row = jnp.where(leading, masked_pos[0], masked_pos[1])[None]
    earlier = jnp.sum((seg_row < seg_row.T).astype(jnp.int32), axis=1)
    places = lax.iota(jnp.int32, N) - earlier
    embed_vec = jnp.stack([embed_gain, embed_bias])

    def chunked(arrays):
        return jnp.concatenate([array.reshape(devices, -1, D) for array in arrays], axis=1)

    def split_halves(values):
        mine = jnp.where(leading, values[:half], values[half:])
        theirs = jnp.where(leading, values[half:], values[:half])
        return mine, theirs

    def join_halves(mine, theirs):
        return jnp.where(leading, jnp.concatenate([mine, theirs]), jnp.concatenate([theirs, mine]))

    picked, saved0, saved1, hat_e, stat_e = forward_call(
        flag, slot_rows, dense_rows, slot_col, places[:, None], seg_row.T, seg_row, mask_row.T, position_table, embed_vec, own, other
    )
    mine, theirs = split_halves(picked)
    head_rows = join_halves(mine, swap(theirs))
    small = devices <= 16
    heads = [partner(head_rows, "dp", 4 * step) for step in (1, 2, 3)] if small else [lax.all_gather(head_rows, "dp", axis=0)]
    rows_back = back_pass(flat_grad, table)
    rows_back, heads = lax.optimization_barrier((rows_back, heads))
    if small:
        heads = jnp.stack([head_rows] + heads)
        heads = [heads, partner(heads, "dp", 2)]
    grad_parts = after(grad_parts, rows_back)
    grad_rows = exchange(grad_parts).reshape(devices * masks, shard_rows)
    mine, theirs = split_halves(rows_back)
    picked_back = join_halves(mine, swap(theirs)).astype(BF)

    def spread_on(array):
        if devices <= 16:
            return array
        groups = [list(range(low, devices, 16)) for low in range(16)]
        return lax.psum(array.astype(F32), "dp", axis_index_groups=groups).astype(BF)

    low_place = (place % 16).astype(jnp.int32).reshape(1)
    side_y = ((place // 2) % 2).astype(jnp.int32).reshape(1)
    me_z = ((place // 4) % 4).astype(jnp.int32).reshape(1)

    def across_z(parts):
        return [spread_on(parts[0])] + [partner(spread_on(parts[step]), "dp", 4 * step) for step in (1, 2, 3)]

    sixteens = [list(range(low, low + 16)) for low in range(0, devices, 16)]

    def sum_to_owner(packed):
        return spread_on(lax.psum_scatter(packed, "dp", scatter_dimension=0, axis_index_groups=sixteens, tiled=True)[0])

    packed_a1, attn1, low1, vec1 = backward_a_call(False, flag, [picked_back, mask_row], own, other, saved1)
    part_a1 = sum_to_owner(packed_a1)
    keep_b1, away_b1, middle = backward_b_call(False, flag, [attn1, low1, vec1], own, other, saved1)
    middle, away_b1 = lax.optimization_barrier((middle, away_b1))
    came_b1 = partner(away_b1, "dp", 1)
    keep_a0, away_a0, attn0, low0, vec0 = backward_a_call(True, flag, [middle], own, other, saved0)
    attn0, heads, away_a0, grad_rows = lax.optimization_barrier((attn0, heads, away_a0, grad_rows))
    if small:
        heads = jnp.concatenate(heads)
        heads = [heads, partner(heads, "dp", 1)]
    came_a0 = partner(away_a0, "dp", 1)
    keep_b0, away_b0, back, slot_grad = backward_b_call(
        True, flag, [attn0, low0, vec0, slot_row, places[None], hat_e, stat_e, embed_vec], own, other, saved0, slots
    )
    slot_grad, away_b0, came_a0, came_b1, heads = lax.optimization_barrier((slot_grad, away_b0, came_a0, came_b1, heads))
    keep_a0, away_a0 = step_y(side_y, keep_a0, came_a0)
    away_a0, away_b0, head_rows, slot_grad, keep_b1, came_b1 = lax.optimization_barrier(
        (away_a0, away_b0, head_rows, slot_grad, keep_b1, came_b1)
    )
    came_a0 = partner(away_a0, "dp", 2)
    came_b0 = partner(away_b0, "dp", 1)
    logits = logit_pass(head_rows, table)
    keep_b1, away_b1 = step_y(side_y, keep_b1, came_b1)
    came_b1 = partner(away_b1, "dp", 2)
    keep_b0, away_b0 = step_y(side_y, keep_b0, came_b0)
    came_a0, logits, away_b0, came_b1 = lax.optimization_barrier((came_a0, logits, away_b0, came_b1))
    logits = logits.reshape(2, half, vocab)
    local_a0 = step_z(me_z, keep_a0, came_a0)
    local_a0, away_b0, keep_b1 = lax.optimization_barrier((local_a0, away_b0, keep_b1))
    parts_a0 = across_z(local_a0)
    came_b0 = partner(away_b0, "dp", 2)
    local_b1 = step_z(me_z, keep_b1, came_b1)
    local_b0 = step_z(me_z, keep_b0, came_b0)

    sent = exchange(slot_grad.reshape(devices, room, D)).reshape(slots, D)
    crowd_sum = lax.cond(
        crowded,
        lambda: dense_call(base, gather_by_exchange(ids[None]), gather_by_exchange(back), shard_rows),
        lambda: jnp.zeros((shard_rows, D), F32),
    )
    names = jnp.where(crowded, -1, asked)
    if small:
        partial = owner_call(low_place, base, names, sent, grad_rows, heads, crowd_sum)
    else:
        one_hot = (names.reshape(1, slots) == (lax.iota(jnp.int32, shard_rows) + base)[:, None]).astype(BF)
        partial = jnp.dot(one_hot, sent, preferred_element_type=F32) + crowd_sum
        every_head = heads[0].reshape(devices * masks, D)
        partial += lax.dot_general(grad_rows, every_head, (((0,), (0,)), ((), ())), preferred_element_type=F32)
        partial = partial.astype(BF)
    def to_all(chunk, earlier):
        held = jnp.stack([chunk] + [partner(chunk, "dp", 4 * step) for step in (1, 2, 3)])
        held = after(held, earlier)
        held = jnp.concatenate([held, partner(held, "dp", 2)])
        return held, partner(held, "dp", 1)

    parts_a0, local_b0, local_b1, partial = lax.optimization_barrier((parts_a0, local_b0, local_b1, partial))
    parts_b0 = across_z(local_b0)
    parts_b1 = across_z(local_b1)
    mine_b, theirs_b = finish_call(1, flag, low_place, parts_b1, parts_b0)
    theirs_b = swap(theirs_b)
    chunk_b = (mine_b.astype(F32) + theirs_b.astype(F32)).astype(BF)
    mine_a, theirs_a = finish_call(0, flag, low_place, [part_a1], parts_a0)
    theirs_a = swap(theirs_a)
    chunk_a = (mine_a.astype(F32) + theirs_a.astype(F32)).astype(BF)
    all_a = lax.all_gather(chunk_a, "dp", axis=0, axis_index_groups=sixteens)
    swapped = swap(partial)
    table_total = partial.astype(F32) + swapped.astype(F32)
    shrink_total, expand_total, output_total, query_total, key_total, value_total, vec_total, embed_total, position_total = unpack_call(
        flag, low_place, all_a, *to_all(chunk_b, swapped)
    )
    embed_total = embed_total.reshape(2, D // 2)
    return (
        logits,
        table_total,
        position_total,
        embed_total[0],
        embed_total[1],
        query_total[None],
        key_total[None],
        value_total[None],
        output_total[None],
        vec_total[0:1],
        vec_total[1:2],
        expand_total.reshape(1, GROUPS, WIDE, D),
        jnp.swapaxes(shrink_total.reshape(1, GROUPS, WIDE, D), 2, 3),
        vec_total[2:3],
        vec_total[3:4],
    )


def solution(mesh):
    placed = (
        P("dp", None),
        P("dp", None),
        P("dp", None),
        P("dp", None),
        P(),
        P(),
        P(),
        P("section", None, None, None),
        P("section", None, None, None),
        P("section", None, None, None),
        P("section", None, None),
        P("section", None),
        P("section", None),
        P("section", None, None, None),
        P("section", None, None, None),
        P("section", None),
        P("section", None),
        P("dp", "section", None),
    )
    return jax.shard_map(
        per_device,
        mesh=mesh,
        in_specs=placed,
        out_specs=(
            P("dp", "section", None),
            P("dp", None),
            P(None, "section"),
            P("section"),
            P("section"),
            P("section", None, None, None),
            P("section", None, None, None),
            P("section", None, None, None),
            P("section", None, None),
            P("section", None),
            P("section", None),
            P("section", None, None, None),
            P("section", None, None, None),
            P("section", None),
            P("section", None),
        ),
        check_vma=False,
    )
```

```python
import functools
import jax
import jax.numpy as jnp
from jax import lax
from jax.sharding import PartitionSpec as P
from jax.experimental import pallas as pl
from jax.experimental.pallas import tpu as pltpu

HEAD = 64
norm_eps = 1e-06
BF = jnp.bfloat16
F32 = jnp.float32
LANE = 128
N = 512
D = 768
FF = 3072
GROUPS = 4
WIDE = 192
HEADS = 12
PAIRS = 6
VMEM_LIMIT = 60 * 1024 * 1024
QKV_ROWS = 768
CHUNKS = 16
ROWS_A = 144
ROWS_B = 48
SLAB = 16
GFLOP = 10 ** 9


def mm(a, b):
    return lax.dot_general(a, b, (((1,), (0,)), ((), ())), preferred_element_type=F32)


def mm_nt(a, b):
    return lax.dot_general(a, b, (((1,), (1,)), ((), ())), preferred_element_type=F32)


def mm_tn(a, b):
    return lax.dot_general(a, b, (((0,), (0,)), ((), ())), preferred_element_type=F32)


def window(group):
    return 384 * (group // 2) + 128 * (group % 2)


def lanes(group):
    return slice(window(group), window(group) + 256)


def own_lanes(group):
    counter = lax.broadcasted_iota(jnp.int32, (1, 256), 1)
    return counter < WIDE if group % 2 == 0 else counter >= 64


def fetch_weights(refs, own, other, use_own, core, sems):
    shrink, expand, output, qkv, vecs = refs
    mine, rest = other[0:4], other[4:8]

    def copies(sources, halves):
        made = []
        for number in range(2):
            half = halves[number]
            shrink_src, expand_src, output_src, qkv_src = sources[number]
            for j in range(2 if shrink is not None else 0):
                made.append(pltpu.make_async_copy(shrink_src.at[pl.ds(j * WIDE, WIDE)], shrink.at[2 * half + j, pl.ds(64 * j, WIDE)], sems.at[6 * number + j]))
                made.append(pltpu.make_async_copy(expand_src.at[pl.ds(j * WIDE, WIDE)], expand.at[2 * half + j, pl.ds(64 * j, WIDE)], sems.at[6 * number + 2 + j]))
            if output is not None:
                made.append(pltpu.make_async_copy(output_src, output.at[pl.ds(pl.multiple_of(half * 384, 384), 384)], sems.at[6 * number + 4]))
            if qkv is not None:
                made.append(pltpu.make_async_copy(qkv_src, qkv.at[pl.ds(pl.multiple_of(half * 288, 288), 288)], sems.at[6 * number + 5]))
        return made

    halves_of = [[ref.at[pl.ds(h * (ref.shape[0] // 2), ref.shape[0] // 2)] for ref in own[0:4]] for h in range(2)]
    whole = copies(halves_of, (0, 1))
    parts = copies((mine, rest), (core, 1 - core))
    if vecs is not None:
        whole.append(pltpu.make_async_copy(own[4], vecs, sems.at[12]))
        parts.append(pltpu.make_async_copy(other[8], vecs, sems.at[12]))

    @pl.when(use_own)
    def _():
        for c in whole:
            c.start()

    @pl.when(jnp.logical_not(use_own))
    def _():
        for c in parts:
            c.start()

    for g in range(GROUPS if shrink is not None else 0):
        at = WIDE * (1 - g % 2)
        shrink[g, at : at + 64, :] = jnp.zeros((64, D), BF)
        expand[g, at : at + 64, :] = jnp.zeros((64, D), BF)
    return whole


def pad_qkv(qkv, padded):
    for which in range(3):
        for g in range(GROUPS):
            at = 64 * (g % 2)
            block = qkv[which * WIDE : (which + 1) * WIDE, lanes(g)]
            padded[which, g, at : at + WIDE, :] = jnp.where(own_lanes(g), block, jnp.zeros_like(block))
            gap = WIDE * (1 - g % 2)
            padded[which, g, gap : gap + 64, :] = jnp.zeros((64, 256), BF)


def norm_parts(values):
    centre = jnp.mean(values, axis=-1, keepdims=True)
    shifted = values - centre
    spread = jnp.mean(shifted * shifted, axis=-1, keepdims=True)
    rstd = lax.rsqrt(spread + norm_eps)
    return shifted * rstd, rstd


def norm_back(gradient, hat, rstd, gain):
    scaled = gradient * gain
    first = jnp.mean(scaled, axis=-1, keepdims=True)
    second = jnp.mean(scaled * hat, axis=-1, keepdims=True)
    return rstd * (scaled - first - hat * second)


def join_pair(low, high):
    return jnp.concatenate([low[:, :128], low[:, 128:] + high[:, :128], high[:, 128:]], axis=1)


def layer_fwd(x_ref, bias_ref, w, saves, stats_ref, grow_ref, save_done):
    shrink, expand, output, qkv_pad, vecs = w
    x_low, q_ref, k_ref, v_ref, e_ref, mix_ref, hat_a, hidden_low, active, slope, hat_f, inv_ref, full_ref = saves
    x_low[...] = x_ref[...].astype(BF)
    for which, target in enumerate((q_ref, k_ref, v_ref)):
        for p in range(2):
            low = mm(x_low[:, lanes(2 * p)], qkv_pad[which, 2 * p])
            high = mm(x_low[:, lanes(2 * p + 1)], qkv_pad[which, 2 * p + 1])
            joined = join_pair(low, high).astype(BF)
            if which == 0:
                joined = joined * jnp.asarray(HEAD ** (-0.5), BF)
            target[:, 384 * p : 384 * (p + 1)] = joined
    save_done(0)
    stats_ref[...] = jnp.zeros_like(stats_ref)
    lane = lax.broadcasted_iota(jnp.int32, (1, LANE), 1)

    def pair_body(p, carry):
        at = pl.ds(pl.multiple_of(p * LANE, LANE), LANE)
        qs, ks, vs = q_ref[:, at], k_ref[:, at], v_ref[:, at]
        outs = []
        for side in range(2):
            mine = (lane < HEAD) if side == 0 else (lane >= HEAD)
            scores = mm_nt(jnp.where(mine, qs, jnp.zeros_like(qs)), ks) + bias_ref[...]
            top = jnp.max(scores, axis=-1, keepdims=True)
            e = jnp.exp(scores - top).astype(BF)
            e_ref[2 * p + side] = e
            outs.append(mm(e, jnp.where(mine, vs, jnp.ones_like(vs))))
        inv = 1.0 / pltpu.roll(jnp.where(lane < HEAD, outs[1], outs[0]), HEAD, 1)
        full = jnp.where(lane < HEAD, outs[0], outs[1]) * inv
        inv_ref[:, at] = inv
        full_ref[:, at] = full
        mix_ref[:, at] = full.astype(BF)
        return carry

    lax.fori_loop(0, PAIRS, pair_body, 0)
    save_done(1)
    residual = x_ref[...] + mm(mix_ref[...], output[...])
    hat, rstd = norm_parts(residual)
    hat_a[...] = hat.astype(BF)
    stats_ref[...] = jnp.where(lane == 12, rstd, stats_ref[...])
    hidden = hat * vecs[0:1, :] + vecs[1:2, :]
    hidden_low[...] = hidden.astype(BF)
    grow_ref[...] = hidden
    for g in range(GROUPS):
        wide = slice(g * D, (g + 1) * D)
        expanded = mm(hidden_low[:, lanes(g)], expand[g])
        phi = 0.5 * (1.0 + lax.erf(expanded * (2.0 ** -0.5)))
        density = jnp.exp(expanded * expanded * -0.5) * (2.0 * jnp.pi) ** -0.5
        act = (expanded * phi).astype(BF)
        active[:, wide] = act
        slope[:, wide] = (phi + expanded * density).astype(BF)
        grow_ref[:, lanes(g)] += mm_nt(act, shrink[g])
    save_done(2)
    hat, rstd = norm_parts(grow_ref[...])
    hat_f[...] = hat.astype(BF)
    stats_ref[...] = jnp.where(lane == 13, rstd, stats_ref[...])
    x_ref[...] = hat * vecs[2:3, :] + vecs[3:4, :]
    save_done(3)


SAVE_SHAPES = (
    (N, D), (N, D), (N, D), (N, D), (HEADS, N, N), (N, D), (N, D), (N, D), (N, FF), (N, FF), (N, D),
    (N, D), (N, D), (N, LANE),
)
SAVE_TYPES = (BF,) * 11 + (F32,) * 3
SAVE_STAGES = ((0, 1, 2, 3), (4, 5, 11, 12), (6, 7, 8, 9), (10, 13))
SAVES = 14


def weight_scratch():
    return [
        pltpu.VMEM((GROUPS, 256, D), BF),
        pltpu.VMEM((GROUPS, 256, D), BF),
        pltpu.VMEM((D, D), BF),
        pltpu.VMEM((3 * WIDE, D), BF),
        pltpu.VMEM((8, D), F32),
    ]


def fwd_kernel(flag, slot_rows, dense_rows, slot_col, place_col, seg_col, seg_row, mask_col, place_table, embed_vec, *rest):
    rest = list(rest)

    def take(n):
        got = rest[:n]
        del rest[:n]
        return got

    own, other = take(5), take(9)
    (picked_ref,) = take(1)
    outs = [take(SAVES), take(SAVES)]
    hat_e_ref, stat_e_ref = take(2)
    weights = [take(5), take(5)]
    qkv_pad, bias_ref, x_ref, grow_ref = take(4)
    saves = take(SAVES)
    sem_w, sem_s, sem_d = take(3)
    leading = flag[0] == 0
    waits = [
        fetch_weights(weights[0], own, other, leading, flag[2], sem_w.at[0]),
        fetch_weights(weights[1], own, other, jnp.logical_not(leading), flag[2], sem_w.at[1]),
    ]
    counter = lax.broadcasted_iota(jnp.int32, (N, N), 1)
    one_hot = (place_col[...] == counter).astype(BF)
    slots = slot_rows.shape[0]
    wanted = (slot_col[...] == lax.broadcasted_iota(jnp.int32, (N, slots), 1)).astype(BF)
    x_ref[...] = mm(wanted, slot_rows[...])

    @pl.when(flag[1] != 0)
    def _():
        c = pltpu.make_async_copy(dense_rows, saves[0], sem_d)
        c.start()
        c.wait()
        x_ref[...] = saves[0][...].astype(F32)

    summed = x_ref[...] + mm(one_hot, place_table[...])
    hat, rstd = norm_parts(summed)
    hat_e_ref[...] = hat.astype(BF)
    stat_e_ref[...] = jnp.broadcast_to(rstd, (N, LANE))
    x_ref[...] = hat * embed_vec[0:1, :] + embed_vec[1:2, :]
    bias_ref[...] = jnp.where(seg_col[...] == seg_row[...], 0.0, -1000000000.0)
    drains = []
    for number in range(2):
        for c in waits[number] + drains:
            c.wait()
        drains = []
        shrink, expand, output, qkv, vecs = weights[number]
        pad_qkv(qkv, qkv_pad)

        def save_done(stage, number=number, drains=drains):
            for i in SAVE_STAGES[stage]:
                c = pltpu.make_async_copy(saves[i], outs[number][i], sem_s.at[number, i])
                c.start()
                drains.append(c)

        layer_fwd(
            x_ref, bias_ref, (shrink, expand, output, qkv_pad, vecs),
            saves[:13], saves[13], grow_ref, save_done,
        )
        if number == 0:
            x_ref[...] = x_ref[...].astype(BF).astype(F32)
    picks = (mask_col[...] == lax.broadcasted_iota(jnp.int32, (mask_col.shape[0], N), 1)).astype(BF)
    picked_ref[...] = mm(picks, x_ref[...].astype(BF)).astype(BF)
    for c in drains:
        c.wait()


def save_structs():
    return [jax.ShapeDtypeStruct(s, t) for s, t in zip(SAVE_SHAPES, SAVE_TYPES)]


def save_scratch():
    return [pltpu.VMEM(s, t) for s, t in zip(SAVE_SHAPES, SAVE_TYPES)]


VM = pl.BlockSpec(memory_space=pltpu.VMEM)
HB = pl.BlockSpec(memory_space=pl.ANY)
SM = pl.BlockSpec(memory_space=pltpu.SMEM)


def forward_call(flag, slot_rows, dense_rows, slot_col, place_col, seg_col, seg_row, mask_col, place_table, embed_vec, own, other):
    masks = mask_col.shape[0]
    out = pl.pallas_call(
        fwd_kernel,
        out_shape=[jax.ShapeDtypeStruct((masks, D), BF)] + save_structs() * 2
        + [jax.ShapeDtypeStruct((N, D), BF), jax.ShapeDtypeStruct((N, LANE), F32)],
        in_specs=[SM, VM, HB] + [VM] * 7 + [HB] * 14,
        out_specs=[VM] + [HB] * (2 * SAVES) + [VM] * 2,
        scratch_shapes=weight_scratch() * 2
        + [pltpu.VMEM((3, GROUPS, 256, 256), BF), pltpu.VMEM((N, N), F32), pltpu.VMEM((N, D), F32), pltpu.VMEM((N, D), F32)]
        + save_scratch()
        + [pltpu.SemaphoreType.DMA((2, 13)), pltpu.SemaphoreType.DMA((2, SAVES)), pltpu.SemaphoreType.DMA],
        compiler_params=pltpu.CompilerParams(vmem_limit_bytes=VMEM_LIMIT),
        cost_estimate=pl.CostEstimate(flops=36 * GFLOP, bytes_accessed=60 << 20, transcendentals=0),
        name="forward_layers",
    )(flag, slot_rows, dense_rows, slot_col, place_col, seg_col, seg_row, mask_col, place_table, embed_vec, *own, *other)
    return out[0], out[1 : 1 + SAVES], out[1 + SAVES : 1 + 2 * SAVES], out[-2], out[-1]


def chunk_place(chunk, core, in_order):
    if in_order:
        return chunk
    return chunk // 2 + (CHUNKS // 2) * (core if chunk % 2 == 0 else 1 - core)


def put_chunks(packed_ref, core, in_order, source, rows, at):
    for chunk in range(CHUNKS):
        packed_ref[chunk_place(chunk, core, in_order), at : at + rows, :] = source[chunk * rows : (chunk + 1) * rows, :].astype(BF)


def ship_chunks(packed_ref, outs, sems):
    if len(outs) == 1:
        made = [pltpu.make_async_copy(packed_ref, outs[0], sems.at[0])]
    else:
        half = CHUNKS // 2
        made = [pltpu.make_async_copy(packed_ref.at[pl.ds(i * half, half)], outs[i], sems.at[i]) for i in range(2)]
    for c in made:
        c.start()
    return made


def bwd_a_kernel(last, flag, *rest):
    rest = list(rest)

    def take(n):
        got = rest[:n]
        del rest[:n]
        return got

    if last:
        (go_in,) = take(1)
    else:
        picked_back, mask_row = take(2)
    own, other = take(5), take(9)
    sources = take(7)
    packed_out = take(2 if last else 1)
    attn_ref, back_low, vec_ref = take(3)
    weights = take(4)
    mid_ref, low_ref, packed_ref = take(3)
    saves = take(7)
    sem_w, sem_s, sem_o, sem_g = take(4)
    mix_ref, hat_a, hidden_low, active, slope, hat_f, stats_ref = saves
    shrink, expand, output, vecs = weights
    leading, core = flag[0] == 0, flag[2]
    use_own = leading if last else jnp.logical_not(leading)
    copies = [pltpu.make_async_copy(sources[i], saves[i], sem_s.at[i]) for i in range(7)]
    wide_copies = []
    for g in range(GROUPS):
        at = pl.ds(g * D, D)
        wide_copies.append([pltpu.make_async_copy(sources[i].at[:, at], saves[i].at[:, at], sem_g.at[i - 3, g]) for i in (3, 4)])
    for i in (5, 6):
        copies[i].start()
    waits = fetch_weights((shrink, expand, output, None, vecs), own, other, use_own, core, sem_w)
    copies[2].start()
    for pair in wide_copies:
        for c in pair:
            c.start()
    for i in (1, 0):
        copies[i].start()
    vec_ref[...] = jnp.zeros_like(vec_ref)
    if last:
        go = go_in[...].astype(F32)
    else:
        masks = mask_row.shape[1]
        spread = (lax.broadcasted_iota(jnp.int32, (N, masks), 0) == mask_row[...]).astype(BF)
        go = mm(spread, picked_back[...])
    lane = lax.broadcasted_iota(jnp.int32, (1, LANE), 1)

    def stat(index):
        return jnp.sum(jnp.where(lane == index, stats_ref[...], 0.0), axis=-1, keepdims=True)

    copies[5].wait()
    copies[6].wait()
    for c in waits:
        c.wait()
    hat = hat_f[...].astype(F32)
    vec_ref[2:3, :] = jnp.sum(go * hat, axis=0, keepdims=True)
    vec_ref[3:4, :] = jnp.sum(go, axis=0, keepdims=True)
    feed_back = norm_back(go, hat, stat(13), vecs[2:3, :])
    mid_ref[...] = feed_back
    low_ref[...] = feed_back.astype(BF)
    copies[2].wait()
    each = WIDE // (CHUNKS // GROUPS)
    for g in range(GROUPS):
        wide = slice(g * D, (g + 1) * D)
        rows = slice(64 * (g % 2), 64 * (g % 2) + WIDE)
        for c in wide_copies[g]:
            c.wait()
        shrink_in = low_ref[:, lanes(g)]
        shrink_grad = mm_tn(shrink_in, active[:, wide])[rows].astype(BF)
        expand_in = (mm(shrink_in, shrink[g]) * slope[:, wide].astype(F32)).astype(BF)
        expand_grad = mm_tn(hidden_low[:, lanes(g)], expand_in)[rows].astype(BF)
        mid_ref[:, lanes(g)] += mm_nt(expand_in, expand[g])
        for part in range(CHUNKS // GROUPS):
            chunk = g * (CHUNKS // GROUPS) + part
            at = chunk_place(chunk, core, not last)
            packed_ref[at, 0:each, :] = shrink_grad[part * each : (part + 1) * each, :]
            packed_ref[at, each : 2 * each, :] = expand_grad[part * each : (part + 1) * each, :]
    copies[1].wait()
    hidden_back = mid_ref[...]
    hat = hat_a[...].astype(F32)
    vec_ref[0:1, :] = jnp.sum(hidden_back * hat, axis=0, keepdims=True)
    vec_ref[1:2, :] = jnp.sum(hidden_back, axis=0, keepdims=True)
    attn_back = norm_back(hidden_back, hat, stat(12), vecs[0:1, :])
    attn_ref[...] = attn_back
    attended_in = attn_back.astype(BF)
    copies[0].wait()
    put_chunks(packed_ref, core, not last, mm_tn(mix_ref[...], attended_in), each, 2 * each)
    ship = ship_chunks(packed_ref, packed_out, sem_o)
    back_low[...] = mm_nt(attended_in, output[...]).astype(BF)
    for c in ship:
        c.wait()


def backward_a_call(last, flag, extra, own, other, saved):
    chosen = (5, 6, 7, 8, 9, 10, 13)
    return pl.pallas_call(
        functools.partial(bwd_a_kernel, last),
        out_shape=([jax.ShapeDtypeStruct((CHUNKS // 2, ROWS_A, D), BF)] * 2 if last else [jax.ShapeDtypeStruct((CHUNKS, ROWS_A, D), BF)])
        + [
            jax.ShapeDtypeStruct((N, D), F32), jax.ShapeDtypeStruct((N, D), BF), jax.ShapeDtypeStruct((16, D), F32),
        ],
        in_specs=[SM] + [VM] * len(extra) + [HB] * (14 + len(chosen)),
        out_specs=[HB] * (2 if last else 1) + [VM, VM, VM],
        scratch_shapes=[
            pltpu.VMEM((GROUPS, 256, D), BF), pltpu.VMEM((GROUPS, 256, D), BF), pltpu.VMEM((D, D), BF), pltpu.VMEM((8, D), F32),
            pltpu.VMEM((N, D), F32), pltpu.VMEM((N, D), BF), pltpu.VMEM((CHUNKS, ROWS_A, D), BF),
        ]
        + [pltpu.VMEM(SAVE_SHAPES[i], SAVE_TYPES[i]) for i in chosen]
        + [pltpu.SemaphoreType.DMA((13,)), pltpu.SemaphoreType.DMA((len(chosen),)), pltpu.SemaphoreType.DMA((2,)), pltpu.SemaphoreType.DMA((2, GROUPS))],
        compiler_params=pltpu.CompilerParams(vmem_limit_bytes=VMEM_LIMIT),
        cost_estimate=pl.CostEstimate(flops=12 * GFLOP, bytes_accessed=20 << 20, transcendentals=0),
        name="backward_first_a" if last else "backward_second_a",
    )(flag, *extra, *own, *other, *[saved[i] for i in chosen])


def bwd_b_kernel(last, flag, attn_in, back_low, vec_in, *rest):
    rest = list(rest)

    def take(n):
        got = rest[:n]
        del rest[:n]
        return got

    if last:
        slot_row, place_row, hat_e_ref, stat_e_ref, embed_vec = take(5)
    own, other = take(5), take(9)
    sources = take(7)
    keep_out, away_out, back_ref = take(3)
    if last:
        (slot_grad,) = take(1)
    qkv, qkv_pad, go_ref, vec_ref, packed_ref = take(5)
    dq_ref, dk_ref, dv_ref, grad_ref = take(4)
    saves = take(7)
    sem_w, sem_s, sem_o = take(3)
    x_low, q_ref, k_ref, v_ref, e_ref, inv_ref, full_ref = saves
    leading, core = flag[0] == 0, flag[2]
    use_own = leading if last else jnp.logical_not(leading)
    whole = pltpu.make_async_copy(sources[0], saves[0], sem_s.at[0, 0])

    def pair_copies(p):
        at = pl.ds(p * LANE if isinstance(p, int) else pl.multiple_of(p * LANE, LANE), LANE)
        made = [pltpu.make_async_copy(sources[4].at[pl.ds(2 * p, 2)], saves[4].at[pl.ds(2 * p, 2)], sem_s.at[4, p])]
        for i in (1, 2, 3, 5, 6):
            made.append(pltpu.make_async_copy(sources[i].at[:, at], saves[i].at[:, at], sem_s.at[i, p]))
        return made

    for p in range(PAIRS):
        for c in pair_copies(p):
            c.start()
    waits = fetch_weights((None, None, None, qkv, None), own, other, use_own, core, sem_w)
    whole.start()
    lane = lax.broadcasted_iota(jnp.int32, (1, LANE), 1)

    def pair_body(p, carry):
        for c in pair_copies(p):
            c.wait()
        at = pl.ds(pl.multiple_of(p * LANE, LANE), LANE)
        first = lane < HEAD
        d_low = (back_low[:, at].astype(F32) * inv_ref[:, at]).astype(BF)
        weighted = d_low.astype(F32) * full_ref[:, at]
        qs, ks, vs = q_ref[:, at], k_ref[:, at], v_ref[:, at]
        d_v = d_q = d_k = None
        for side in range(2):
            mine = first if side == 0 else jnp.logical_not(first)
            delta = jnp.sum(jnp.where(mine, weighted, 0.0), axis=-1, keepdims=True)
            e = e_ref[2 * p + side]
            d_side = jnp.where(mine, d_low, jnp.zeros_like(d_low))
            prob_back = mm_nt(d_side, vs)
            d_s = (e.astype(F32) * (prob_back - delta)).astype(BF)
            part_v = mm_tn(e, d_side)
            part_q = mm(d_s, jnp.where(mine, ks, jnp.zeros_like(ks)))
            part_k = mm_tn(d_s, jnp.where(mine, qs, jnp.zeros_like(qs)))
            d_v = part_v if d_v is None else d_v + part_v
            d_q = part_q if d_q is None else d_q + part_q
            d_k = part_k if d_k is None else d_k + part_k
        dv_ref[:, at] = d_v.astype(BF)
        dq_ref[:, at] = (d_q * HEAD ** (-0.5)).astype(BF)
        dk_ref[:, at] = d_k.astype(BF)
        return carry

    lax.fori_loop(0, PAIRS, pair_body, 0)
    whole.wait()
    for c in waits:
        c.wait()
    pad_qkv(qkv, qkv_pad)
    go_ref[...] = attn_in[...]
    vec_ref[...] = jnp.zeros_like(vec_ref)
    vec_ref[0:8, :] = vec_in[0:8, :]
    for which, d_ref in enumerate((dq_ref, dk_ref, dv_ref)):
        for p in range(2):
            made = []
            for g in (2 * p, 2 * p + 1):
                rows = slice(64 * (g % 2), 64 * (g % 2) + WIDE)
                d_part = d_ref[:, lanes(g)]
                made.append(jnp.where(own_lanes(g), mm_tn(x_low[:, lanes(g)], d_part)[rows], 0.0))
                go_ref[:, lanes(g)] += mm_nt(d_part, qkv_pad[which, g])
            grad_ref[which * WIDE : (which + 1) * WIDE, 384 * p : 384 * (p + 1)] = join_pair(*made).astype(BF)
    go = go_ref[...]
    if last:
        hat = hat_e_ref[...].astype(F32)
        gain_row = jnp.sum(go * hat, axis=0, keepdims=True)
        bias_row = jnp.sum(go, axis=0, keepdims=True)
        for s in range(2):
            at = slice(s * (D // 2), (s + 1) * (D // 2))
            vec_ref[8 + s : 9 + s, :] = jnp.concatenate([gain_row[:, at], bias_row[:, at]], axis=1)
        back = norm_back(go, hat, stat_e_ref[:, 0:1], embed_vec[0:1, :]).astype(BF)
        back_ref[...] = back
        places = (lax.broadcasted_iota(jnp.int32, (N, N), 0) == place_row[...]).astype(BF)
        grad = mm(places, back).astype(BF)
        for s in range(2):
            block = jnp.concatenate([grad[part * (N // 2) : (part + 1) * (N // 2), s * 384 : (s + 1) * 384] for part in range(2)], axis=1)
            put_chunks(packed_ref, core, False, block, SLAB, ROWS_B + s * SLAB)
        slots = slot_grad.shape[0]
        slot_grad[...] = mm((lax.broadcasted_iota(jnp.int32, (slots, N), 0) == slot_row[...]).astype(BF), back).astype(BF)
    else:
        back_ref[...] = go.astype(BF)
    grad_ref[3 * WIDE :, :] = vec_ref[...].astype(BF)
    put_chunks(packed_ref, core, False, grad_ref, ROWS_B, 0)
    for c in ship_chunks(packed_ref, (keep_out, away_out), sem_o):
        c.wait()


def backward_b_call(last, flag, extra, own, other, saved, slots=0):
    chosen = (0, 1, 2, 3, 4, 11, 12)
    rows = ROWS_B + 2 * SLAB if last else ROWS_B
    out_shape = [
        jax.ShapeDtypeStruct((CHUNKS // 2, rows, D), BF), jax.ShapeDtypeStruct((CHUNKS // 2, rows, D), BF),
        jax.ShapeDtypeStruct((N, D), BF),
    ]
    if last:
        out_shape.append(jax.ShapeDtypeStruct((slots, D), BF))
    return pl.pallas_call(
        functools.partial(bwd_b_kernel, last),
        out_shape=out_shape,
        in_specs=[SM] + [VM] * len(extra) + [HB] * (14 + len(chosen)),
        out_specs=[HB, HB] + [VM] * (len(out_shape) - 2),
        scratch_shapes=[
            pltpu.VMEM((3 * WIDE, D), BF), pltpu.VMEM((3, GROUPS, 256, 256), BF), pltpu.VMEM((N, D), F32),
            pltpu.VMEM((QKV_ROWS - 3 * WIDE, D), F32), pltpu.VMEM((CHUNKS, rows, D), BF),
        ]
        + [pltpu.VMEM((N, D), BF)] * 3 + [pltpu.VMEM((QKV_ROWS, D), BF)]
        + [pltpu.VMEM(SAVE_SHAPES[i], SAVE_TYPES[i]) for i in chosen]
        + [pltpu.SemaphoreType.DMA((13,)), pltpu.SemaphoreType.DMA((len(chosen), PAIRS)), pltpu.SemaphoreType.DMA((2,))],
        compiler_params=pltpu.CompilerParams(vmem_limit_bytes=VMEM_LIMIT),
        cost_estimate=pl.CostEstimate(flops=15 * GFLOP, bytes_accessed=20 << 20, transcendentals=0),
        name="backward_first_b" if last else "backward_second_b",
    )(flag, *extra, *own, *other, *[saved[i] for i in chosen])


def step_y_kernel(side_ref, keep_ref, came_ref, next_keep, next_away):
    side = side_ref[0]
    for j in range(next_keep.shape[0]):
        for target, which in ((next_keep, side), (next_away, 1 - side)):
            at = 2 * j + which
            target[j] = (keep_ref[at].astype(F32) + came_ref[at].astype(F32)).astype(BF)


def step_y(side, keep, came):
    half = jax.ShapeDtypeStruct((keep.shape[0] // 2,) + keep.shape[1:], BF)
    return pl.pallas_call(
        step_y_kernel, out_shape=[half, half], in_specs=[SM, VM, VM], out_specs=[VM, VM],
        compiler_params=pltpu.CompilerParams(vmem_limit_bytes=VMEM_LIMIT),
        cost_estimate=pl.CostEstimate(flops=GFLOP, bytes_accessed=6 << 20, transcendentals=0), name="halve_chunks",
    )(side, keep, came)


def step_z_kernel(me_ref, keep_ref, came_ref, *outs):
    for step in range(4):
        at = me_ref[0] ^ step
        outs[step][...] = (keep_ref[at].astype(F32) + came_ref[at].astype(F32)).astype(BF)


def step_z(me, keep, came):
    one = jax.ShapeDtypeStruct(keep.shape[1:], BF)
    return pl.pallas_call(
        step_z_kernel, out_shape=[one] * 4, in_specs=[SM, VM, VM], out_specs=[VM] * 4,
        compiler_params=pltpu.CompilerParams(vmem_limit_bytes=VMEM_LIMIT),
        cost_estimate=pl.CostEstimate(flops=GFLOP, bytes_accessed=4 << 20, transcendentals=0), name="four_chunks",
    )(me, keep, came)


def finish_kernel(part, count1, flag, place_ref, *refs):
    parts1, parts0 = refs[:count1], refs[count1:-2]
    mine, theirs = refs[-2:]
    sums = []
    for parts in (parts0, parts1):
        total = parts[0][...].astype(F32)
        for ref in parts[1:]:
            total = total + ref[...].astype(F32)
        sums.append(total)
    first, second = sums
    if part == 1:
        row = lax.broadcasted_iota(jnp.int32, (ROWS_B, 1), 0) + place_ref[0] * ROWS_B
        extra = jnp.where(row >= 3 * WIDE + 8, first[:ROWS_B], 0.0)
        second = jnp.concatenate([second + extra, first[ROWS_B + SLAB :]], axis=0)
        first = first[: ROWS_B + SLAB]
    leading = flag[0] == 0
    mine[...] = jnp.where(leading, first, second).astype(BF)
    theirs[...] = jnp.where(leading, second, first).astype(BF)


def finish_call(part, flag, place, parts1, parts0):
    rows = ROWS_A if part == 0 else ROWS_B + SLAB
    one = jax.ShapeDtypeStruct((rows, D), BF)
    return pl.pallas_call(
        functools.partial(finish_kernel, part, len(parts1)), out_shape=[one, one],
        in_specs=[SM, SM] + [VM] * (len(parts1) + len(parts0)), out_specs=[VM] * 2,
        compiler_params=pltpu.CompilerParams(vmem_limit_bytes=VMEM_LIMIT),
        cost_estimate=pl.CostEstimate(flops=GFLOP, bytes_accessed=2 << 20, transcendentals=0), name="finish_chunks",
    )(flag, place, *parts1, *parts0)


def unpack_kernel(flag, place_ref, a_all, b_own, b_came, shrink, expand, output, query, key, value, vecs, embed, position, grid, slab):
    each = ROWS_A // 3
    half = CHUNKS // 2
    for i in range(CHUNKS):
        rows = slice(i * each, (i + 1) * each)
        block = a_all[i].astype(F32)
        shrink[rows, :] = block[0:each]
        expand[rows, :] = block[each : 2 * each]
        output[rows, :] = block[2 * each :]
    for core in range(2):
        b_ref = b_own if core == 0 else b_came
        for i in range(half):
            device = place_ref[0] ^ (4 * (i % 4) + 2 * (i // 4) + core)
            block = b_ref[i].astype(F32)
            grid[pl.ds(pl.multiple_of(device * ROWS_B, ROWS_B), ROWS_B), :] = block[:ROWS_B]
            slab[pl.ds(pl.multiple_of(device * SLAB, SLAB), SLAB), :] = block[ROWS_B:]
    for which, target in enumerate((query, key, value)):
        for g in range(GROUPS):
            target[g] = grid[which * WIDE : (which + 1) * WIDE, g * WIDE : (g + 1) * WIDE]
    vecs[...] = grid[3 * WIDE : 3 * WIDE + 8, :]
    rows = grid[3 * WIDE + 8 : 3 * WIDE + 16, :]
    embed[...] = jnp.where(flag[0] == 0, rows[0:1], rows[1:2])
    for part in range(2):
        position[part * (N // 2) : (part + 1) * (N // 2), :] = slab[:, part * (D // 2) : (part + 1) * (D // 2)]


def unpack_call(flag, place, a_all, b_own, b_came):
    square = jax.ShapeDtypeStruct((D, D), F32)
    group = jax.ShapeDtypeStruct((GROUPS, WIDE, WIDE), F32)
    return pl.pallas_call(
        unpack_kernel,
        out_shape=[square] * 3 + [group] * 3
        + [jax.ShapeDtypeStruct((8, D), F32), jax.ShapeDtypeStruct((1, D), F32), jax.ShapeDtypeStruct((N, D // 2), F32)],
        in_specs=[SM, SM] + [VM] * 3,
        out_specs=[VM] * 9,
        scratch_shapes=[pltpu.VMEM((QKV_ROWS, D), F32), pltpu.VMEM((CHUNKS * SLAB, D), F32)],
        compiler_params=pltpu.CompilerParams(vmem_limit_bytes=VMEM_LIMIT),
        cost_estimate=pl.CostEstimate(flops=GFLOP, bytes_accessed=16 << 20, transcendentals=0), name="unpack_sums",
    )(flag, place, a_all, b_own, b_came)


def plan_kernel(room, id_row, id_col, owner_row, owner_col, slot_col, slot_row, want_ref, most_ref):
    slots = want_ref.shape[1]
    across = lax.broadcasted_iota(jnp.int32, (N, N), 1)
    down = lax.broadcasted_iota(jnp.int32, (N, N), 0)
    same = id_col[...] == id_row[...]
    first_col = jnp.min(jnp.where(same, across, N).astype(F32), axis=1, keepdims=True).astype(jnp.int32)
    first_row = jnp.min(jnp.where(same, down, N).astype(F32), axis=0, keepdims=True).astype(jnp.int32)
    fresh_row = first_row == lax.broadcasted_iota(jnp.int32, (1, N), 1)
    fresh_col = first_col == lax.broadcasted_iota(jnp.int32, (N, 1), 0)
    mates = owner_col[...] == owner_row[...]
    rank_col = jnp.sum(jnp.where(mates & fresh_row & (across < first_col), 1.0, 0.0), axis=1, keepdims=True).astype(jnp.int32)
    rank_row = jnp.sum(jnp.where(mates & fresh_col & (down < first_row), 1.0, 0.0), axis=0, keepdims=True).astype(jnp.int32)
    col = jnp.where(rank_col < room, owner_col[...] * room + rank_col, -1)
    slot_col[...] = col
    slot_row[...] = jnp.where(rank_row < room, owner_row[...] * room + rank_row, -1)
    chosen = (col == lax.broadcasted_iota(jnp.int32, (N, slots), 1)) & fresh_col
    want = jnp.sum(jnp.where(chosen, (id_col[...] + 1).astype(F32), 0.0), axis=0, keepdims=True)
    want_ref[...] = want.astype(jnp.int32) - 1
    most = jnp.max(rank_row.astype(F32), axis=1, keepdims=True).astype(jnp.int32) + 1
    most_ref[...] = jnp.broadcast_to(most, most_ref.shape)


def plan_call(ids, owners, room, slots):
    return pl.pallas_call(
        functools.partial(plan_kernel, room),
        out_shape=[
            jax.ShapeDtypeStruct((N, 1), jnp.int32), jax.ShapeDtypeStruct((1, N), jnp.int32),
            jax.ShapeDtypeStruct((1, slots), jnp.int32), jax.ShapeDtypeStruct((8, LANE), jnp.int32),
        ],
        in_specs=[VM] * 4,
        out_specs=[VM] * 4,
        compiler_params=pltpu.CompilerParams(vmem_limit_bytes=VMEM_LIMIT),
        name="plan_slots",
    )(ids[None], ids[:, None], owners[None], owners[:, None])


def serve_kernel(base_ref, ids_ref, table_ref, out_ref):
    counter = lax.broadcasted_iota(jnp.int32, (ids_ref.shape[0], table_ref.shape[0]), 1) + base_ref[0]
    out_ref[...] = mm((ids_ref[...] == counter).astype(BF), table_ref[...]).astype(BF)


def serve_call(base, ids_col, table):
    return pl.pallas_call(
        serve_kernel,
        out_shape=jax.ShapeDtypeStruct((ids_col.shape[0], D), BF),
        in_specs=[SM, VM, VM],
        out_specs=VM,
        compiler_params=pltpu.CompilerParams(vmem_limit_bytes=VMEM_LIMIT),
        cost_estimate=pl.CostEstimate(flops=3 * GFLOP, bytes_accessed=20 << 20, transcendentals=0),
        name="serve_rows",
    )(base, ids_col, table)


def back_pass_kernel(grad_ref, table_ref, back_ref):
    @pl.when(pl.program_id(0) == 0)
    def _():
        back_ref[...] = jnp.zeros_like(back_ref)

    back_ref[...] += mm(grad_ref[...], table_ref[...])


def back_pass(flat_grad, table):
    vocab, masks = table.shape[0], flat_grad.shape[0]
    tile = 1536
    return pl.pallas_call(
        back_pass_kernel,
        grid=(vocab // tile,),
        out_shape=jax.ShapeDtypeStruct((masks, D), F32),
        in_specs=[pl.BlockSpec((masks, tile), lambda i: (0, i)), pl.BlockSpec((tile, D), lambda i: (i, 0))],
        out_specs=pl.BlockSpec((masks, D), lambda i: (0, 0)),
        compiler_params=pltpu.CompilerParams(vmem_limit_bytes=VMEM_LIMIT),
        cost_estimate=pl.CostEstimate(flops=10 * GFLOP, bytes_accessed=20 << 20, transcendentals=0),
        name="table_back_pass",
    )(flat_grad, table)


def logit_pass_kernel(head_ref, table_ref, logit_ref):
    logit_ref[...] = mm_nt(head_ref[...], table_ref[...]).astype(BF)


def logit_pass(head_rows, table):
    vocab, masks = table.shape[0], head_rows.shape[0]
    tile = 1536
    return pl.pallas_call(
        logit_pass_kernel,
        grid=(vocab // tile,),
        out_shape=jax.ShapeDtypeStruct((masks, vocab), BF),
        in_specs=[pl.BlockSpec((masks, D), lambda i: (0, 0)), pl.BlockSpec((tile, D), lambda i: (i, 0))],
        out_specs=pl.BlockSpec((masks, tile), lambda i: (0, i)),
        compiler_params=pltpu.CompilerParams(vmem_limit_bytes=VMEM_LIMIT),
        cost_estimate=pl.CostEstimate(flops=10 * GFLOP, bytes_accessed=20 << 20, transcendentals=0),
        name="table_logit_pass",
    )(head_rows, table)


def owner_kernel(place_ref, base_ref, ids_ref, rows_ref, grads_ref, heads_own, heads_came, crowd_ref, out_ref, ordered):
    masks = heads_own.shape[1]
    for core in range(2):
        heads = heads_own if core == 0 else heads_came
        for i in range(heads.shape[0]):
            device = place_ref[0] ^ (4 * (i % 4) + 2 * (i // 4) + core)
            ordered[pl.ds(pl.multiple_of(device * masks, masks), masks), :] = heads[i]
    counter = lax.broadcasted_iota(jnp.int32, (out_ref.shape[0], ids_ref.shape[1]), 0) + base_ref[0]
    total = crowd_ref[...] + mm((counter == ids_ref[...]).astype(BF), rows_ref[...])
    out_ref[...] = (total + mm_tn(grads_ref[...], ordered[...])).astype(BF)


def owner_call(place, base, ids_row, rows, grads, heads, crowd):
    masks = heads[0].shape[1]
    return pl.pallas_call(
        owner_kernel,
        out_shape=jax.ShapeDtypeStruct(crowd.shape, BF),
        in_specs=[SM, SM] + [VM] * 6,
        out_specs=VM,
        scratch_shapes=[pltpu.VMEM((2 * heads[0].shape[0] * masks, D), BF)],
        compiler_params=pltpu.CompilerParams(vmem_limit_bytes=VMEM_LIMIT),
        cost_estimate=pl.CostEstimate(flops=6 * GFLOP, bytes_accessed=20 << 20, transcendentals=0),
        name="owner_sum",
    )(place, base, ids_row, rows, grads, heads[0], heads[1], crowd)


def dense_kernel(base_ref, ids_ref, rows_ref, out_ref):
    @pl.when(pl.program_id(0) == 0)
    def _():
        out_ref[...] = jnp.zeros_like(out_ref)

    counter = lax.broadcasted_iota(jnp.int32, (out_ref.shape[0], N), 0) + base_ref[0]
    out_ref[...] += mm((counter == ids_ref[0]).astype(BF), rows_ref[0])


def dense_call(base, ids, rows, entries):
    return pl.pallas_call(
        dense_kernel,
        grid=(ids.shape[0],),
        out_shape=jax.ShapeDtypeStruct((entries, D), F32),
        in_specs=[SM, pl.BlockSpec((1, 1, N), lambda i: (i, 0, 0)), pl.BlockSpec((1, N, D), lambda i: (i, 0, 0))],
        out_specs=pl.BlockSpec((entries, D), lambda i: (0, 0)),
        compiler_params=pltpu.CompilerParams(vmem_limit_bytes=VMEM_LIMIT),
        name="dense_sum",
    )(base, ids, rows)


def partner(values, axis, bit):
    size = lax.axis_size(axis)
    return lax.ppermute(values, axis, [(i, i ^ bit) for i in range(size)])


def bits_of(axis):
    return [1 << b for b in range(lax.axis_size(axis).bit_length() - 1)]


def packed(weight):
    return jnp.swapaxes(weight, 0, 1).reshape(WIDE, D)


def per_device(
    token_ids,
    segment_ids,
    masked_pos,
    word_table,
    position_table,
    embed_gain,
    embed_bias,
    query_weight,
    key_weight,
    value_weight,
    output_weight,
    attention_gain,
    attention_bias,
    expand_weight,
    shrink_weight,
    feed_gain,
    feed_bias,
    logit_grad,
):
    section = lax.axis_index("section")
    place = lax.axis_index("dp")
    devices = lax.axis_size("dp")
    leading = section == 0
    shard_rows = word_table.shape[0]
    vocab = shard_rows * devices
    masks = masked_pos.shape[1]
    half = masks // 2
    room = max(16, 768 // devices)
    slots = room * devices
    base = (place * shard_rows).astype(jnp.int32).reshape(1)

    def swap(values):
        return lax.ppermute(values, "section", [(0, 1), (1, 0)])

    core = place % 2

    def after(values, *others):
        return lax.optimization_barrier((values, *others))[0]

    def exchange(values):
        return lax.all_to_all(values, "dp", 0, 0, tiled=True)

    ids = jnp.where(leading, token_ids[0], token_ids[1])
    table = lax.all_gather(word_table, "dp", axis=0, tiled=True)
    flat_grad = logit_grad.reshape(masks, vocab)

    def gather_by_exchange(array):
        if devices > 16:
            return lax.all_gather(array, "dp")
        return exchange(jnp.broadcast_to(array[None], (devices,) + array.shape))

    slot_col, slot_row, want, most = plan_call(ids, ids // shard_rows, room, slots)
    told = jnp.concatenate([want.reshape(devices, room), jnp.broadcast_to(most[:1, :16], (devices, 16))], axis=1)
    heard = exchange(told)
    asked = heard[:, :room].reshape(1, slots)
    served = serve_call(base, asked.reshape(slots, 1), word_table)
    slot_rows = exchange(served.reshape(devices, room, D)).reshape(slots, D)
    grad_parts = jnp.swapaxes(flat_grad.reshape(masks, devices, shard_rows), 0, 1)
    slot_rows, grad_parts = lax.optimization_barrier((slot_rows, grad_parts))

    most = after(jnp.max(heard[:, room:]).reshape(1, 1), served)
    most = jnp.maximum(most, swap(most))[0, 0]
    crowded = most > room
    flag = jnp.stack([section.astype(jnp.int32), crowded.astype(jnp.int32), core.astype(jnp.int32)])
    dense_rows = lax.cond(
        crowded,
        lambda: gather_by_exchange(word_table).reshape(vocab, D)[ids],
        lambda: jnp.zeros((N, D), BF),
    )

    vectors = jnp.concatenate([attention_gain, attention_bias, feed_gain, feed_bias, jnp.zeros((4, D), F32)], axis=0)
    own = (
        jnp.swapaxes(shrink_weight[0], 1, 2).reshape(D, D),
        expand_weight[0].reshape(D, D),
        output_weight[0],
        jnp.concatenate([packed(query_weight[0]), packed(key_weight[0]), packed(value_weight[0])], axis=0),
        vectors,
    )
    halves = []
    for array in own[:4]:
        rows = array.shape[0] // 2
        halves.append(swap(lax.dynamic_slice_in_dim(array, core * rows, rows, 0)))
    rest = [partner(array, "dp", 1) for array in halves]
    other = tuple(halves) + tuple(rest) + (swap(own[4]),)

    seg_row = jnp.where(leading, segment_ids[0], segment_ids[1])[None]
    mask_row = jnp.where(leading, masked_pos[0], masked_pos[1])[None]
    earlier = jnp.sum((seg_row < seg_row.T).astype(jnp.int32), axis=1)
    places = lax.iota(jnp.int32, N) - earlier
    embed_vec = jnp.stack([embed_gain, embed_bias])

    def chunked(arrays):
        return jnp.concatenate([array.reshape(devices, -1, D) for array in arrays], axis=1)

    def split_halves(values):
        mine = jnp.where(leading, values[:half], values[half:])
        theirs = jnp.where(leading, values[half:], values[:half])
        return mine, theirs

    def join_halves(mine, theirs):
        return jnp.where(leading, jnp.concatenate([mine, theirs]), jnp.concatenate([theirs, mine]))

    picked, saved0, saved1, hat_e, stat_e = forward_call(
        flag, slot_rows, dense_rows, slot_col, places[:, None], seg_row.T, seg_row, mask_row.T, position_table, embed_vec, own, other
    )
    mine, theirs = split_halves(picked)
    head_rows = join_halves(mine, swap(theirs))
    small = devices <= 16
    heads = [partner(head_rows, "dp", 4 * step) for step in (1, 2, 3)] if small else [lax.all_gather(head_rows, "dp", axis=0)]
    rows_back = back_pass(flat_grad, table)
    rows_back, heads = lax.optimization_barrier((rows_back, heads))
    if small:
        heads = jnp.stack([head_rows] + heads)
        heads = [heads, partner(heads, "dp", 2)]
    grad_parts = after(grad_parts, rows_back)
    grad_rows = exchange(grad_parts).reshape(devices * masks, shard_rows)
    mine, theirs = split_halves(rows_back)
    picked_back = join_halves(mine, swap(theirs)).astype(BF)

    def spread_on(array):
        if devices <= 16:
            return array
        groups = [list(range(low, devices, 16)) for low in range(16)]
        return lax.psum(array.astype(F32), "dp", axis_index_groups=groups).astype(BF)

    low_place = (place % 16).astype(jnp.int32).reshape(1)
    side_y = ((place // 2) % 2).astype(jnp.int32).reshape(1)
    me_z = ((place // 4) % 4).astype(jnp.int32).reshape(1)

    def across_z(parts):
        return [spread_on(parts[0])] + [partner(spread_on(parts[step]), "dp", 4 * step) for step in (1, 2, 3)]

    sixteens = [list(range(low, low + 16)) for low in range(0, devices, 16)]

    def sum_to_owner(packed):
        return spread_on(lax.psum_scatter(packed, "dp", scatter_dimension=0, axis_index_groups=sixteens, tiled=True)[0])

    packed_a1, attn1, low1, vec1 = backward_a_call(False, flag, [picked_back, mask_row], own, other, saved1)
    part_a1 = sum_to_owner(packed_a1)
    keep_b1, away_b1, middle = backward_b_call(False, flag, [attn1, low1, vec1], own, other, saved1)
    middle, away_b1 = lax.optimization_barrier((middle, away_b1))
    came_b1 = partner(away_b1, "dp", 1)
    keep_a0, away_a0, attn0, low0, vec0 = backward_a_call(True, flag, [middle], own, other, saved0)
    attn0, heads, away_a0, grad_rows = lax.optimization_barrier((attn0, heads, away_a0, grad_rows))
    if small:
        heads = jnp.concatenate(heads)
        heads = [heads, partner(heads, "dp", 1)]
    came_a0 = partner(away_a0, "dp", 1)
    keep_b0, away_b0, back, slot_grad = backward_b_call(
        True, flag, [attn0, low0, vec0, slot_row, places[None], hat_e, stat_e, embed_vec], own, other, saved0, slots
    )
    slot_grad, away_b0, came_a0, came_b1, heads = lax.optimization_barrier((slot_grad, away_b0, came_a0, came_b1, heads))
    keep_a0, away_a0 = step_y(side_y, keep_a0, came_a0)
    away_a0, away_b0, head_rows = lax.optimization_barrier((away_a0, away_b0, head_rows))
    came_a0 = partner(away_a0, "dp", 2)
    came_b0 = partner(away_b0, "dp", 1)
    logits = logit_pass(head_rows, table)
    logits, slot_grad, keep_b1, came_b1 = lax.optimization_barrier((logits, slot_grad, keep_b1, came_b1))
    keep_b1, away_b1 = step_y(side_y, keep_b1, came_b1)
    came_b1 = partner(away_b1, "dp", 2)
    keep_b0, away_b0 = step_y(side_y, keep_b0, came_b0)
    came_a0, logits, away_b0, came_b1 = lax.optimization_barrier((came_a0, logits, away_b0, came_b1))
    logits = logits.reshape(2, half, vocab)
    local_a0 = step_z(me_z, keep_a0, came_a0)
    local_a0, away_b0, keep_b1 = lax.optimization_barrier((local_a0, away_b0, keep_b1))
    parts_a0 = across_z(local_a0)
    came_b0 = partner(away_b0, "dp", 2)
    local_b1 = step_z(me_z, keep_b1, came_b1)
    local_b0 = step_z(me_z, keep_b0, came_b0)

    sent = exchange(slot_grad.reshape(devices, room, D)).reshape(slots, D)
    crowd_sum = lax.cond(
        crowded,
        lambda: dense_call(base, gather_by_exchange(ids[None]), gather_by_exchange(back), shard_rows),
        lambda: jnp.zeros((shard_rows, D), F32),
    )
    names = jnp.where(crowded, -1, asked)
    if small:
        partial = owner_call(low_place, base, names, sent, grad_rows, heads, crowd_sum)
    else:
        one_hot = (names.reshape(1, slots) == (lax.iota(jnp.int32, shard_rows) + base)[:, None]).astype(BF)
        partial = jnp.dot(one_hot, sent, preferred_element_type=F32) + crowd_sum
        every_head = heads[0].reshape(devices * masks, D)
        partial += lax.dot_general(grad_rows, every_head, (((0,), (0,)), ((), ())), preferred_element_type=F32)
        partial = partial.astype(BF)
    def to_all(chunk, earlier):
        held = jnp.stack([chunk] + [partner(chunk, "dp", 4 * step) for step in (1, 2, 3)])
        held = after(held, earlier)
        held = jnp.concatenate([held, partner(held, "dp", 2)])
        return held, partner(held, "dp", 1)

    parts_a0, local_b0, local_b1, partial = lax.optimization_barrier((parts_a0, local_b0, local_b1, partial))
    parts_b0 = across_z(local_b0)
    parts_b1 = across_z(local_b1)
    mine_b, theirs_b = finish_call(1, flag, low_place, parts_b1, parts_b0)
    theirs_b = swap(theirs_b)
    chunk_b = (mine_b.astype(F32) + theirs_b.astype(F32)).astype(BF)
    mine_a, theirs_a = finish_call(0, flag, low_place, [part_a1], parts_a0)
    theirs_a = swap(theirs_a)
    chunk_a = (mine_a.astype(F32) + theirs_a.astype(F32)).astype(BF)
    all_a = lax.all_gather(chunk_a, "dp", axis=0, axis_index_groups=sixteens)
    swapped = swap(partial)
    table_total = partial.astype(F32) + swapped.astype(F32)
    shrink_total, expand_total, output_total, query_total, key_total, value_total, vec_total, embed_total, position_total = unpack_call(
        flag, low_place, all_a, *to_all(chunk_b, swapped)
    )
    embed_total = embed_total.reshape(2, D // 2)
    return (
        logits,
        table_total,
        position_total,
        embed_total[0],
        embed_total[1],
        query_total[None],
        key_total[None],
        value_total[None],
        output_total[None],
        vec_total[0:1],
        vec_total[1:2],
        expand_total.reshape(1, GROUPS, WIDE, D),
        jnp.swapaxes(shrink_total.reshape(1, GROUPS, WIDE, D), 2, 3),
        vec_total[2:3],
        vec_total[3:4],
    )


def solution(mesh):
    placed = (
        P("dp", None),
        P("dp", None),
        P("dp", None),
        P("dp", None),
        P(),
        P(),
        P(),
        P("section", None, None, None),
        P("section", None, None, None),
        P("section", None, None, None),
        P("section", None, None),
        P("section", None),
        P("section", None),
        P("section", None, None, None),
        P("section", None, None, None),
        P("section", None),
        P("section", None),
        P("dp", "section", None),
    )
    return jax.shard_map(
        per_device,
        mesh=mesh,
        in_specs=placed,
        out_specs=(
            P("dp", "section", None),
            P("dp", None),
            P(None, "section"),
            P("section"),
            P("section"),
            P("section", None, None, None),
            P("section", None, None, None),
            P("section", None, None, None),
            P("section", None, None),
            P("section", None),
            P("section", None),
            P("section", None, None, None),
            P("section", None, None, None),
            P("section", None),
            P("section", None),
        ),
        check_vma=False,
    )
```
